32 devices in a mesh: groups: 2 (over y), stripe: 8 (over z, x), exp: 2 (over core).
Axes of the slice: x: 2, y: 2, z: 4, core: 2. Of those that a mesh axis runs over, the one named last changes fastest.
Arguments:
- template: float32 [256, 2048], P(('groups', 'stripe'), 'exp'), parts along dimension 0, may hold values from -6 to 6
- exposure: float32 [4, 128, 2048], P(('groups', 'exp'), 'stripe'), parts along dimension 0, may hold values from -30 to 30
- cosmic_mask: int32 [4, 128, 2048], P(('groups', 'exp'), 'stripe'), parts along dimension 0, may hold values 0 or 1
- stamp_blocks: int32 [16, 16], P(('groups', 'stripe')), parts along dimension 0, may hold values from 0 to 31, as said below
- row_filters: float32 [19, 19], replicated, may hold values from -1 to 2.5
- col_filters: float32 [19, 19], replicated, may hold values from -1 to 2.5
Outputs:
- filtered: float32 [4, 128, 2048], P(('groups', 'exp'), 'stripe'), parts along dimension 0
- coefficients: float32 [4, 64], P(('groups', 'exp')), parts along dimension 0
The draws below stay inside these ranges and needn't reach their ends.
There are 2 independent parts, one for each index of `groups`. The reference program is written for one: setup_inputs(seed, part) draws one part's arguments, and reference() takes and returns one part's arrays. A program takes and returns all parts, laid end to end along the dimension named above; an argument that names none is the same for every part. Nothing has to cross between parts.
Inputs may be any that keep to these rules, and one draw needn't show every extreme that they name: `stamp_blocks`: each row lists the stamps of one stripe; stamp j lies in column block 2 j or 2 j + 1.
All inputs are finite; a program needn't handle non-finite values. No bound on the sum of `cosmic_mask` on one device may be relied on, other than what follows from the above.
Results may differ from the reference program's by a relative error of at most 0.0003.
Values sent between devices are 32-bit elements; how exact they have to be, the bound alone decides.
No kernel may reach another device: no remote copies, remote signals or barrier semaphores. Data moves between devices by JAX's collectives and lax.ppermute only.
A program may use at most 64 MiB of HBM per device.

```python
import math
import jax
import jax.numpy as jnp
from jax import lax

ROWS_DEV = 16
COLS = 2048
HALF = 9
BASES = 19
STAMP_W = 64
TAPS = 19
NCOL = 64
NSTAMP = 16
STRIPES = 8
NR = 128
NEXP = 2


def sky_field(key):
    return jnp.clip(jax.random.normal(jax.random.fold_in(key, 101), (NR, COLS), jnp.float32), -5.0, 5.0)


def draw_template(key, part):
    sky = sky_field(key)
    extra = jnp.clip(jax.random.normal(jax.random.fold_in(key, 103), (NR, COLS), jnp.float32), -5.0, 5.0)
    return sky + 0.1 * extra


def blur_axis(field, near, far, axis_id):
    centre = 1.0 - 2.0 * near - 2.0 * far
    result = centre * field + near * (jnp.roll(field, 1, axis_id) + jnp.roll(field, -1, axis_id))
    return result + far * (jnp.roll(field, 2, axis_id) + jnp.roll(field, -2, axis_id))


def draw_exposure(key, part):
    sky = sky_field(key)
    row_pos = (2.0 * jnp.arange(NR, dtype=jnp.float32) + 1.0) / NR - 1.0
    col_pos = (2.0 * jnp.arange(COLS, dtype=jnp.float32) + 1.0) / COLS - 1.0
    amplitude = (1.3 + row_pos + 0.8 * row_pos * row_pos)[:, None] * (1.0 + 0.4 * jnp.cos(3.0 * math.pi * col_pos))[None, :]
    frames = []
    for frame in range(NEXP):
        frame_key = jax.random.fold_in(key, 200 + frame)
        params = jax.random.uniform(frame_key, (5,), jnp.float32)
        blurred = blur_axis(sky, 0.15 + 0.15 * params[0], 0.02 + 0.08 * params[1], 0)
        blurred = blur_axis(blurred, 0.15 + 0.15 * params[2], 0.02 + 0.08 * params[3], 1)
        jitter = 0.3 * jnp.clip(jax.random.normal(jax.random.fold_in(frame_key, 7), (NR, COLS), jnp.float32), -5.0, 5.0)
        offset_level = 0.5 * params[4] + 0.4 * col_pos[None, :] + 0.3 * row_pos[:, None] * col_pos[None, :]
        frames.append(amplitude * blurred + offset_level + jitter)
    return jnp.stack(frames)


def filter_bank(key, salt):
    taps_pos = jnp.arange(TAPS, dtype=jnp.float32) - HALF
    sigma = jnp.exp(jax.random.uniform(jax.random.fold_in(key, salt), (BASES, 1), jnp.float32, math.log(0.6), math.log(3.5)))
    profile = jnp.exp(-taps_pos[None, :] ** 2 / (2.0 * sigma * sigma)) / (2.5 * sigma)
    first = jnp.clip(jax.random.normal(jax.random.fold_in(key, salt + 1), (BASES, TAPS), jnp.float32), -4.0, 4.0)
    second = jnp.clip(jax.random.normal(jax.random.fold_in(key, salt + 2), (BASES, TAPS), jnp.float32), -4.0, 4.0)
    return profile * (1.0 + 0.3 * first) + 0.12 * second


def draw_row_filters(key, part):
    return filter_bank(key, 301)


def draw_col_filters(key, part):
    return filter_bank(key, 311)


def draw_stamp_blocks(key, part):
    choose = jax.random.randint(jax.random.fold_in(key, 401), (STRIPES, NSTAMP), 0, 2)
    row_id = jnp.arange(STRIPES, dtype=jnp.int32)[:, None]
    slot_id = jnp.arange(NSTAMP, dtype=jnp.int32)[None, :]
    choose = jnp.where((row_id == 0) & (slot_id == 0), 0, choose)
    choose = jnp.where((row_id == 0) & (slot_id == NSTAMP - 1), 1, choose)
    return (2 * slot_id + choose).astype(jnp.int32)


def touch_ends(drawn, own_key, least, largest):
    longest = drawn.shape.index(max(drawn.shape))
    spots = []
    for shift in (0, 1):
        where = [jax.random.randint(jax.random.fold_in(own_key, axis), (), 0, length) for axis, length in enumerate(drawn.shape)]
        where[longest] = (where[longest] + shift) % drawn.shape[longest]
        spots.append(tuple(where))
    return drawn.at[spots[0]].set(least).at[spots[1]].set(largest)


def setup_inputs(seed: int = 0, part: int = 0) -> dict:
    key_of = jax.random.split(jax.random.key(seed), 7)
    own_keys = jax.random.split(jax.random.fold_in(key_of[6], part), 7)
    return {
        "template": draw_template(jax.random.fold_in(jax.random.fold_in(key_of[6], part), 71), part),
        "exposure": draw_exposure(jax.random.fold_in(jax.random.fold_in(key_of[6], part), 71), part),
        "cosmic_mask": touch_ends((jax.random.randint(own_keys[2], (NEXP, NR, COLS), 0, 32) < 31).astype(jnp.int32), jax.random.fold_in(own_keys[2], 1), 0, 1),
        "stamp_blocks": draw_stamp_blocks(jax.random.fold_in(jax.random.fold_in(key_of[6], part), 71), part),
        "row_filters": draw_row_filters(jax.random.fold_in(key_of[6], 71), part),
        "col_filters": draw_col_filters(jax.random.fold_in(key_of[6], 71), part),
    }


def stripe_bases(extended, row_filters, col_filters):
    row_span = extended.shape[0] - 2 * HALF
    col_span = extended.shape[1] - 2 * HALF
    vertical = row_filters[:, 0, None, None] * extended[None, 0:row_span, :]
    for offset in range(1, 2 * HALF + 1):
        vertical = vertical + row_filters[:, offset, None, None] * extended[None, offset:offset + row_span, :]
    result = col_filters[:, 0, None, None] * vertical[:, :, 0:col_span]
    for offset in range(1, 2 * HALF + 1):
        result = result + col_filters[:, offset, None, None] * vertical[:, :, offset:offset + col_span]
    return result

def background_terms(horiz_pos, vert_pos):
    constant = jnp.ones_like(horiz_pos)
    u_square = 0.5 * (3.0 * horiz_pos * horiz_pos - 1.0)
    v_square = 0.5 * (3.0 * vert_pos * vert_pos - 1.0)
    return jnp.stack([constant, horiz_pos, vert_pos, horiz_pos * vert_pos, u_square, v_square, horiz_pos * v_square])

def design_matrix(picked, horiz_pos, vert_pos):
    kernel = jnp.stack([picked, picked * horiz_pos, picked * vert_pos], axis=1).reshape(3 * picked.shape[0], -1)
    background = background_terms(horiz_pos, vert_pos).reshape(7, -1)
    return jnp.concatenate([kernel, background], axis=0).astype(jnp.bfloat16)

def solve_normal(normal_aug):
    factor = jnp.linalg.cholesky(normal_aug[:, :-1])
    lower_sol = jax.scipy.linalg.solve_triangular(factor, normal_aug[:, -1], lower=True)
    return jax.scipy.linalg.solve_triangular(factor, lower_sol, lower=True, trans=1)

def model_values(bases, solution, horiz_pos, vert_pos):
    kernel_part = solution[:3 * BASES].reshape(BASES, 3)
    steady = jnp.einsum('bij,b->ij', bases, kernel_part[:, 0], precision=lax.Precision.HIGHEST)
    along_u = jnp.einsum('bij,b->ij', bases, kernel_part[:, 1], precision=lax.Precision.HIGHEST)
    along_v = jnp.einsum('bij,b->ij', bases, kernel_part[:, 2], precision=lax.Precision.HIGHEST)
    background = background_terms(horiz_pos, vert_pos)
    level = jnp.einsum('mij,m->ij', background, solution[3 * BASES:], precision=lax.Precision.HIGHEST)
    return steady + horiz_pos * along_u + vert_pos * along_v + level

def reference(template, exposure, cosmic_mask, stamp_blocks, row_filters, col_filters):
    padded = jnp.pad(template, ((HALF, HALF), (HALF, HALF)))
    col_index = jnp.arange(COLS, dtype=jnp.int32)
    horiz_all = (2.0 * col_index.astype(jnp.float32) + 1.0) / COLS - 1.0
    offsets = jnp.arange(STAMP_W, dtype=jnp.int32)

    def stripe_rows(stripe_id):
        row_index = stripe_id * ROWS_DEV + jnp.arange(ROWS_DEV, dtype=jnp.int32)
        return (2.0 * row_index.astype(jnp.float32) + 1.0) / NR - 1.0

    def fit_stripe(normal_sum, stripe_id):
        extended = lax.dynamic_slice_in_dim(padded, (stripe_id * ROWS_DEV).astype(jnp.int32), ROWS_DEV + 2 * HALF, 0)
        bases = stripe_bases(extended, row_filters, col_filters)
        blocks = lax.dynamic_index_in_dim(stamp_blocks, stripe_id, 0, keepdims=False)
        chosen = (blocks[:, None] * STAMP_W + offsets[None, :]).reshape(-1).astype(jnp.int32)
        picked = jnp.take(bases, chosen, axis=2)
        horiz_pos = jnp.broadcast_to(horiz_all[chosen][None, :], (ROWS_DEV, chosen.shape[0]))
        vert_pos = jnp.broadcast_to(stripe_rows(stripe_id)[:, None], (ROWS_DEV, chosen.shape[0]))
        design = design_matrix(picked, horiz_pos, vert_pos)
        science = lax.dynamic_slice_in_dim(exposure, (stripe_id * ROWS_DEV).astype(jnp.int32), ROWS_DEV, 1)
        good = lax.dynamic_slice_in_dim(cosmic_mask, (stripe_id * ROWS_DEV).astype(jnp.int32), ROWS_DEV, 1)
        science_sel = jnp.take(science, chosen, axis=2)
        good_sel = jnp.take(good, chosen, axis=2).astype(jnp.float32)
        weighted = design[None] * good_sel.reshape(NEXP, 1, -1).astype(jnp.bfloat16)
        target = (good_sel * science_sel).reshape(NEXP, 1, -1).astype(jnp.bfloat16)
        augmented = jnp.concatenate([weighted, target], axis=1)
        normal = jnp.einsum('enp,emp->enm', weighted.astype(jnp.float32), augmented.astype(jnp.float32), precision=lax.Precision.HIGHEST)
        return (normal_sum + normal, None)
    start_sum = jnp.zeros((NEXP, NCOL, NCOL + 1), jnp.float32)
    normal_total, _ = lax.scan(fit_stripe, start_sum, jnp.arange(STRIPES, dtype=jnp.int32))
    coefficients = jax.vmap(solve_normal)(normal_total)

    def model_stripe(stripe_id):
        extended = lax.dynamic_slice_in_dim(padded, (stripe_id * ROWS_DEV).astype(jnp.int32), ROWS_DEV + 2 * HALF, 0)
        bases = stripe_bases(extended, row_filters, col_filters)
        horiz_pos = jnp.broadcast_to(horiz_all[None, :], (ROWS_DEV, COLS))
        vert_pos = jnp.broadcast_to(stripe_rows(stripe_id)[:, None], (ROWS_DEV, COLS))
        models = jax.vmap(lambda solution: model_values(bases, solution, horiz_pos, vert_pos))(coefficients)
        science = lax.dynamic_slice_in_dim(exposure, (stripe_id * ROWS_DEV).astype(jnp.int32), ROWS_DEV, 1)
        good = lax.dynamic_slice_in_dim(cosmic_mask, (stripe_id * ROWS_DEV).astype(jnp.int32), ROWS_DEV, 1)
        return good.astype(jnp.float32) * (science - models)
    stacked = lax.map(model_stripe, jnp.arange(STRIPES, dtype=jnp.int32))
    difference = jnp.transpose(stacked, (1, 0, 2, 3)).reshape(NEXP, NR, COLS)
    framed = jnp.pad(difference, ((0, 0), (1, 1), (1, 1)))
    neighbours = framed[:, 2:, 1:-1] + framed[:, :-2, 1:-1] + framed[:, 1:-1, 2:] + framed[:, 1:-1, :-2]
    filtered = 4.0 * difference - neighbours
    return (filtered, coefficients)
```

```python
import functools

import jax
import jax.numpy as jnp
from jax import lax
from jax.experimental import pallas as pl
from jax.experimental.pallas import tpu as pltpu
from jax.sharding import PartitionSpec as P

HALF = 9
TAPS = 2 * HALF + 1
BASES = 19
STAMP_W = 64
LANES = 128
BASE_PAD = 24
BACK = 7
FIT_ROWS = 3 * BASE_PAD + BACK + 1
REACH = HALF + 1
GROUP = 32
GROUPS_TILE = LANES // GROUP
MAIN_TILES = 5
MAIN = MAIN_TILES * LANES
DEPTH = MAIN + LANES
EXTRA_ROWS = 80
F32 = jnp.float32
BF16 = jnp.bfloat16


def lane_id(rows):
    return lax.broadcasted_iota(jnp.int32, (rows, LANES), 1)


def row_id(rows):
    return lax.broadcasted_iota(jnp.int32, (rows, LANES), 0)


def split_two(values):
    high = values.astype(BF16)
    low = (values - high.astype(F32)).astype(BF16)
    return high, low


def position(index, total):
    return (2.0 * index.astype(F32) + 1.0) / total - 1.0


def even_stripe():
    return lax.rem(lax.axis_index("stripe"), 2) == 0


def edge_kernel(cores, *refs):
    pieces = refs[:cores]
    science_ref, good_ref, near_ref, far_ref, ext = refs[cores:]
    rows, half = pieces[0].shape
    wide = science_ref.shape[2]
    me = lax.axis_index("exp")
    for step in range(cores):
        start = lax.rem(me + step, cores) * half
        ext[:, pl.ds(pl.multiple_of(start, LANES), half)] = pieces[step][...]
    fold = wide // 2
    low_first = rows - 8

    def edge(first, extra, outer):
        parts = [ext[first : first + 8, :fold], ext[first : first + 8, fold:]]
        tail = []
        for line in (extra, extra + 1):
            tail += [ext[line : line + 1, :fold], ext[line : line + 1, fold:]]
        science = science_ref[0, outer : outer + 1, :]
        good = good_ref[0, outer : outer + 1, :].astype(F32)
        for line in (science, good):
            tail += [line[:, :fold], line[:, fold:]]
        return jnp.concatenate(parts + tail, axis=0)

    bottom = edge(low_first, rows - REACH, rows - 1)
    top = edge(0, 8, 0)
    even = even_stripe()
    near_ref[...] = jnp.where(even, bottom, top)
    far_ref[...] = jnp.where(even, top, bottom)


def weight_kernel(row_ref, col_ref, high_ref, low_ref, base_ref, pad):
    pad[...] = jnp.zeros_like(pad)
    pad[0, 0:BASES, 0:TAPS] = row_ref[...]
    pad[1, 0:BASES, 0:TAPS] = col_ref[...]
    row = pad[0]
    lane = lane_id(BASE_PAD)
    spot = lax.rem(lane, GROUP)
    group = lane // GROUP
    tiled = row
    for part in range(1, GROUPS_TILE):
        tiled = tiled + pltpu.roll(row, part * GROUP, 1)
    columns = [
        jnp.broadcast_to(pad[1, :, tap : tap + 1], (BASE_PAD, LANES)) for tap in range(TAPS)
    ]
    zero = jnp.zeros((BASE_PAD, LANES), F32)
    mains = []
    for tile in range(MAIN_TILES):
        spread = zero
        for part in range(GROUPS_TILE):
            tap = tile * GROUPS_TILE + part
            if tap < TAPS:
                spread = jnp.where(group == part, columns[tap], spread)
        mains.append(tiled * spread)
    spread = zero
    for tap in range(TAPS):
        spread = jnp.where(lane // 4 == tap, columns[tap], spread)
    corner = lax.rem(lane, 4)

    def tap_at(tap):
        return jnp.broadcast_to(pad[0, :, tap : tap + 1], (BASE_PAD, LANES))

    outer = jnp.where(
        corner == 0,
        tap_at(0),
        jnp.where(corner == 1, tap_at(1), jnp.where(corner == 2, tap_at(TAPS - 2), tap_at(TAPS - 1))),
    )
    inner = jnp.where(corner == 1, tap_at(0), jnp.where(corner == 2, tap_at(TAPS - 1), 0.0))
    outer = outer * spread
    inner = inner * spread
    for tile in range(MAIN_TILES):
        base_ref[:, tile * LANES : (tile + 1) * LANES] = mains[tile]
    base_ref[:, MAIN : MAIN + LANES] = outer
    base_ref[:, MAIN + LANES :] = inner
    rows = high_ref.shape[0] // BASE_PAD
    for line in range(rows):
        tap = spot - (line - 1)
        inside = (tap >= 0) & (tap < TAPS)
        tiles = [
            jnp.where(inside, pltpu.roll(main, (line - 1) % LANES, 1), 0.0) for main in mains
        ]
        if line == 0:
            tiles.append(jnp.where(corner < 2, inner, 0.0))
        elif line == rows - 1:
            tiles.append(jnp.where(corner >= 2, inner, 0.0))
        else:
            tiles.append(zero)
        high, low = split_two(jnp.concatenate(tiles, axis=1))
        where = pl.ds(line * BASE_PAD, BASE_PAD)
        high_ref[where, :] = high.astype(F32)
        low_ref[where, :] = low.astype(F32)


def fill_extended(ext, cores, pieces, near_ref, far_ref):
    rows, half = pieces[0].shape
    wide = half * cores
    fold = wide // 2
    ext[:, 0:LANES] = jnp.zeros((ext.shape[0], LANES), F32)
    ext[:, LANES + wide :] = jnp.zeros((ext.shape[0], LANES), F32)
    me = lax.axis_index("exp")
    for step in range(cores):
        start = lax.rem(me + step, cores) * half + LANES
        ext[8 : 8 + rows, pl.ds(pl.multiple_of(start, LANES), half)] = pieces[step][...]
    even = even_stripe()
    near = near_ref[...]
    far = far_ref[...]
    top = jnp.where(even, far, near)
    bottom = jnp.where(even, near, far)
    for side in range(2):
        where = pl.ds(LANES + side * fold, fold)
        ext[0:8, where] = top[8 * side : 8 * side + 8]
        ext[8 + rows : 16 + rows, where] = bottom[8 * side : 8 * side + 8]
        spare = [
            top[16 + side : 17 + side],
            top[18 + side : 19 + side],
            bottom[16 + side : 17 + side],
            bottom[18 + side : 19 + side],
        ]
        ext[16 + rows : 24 + rows, where] = jnp.concatenate(spare + spare, axis=0)
    return top, bottom


def spread_window(shifted, put):
    for tap in range(TAPS):
        put(tap * GROUP, shifted(tap, slice(0, GROUP)))
    extra = slice(GROUP, GROUP + 8)
    early = row_id(8) < 4
    for quad in range(MAIN_TILES):
        lines = [shifted(4 * quad + part, extra) for part in range(4)]
        put(
            MAIN + 16 * quad,
            jnp.concatenate(
                [jnp.where(early, lines[0], lines[1]), jnp.where(early, lines[2], lines[3])], axis=0
            ),
        )


def clear_spare(tile_refs, columns):
    for ref in tile_refs:
        ref[TAPS * GROUP : MAIN, columns] = jnp.zeros((MAIN - TAPS * GROUP, LANES), BF16)
        ref[MAIN + EXTRA_ROWS :, columns] = jnp.zeros((LANES - EXTRA_ROWS, LANES), BF16)


def back_profile(horiz):
    steady = jnp.ones_like(horiz)
    square = 0.5 * (3.0 * horiz * horiz - 1.0)
    return [steady, horiz, steady, horiz, square, steady, horiz]


def fit_kernel(cores, stripes, stamps_ref, *refs):
    pieces = refs[:cores]
    near_ref, far_ref, science_ref, good_ref, high_ref, low_ref, out_ref, ext, xhigh, xlow = refs[cores:]
    rows = pieces[0].shape[0]
    wide = science_ref.shape[2]
    pairs = wide // (4 * STAMP_W)
    fill_extended(ext, cores, pieces, near_ref, far_ref)
    lane = lane_id(1)
    lane_ext = lane_id(ext.shape[0])
    first_row = lax.axis_index("stripe") * rows

    def odd_of(stamp):
        return lax.rem(stamps_ref[0, stamp], 2)

    def window(stamp, offset):
        odd = odd_of(stamp)
        left = ext[:, stamp * LANES : (stamp + 1) * LANES]
        centre = ext[:, (stamp + 1) * LANES : (stamp + 2) * LANES]
        right = ext[:, (stamp + 2) * LANES : (stamp + 3) * LANES]
        taken = jnp.where(
            odd == 1,
            jnp.where(lane_ext < HALF, right, centre),
            jnp.where(lane_ext >= LANES - HALF, left, centre),
        )
        amount = jnp.where(odd == 1, HALF + STAMP_W, HALF) + offset
        return pltpu.roll(taken, lax.rem(amount, LANES), 1)

    def picked(values, stamp, offset):
        return pltpu.roll(values, odd_of(stamp) * STAMP_W + offset, 1)

    total = jnp.zeros((FIT_ROWS, FIT_ROWS), F32)
    chunk = 2
    for start in range(0, pairs, chunk):
        for pair in range(start, start + chunk):
            first = window(2 * pair, 0)
            second = window(2 * pair + 1, STAMP_W)
            columns = slice(pair * LANES, (pair + 1) * LANES)

            def shifted(tap, lines):
                back = (LANES - tap) % LANES
                a = first[lines]
                b = second[lines]
                if back:
                    a = pltpu.roll(a, back, 1)
                    b = pltpu.roll(b, back, 1)
                return jnp.where(lane_id(a.shape[0]) < STAMP_W, a, b)

            def put(place, values):
                high, low = split_two(values)
                xhigh[place : place + values.shape[0], columns] = high
                xlow[place : place + values.shape[0], columns] = low

            spread_window(shifted, put)
            clear_spare((xhigh, xlow), columns)
        span = slice(start * LANES, (start + chunk) * LANES)
        weights_high = high_ref[...].astype(BF16)
        weights_low = low_ref[...].astype(BF16)
        bases = (
            jnp.dot(weights_high, xhigh[:, span], preferred_element_type=F32)
            + jnp.dot(weights_low, xhigh[:, span], preferred_element_type=F32)
            + jnp.dot(weights_high, xlow[:, span], preferred_element_type=F32)
        )
        horiz_parts, science_parts, good_parts = [], [], []
        for pair in range(start, start + chunk):
            low_half = lane < STAMP_W
            block = jnp.where(low_half, stamps_ref[0, 2 * pair], stamps_ref[0, 2 * pair + 1] - 1)
            horiz_parts.append(position(block * STAMP_W + lane, wide))
            for source, parts in ((science_ref, science_parts), (good_ref, good_parts)):
                a = source[0, :, 2 * pair * LANES : (2 * pair + 1) * LANES].astype(F32)
                b = source[0, :, (2 * pair + 1) * LANES : (2 * pair + 2) * LANES].astype(F32)
                a = picked(a, 2 * pair, 0)
                b = picked(b, 2 * pair + 1, STAMP_W)
                parts.append(jnp.where(lane_id(rows) < STAMP_W, a, b))
        horiz = jnp.concatenate(horiz_parts, axis=1)
        good = jnp.concatenate(good_parts, axis=1)
        target = good * jnp.concatenate(science_parts, axis=1)
        profile = jnp.concatenate(back_profile(horiz), axis=0)
        for line in range(rows):
            keep = good[line : line + 1]
            own = bases[line * BASE_PAD : (line + 1) * BASE_PAD] * keep
            vert = position(jnp.full((1, chunk * LANES), first_row + line, jnp.int32), rows * stripes)
            square = 0.5 * (3.0 * vert * vert - 1.0)
            steady = jnp.ones_like(vert)
            scale = jnp.concatenate([steady, steady, vert, vert, steady, square, square], axis=0)
            ground = profile * scale * keep
            design = jnp.concatenate(
                [own, own * horiz, own * vert, ground, target[line : line + 1]], axis=0
            ).astype(BF16)
            total = total + lax.dot_general(
                design, design, (((1,), (1,)), ((), ())), preferred_element_type=F32
            )
    out_ref[...] = jnp.concatenate(
        [total, jnp.zeros((FIT_ROWS, LANES - FIT_ROWS), F32)], axis=1
    )


def pivots():
    return [t * BASE_PAD + b for t in range(3) for b in range(BASES)] + [
        3 * BASE_PAD + m for m in range(BACK)
    ]


def solve_rows(matrix):
    line = row_id(FIT_ROWS)
    lane = lane_id(FIT_ROWS)
    used = (line >= 3 * BASE_PAD) | (lax.rem(line, BASE_PAD) < BASES)
    matrix = jnp.where((line == lane) & ~used, 1.0, matrix)
    for pivot in pivots():
        column = jnp.broadcast_to(matrix[:, pivot : pivot + 1], (FIT_ROWS, LANES))
        row = matrix[pivot : pivot + 1] / column[pivot : pivot + 1]
        matrix = matrix - jnp.where(line == pivot, 0.0, column) * row
    right = jnp.broadcast_to(matrix[:, FIT_ROWS - 1 : FIT_ROWS], (FIT_ROWS, LANES))
    diagonal = jnp.sum(jnp.where(line == lane, matrix, 0.0), axis=1, keepdims=True)
    return right / jnp.broadcast_to(diagonal, (FIT_ROWS, LANES))


def model_kernel(cores, stripes, normal_ref, *refs):
    pieces = refs[:cores]
    near_ref, far_ref, science_ref, good_ref, base_ref, out_ref, coef_ref, ext, xhigh, xlow = refs[cores:]
    rows = pieces[0].shape[0]
    wide = science_ref.shape[2]
    fold = wide // 2
    top, bottom = fill_extended(ext, cores, pieces, near_ref, far_ref)
    tiles = wide // LANES
    lane_ext = lane_id(ext.shape[0])
    for tile in range(tiles):
        columns = slice(tile * LANES, (tile + 1) * LANES)
        left = ext[:, tile * LANES : (tile + 1) * LANES]
        centre = ext[:, (tile + 1) * LANES : (tile + 2) * LANES]
        right = ext[:, (tile + 2) * LANES : (tile + 3) * LANES]

        def shifted(tap, lines):
            move = HALF - tap
            middle = centre[lines]
            if move == 0:
                return middle
            where = lane_ext[lines]
            if move > 0:
                mixed = jnp.where(where >= LANES - move, left[lines], middle)
            else:
                mixed = jnp.where(where < -move, right[lines], middle)
            return pltpu.roll(mixed, move % LANES, 1)

        def put(place, values):
            high, low = split_two(values)
            xhigh[place : place + values.shape[0], columns] = high
            xlow[place : place + values.shape[0], columns] = low

        spread_window(shifted, put)
        clear_spare((xhigh, xlow), columns)

    coef = solve_rows(normal_ref[...])
    lane = lane_id(FIT_ROWS)
    home = jnp.where(
        lane < 3 * BASES, lax.rem(lane, 3) * BASE_PAD + lane // 3, lane + 3 * (BASE_PAD - BASES)
    )
    flat = jnp.sum(jnp.where(row_id(FIT_ROWS) == home, coef, 0.0), axis=0, keepdims=True)
    coef_ref[...] = flat[:, : coef_ref.shape[1]]

    line = row_id(BASE_PAD)
    lane = lane_id(BASE_PAD)
    spot = lax.rem(lane, GROUP)
    shift = jnp.where(line == rows + 1, -2, line - 1)
    tap = spot - shift
    inside = (tap >= 0) & (tap < TAPS)
    corner = lax.rem(lane, 4)
    blocks = []
    for term in range(3):
        share = coef[term * BASE_PAD : (term + 1) * BASE_PAD]
        parts = []
        for tile in range(MAIN_TILES + 2):
            mixed = base_ref[:, tile * LANES : (tile + 1) * LANES] * share
            parts.append(jnp.broadcast_to(jnp.sum(mixed, axis=0, keepdims=True), (BASE_PAD, LANES)))
        wanted = []
        for tile in range(MAIN_TILES):
            moved = jnp.concatenate(
                [
                    pltpu.roll(
                        pltpu.roll(parts[tile][:8], (start - 1) % LANES, 1), 0, 1, stride=1, stride_axis=0
                    )
                    for start in range(0, BASE_PAD, 8)
                ],
                axis=0,
            )
            moved = jnp.where(line == rows + 1, pltpu.roll(parts[tile], LANES - 2, 1), moved)
            wanted.append(jnp.where(inside, moved, 0.0))
        outer, inner = parts[MAIN_TILES], parts[MAIN_TILES + 1]
        spare = jnp.where((line == rows + 1) & (corner < 2), outer, 0.0)
        spare = jnp.where((line == 0) & (corner < 2), inner, spare)
        spare = jnp.where((line == rows - 1) & (corner >= 2), inner, spare)
        spare = jnp.where((line == rows) & (corner >= 2), outer, spare)
        wanted.append(spare)
        blocks.append(jnp.concatenate(wanted, axis=1))
    kernel_high, kernel_low = split_two(jnp.concatenate(blocks, axis=0))
    level = [coef[3 * BASE_PAD + m : 3 * BASE_PAD + m + 1, 0:1] for m in range(BACK)]
    first_row = lax.axis_index("stripe") * rows
    vert_line = jnp.where(line == rows + 1, -1, line)
    vert = position(first_row + vert_line, rows * stripes)[:, 0:1]
    vert_square = 0.5 * (3.0 * vert * vert - 1.0)
    chunk = min(4 * LANES, wide)
    outs = []
    for start in range(0, wide, chunk):
        span = slice(start, start + chunk)
        sums = (
            jnp.dot(kernel_high, xhigh[:, span], preferred_element_type=F32)
            + jnp.dot(kernel_low, xhigh[:, span], preferred_element_type=F32)
            + jnp.dot(kernel_high, xlow[:, span], preferred_element_type=F32)
        )
        horiz = position(start + lax.broadcasted_iota(jnp.int32, (1, chunk), 1), wide)
        horiz_square = 0.5 * (3.0 * horiz * horiz - 1.0)
        model = (
            sums[:BASE_PAD]
            + horiz * sums[BASE_PAD : 2 * BASE_PAD]
            + vert * sums[2 * BASE_PAD :]
            + (level[0] + level[1] * horiz + level[4] * horiz_square)
            + vert * (level[2] + level[3] * horiz)
            + vert_square * (level[5] + level[6] * horiz)
        )
        outs.append(model)
    model = jnp.concatenate(outs, axis=1)
    own = good_ref[0].astype(F32) * (science_ref[0] - model[:rows])

    def halo(edge, spot):
        science = jnp.concatenate([edge[20:21], edge[21:22]], axis=1)
        good = jnp.concatenate([edge[22:23], edge[23:24]], axis=1)
        return good * (science - model[spot : spot + 1])

    above_row = halo(top, rows + 1)
    below_row = halo(bottom, rows)
    lines = lax.broadcasted_iota(jnp.int32, (rows, wide), 0)
    spots = lax.broadcasted_iota(jnp.int32, (rows, wide), 1)
    above = jnp.where(lines == 0, above_row, pltpu.roll(own, 1, 0))
    below = jnp.where(lines == rows - 1, below_row, pltpu.roll(own, rows - 1, 0))
    before = jnp.where(spots == 0, 0.0, pltpu.roll(own, 1, 1))
    after = jnp.where(spots == wide - 1, 0.0, pltpu.roll(own, wide - 1, 1))
    out_ref[0] = 4.0 * own - (below + above + after + before)


def whole_vmem(count):
    return [pl.BlockSpec(memory_space=pltpu.VMEM)] * count


def summed(values, axis):
    count = lax.axis_size(axis)
    if count & (count - 1):
        return lax.psum(values, axis)
    step = 1
    while step < count:
        values = values + lax.ppermute(values, axis, [(i, i ^ step) for i in range(count)])
        step *= 2
    return values


def shards(template, exposure, cosmic_mask, stamp_blocks, row_filters, col_filters):
    rows, half = template.shape
    wide = exposure.shape[2]
    cores = lax.axis_size("exp")
    stripes = lax.axis_size("stripe")
    params = pltpu.CompilerParams(vmem_limit_bytes=48 * 1024 * 1024)
    pieces = [template] + [
        lax.ppermute(template, "exp", [((i + step) % cores, i) for i in range(cores)])
        for step in range(1, cores)
    ]
    edge_shape = jax.ShapeDtypeStruct((24, wide // 2), F32)
    near, far = pl.pallas_call(
        functools.partial(edge_kernel, cores),
        out_shape=(edge_shape, edge_shape),
        in_specs=whole_vmem(cores + 2),
        out_specs=tuple(whole_vmem(2)),
        scratch_shapes=[pltpu.VMEM((rows, wide), F32)],
        compiler_params=params,
        name="edges",
    )(*pieces, exposure, cosmic_mask)
    near_pairs = [(i, i + 1) for i in range(0, stripes - 1, 2)]
    far_pairs = [(i, i + 1) for i in range(1, stripes - 1, 2)]

    def swapped(values, couples):
        return lax.ppermute(values, "stripe", couples + [(b, a) for a, b in couples])

    near = swapped(near, near_pairs)
    far = swapped(far, far_pairs)
    weight_shape = jax.ShapeDtypeStruct((rows * BASE_PAD, DEPTH), F32)
    high, low, base = pl.pallas_call(
        weight_kernel,
        out_shape=(
            weight_shape,
            weight_shape,
            jax.ShapeDtypeStruct((BASE_PAD, DEPTH + LANES), F32),
        ),
        in_specs=whole_vmem(2),
        out_specs=tuple(whole_vmem(3)),
        scratch_shapes=[pltpu.VMEM((2, BASE_PAD, LANES), F32)],
        compiler_params=params,
        name="weights",
    )(row_filters, col_filters)
    ext_shape = pltpu.VMEM((rows + 24, wide + 2 * LANES), F32)
    normal = pl.pallas_call(
        functools.partial(fit_kernel, cores, stripes),
        out_shape=jax.ShapeDtypeStruct((FIT_ROWS, LANES), F32),
        in_specs=[pl.BlockSpec(memory_space=pltpu.SMEM)] + whole_vmem(cores + 6),
        out_specs=pl.BlockSpec(memory_space=pltpu.VMEM),
        scratch_shapes=[
            ext_shape,
            pltpu.VMEM((DEPTH, wide // 2), BF16),
            pltpu.VMEM((DEPTH, wide // 2), BF16),
        ],
        compiler_params=params,
        name="fit",
    )(stamp_blocks, *pieces, near, far, exposure, cosmic_mask, high, low)
    normal = summed(normal, "stripe")
    filtered, coef = pl.pallas_call(
        functools.partial(model_kernel, cores, stripes),
        out_shape=(
            jax.ShapeDtypeStruct(exposure.shape, F32),
            jax.ShapeDtypeStruct((1, 3 * BASES + BACK), F32),
        ),
        in_specs=whole_vmem(cores + 6),
        out_specs=tuple(whole_vmem(2)),
        scratch_shapes=[
            ext_shape,
            pltpu.VMEM((DEPTH, wide), BF16),
            pltpu.VMEM((DEPTH, wide), BF16),
        ],
        compiler_params=params,
        name="model",
    )(normal, *pieces, near, far, exposure, cosmic_mask, base)
    return filtered, coef


def solution(mesh):
    placed = (
        P(("groups", "stripe"), "exp"),
        P(("groups", "exp"), "stripe", None),
        P(("groups", "exp"), "stripe", None),
        P(("groups", "stripe"), None),
        P(),
        P(),
    )
    return jax.shard_map(
        shards,
        mesh=mesh,
        in_specs=placed,
        out_specs=(P(("groups", "exp"), "stripe", None), P(("groups", "exp"), None)),
        check_vma=False,
    )
```

```python
import functools

import jax
import jax.numpy as jnp
from jax import lax
from jax.experimental import pallas as pl
from jax.experimental.pallas import tpu as pltpu
from jax.sharding import PartitionSpec as P

HALF = 9
TAPS = 2 * HALF + 1
BASES = 19
STAMP_W = 64
LANES = 128
BASE_PAD = 24
BACK = 7
FIT_ROWS = 3 * BASE_PAD + BACK + 1
REACH = HALF + 1
GROUP = 32
GROUPS_TILE = LANES // GROUP
MAIN_TILES = 5
MAIN = MAIN_TILES * LANES
DEPTH = MAIN + LANES
EXTRA_ROWS = 80
F32 = jnp.float32
BF16 = jnp.bfloat16


def lane_id(rows):
    return lax.broadcasted_iota(jnp.int32, (rows, LANES), 1)


def row_id(rows):
    return lax.broadcasted_iota(jnp.int32, (rows, LANES), 0)


def split_two(values):
    high = values.astype(BF16)
    low = (values - high.astype(F32)).astype(BF16)
    return high, low


def position(index, total):
    return (2.0 * index.astype(F32) + 1.0) / total - 1.0


def even_stripe():
    return lax.rem(lax.axis_index("stripe"), 2) == 0


def edge_kernel(cores, *refs):
    pieces = refs[:cores]
    science_ref, good_ref, near_ref, far_ref, ext = refs[cores:]
    rows, half = pieces[0].shape
    wide = science_ref.shape[2]
    me = lax.axis_index("exp")
    for step in range(cores):
        start = lax.rem(me + step, cores) * half
        ext[:, pl.ds(pl.multiple_of(start, LANES), half)] = pieces[step][...]
    fold = wide // 2
    low_first = rows - 8

    def edge(first, extra, outer):
        parts = [ext[first : first + 8, :fold], ext[first : first + 8, fold:]]
        tail = []
        for line in (extra, extra + 1):
            tail += [ext[line : line + 1, :fold], ext[line : line + 1, fold:]]
        science = science_ref[0, outer : outer + 1, :]
        good = good_ref[0, outer : outer + 1, :]
        for line in (science, good):
            tail += [line[:, :fold], line[:, fold:]]
        return jnp.concatenate(parts + tail, axis=0)

    bottom = edge(low_first, rows - REACH, rows - 1)
    top = edge(0, 8, 0)
    even = even_stripe()
    near_ref[...] = jnp.where(even, bottom, top)
    far_ref[...] = jnp.where(even, top, bottom)


def load_kernel(
    template_hbm,
    science_hbm,
    good_hbm,
    stamps_hbm,
    row_hbm,
    col_hbm,
    template_ref,
    science_ref,
    good_ref,
    odd_ref,
    high_ref,
    low_ref,
    base_ref,
    pad,
    row_ref,
    col_ref,
    mask_ref,
    stamps_ref,
    sems,
):
    moves = [
        pltpu.make_async_copy(source, target, sems.at[spot])
        for spot, (source, target) in enumerate(
            [
                (row_hbm, row_ref),
                (col_hbm, col_ref),
                (template_hbm, template_ref),
                (stamps_hbm, stamps_ref),
                (good_hbm, mask_ref),
                (science_hbm, science_ref),
            ]
        )
    ]
    for move in moves:
        move.start()
    pad[...] = jnp.zeros_like(pad)
    for move in moves:
        move.wait()
    good_ref[...] = mask_ref[...].astype(F32)
    odd_ref[...] = jnp.concatenate(
        [
            jnp.full((1, LANES), lax.rem(stamps_ref[0, stamp], 2), jnp.int32)
            for stamp in range(odd_ref.shape[0])
        ],
        axis=0,
    )
    pad[0, 0:BASES, 0:TAPS] = row_ref[...]
    pad[1, 0:BASES, 0:TAPS] = col_ref[...]
    row = pad[0]
    lane = lane_id(BASE_PAD)
    spot = lax.rem(lane, GROUP)
    group = lane // GROUP
    tiled = row
    for part in range(1, GROUPS_TILE):
        tiled = tiled + pltpu.roll(row, part * GROUP, 1)
    columns = [
        jnp.broadcast_to(pad[1, :, tap : tap + 1], (BASE_PAD, LANES)) for tap in range(TAPS)
    ]
    zero = jnp.zeros((BASE_PAD, LANES), F32)
    mains = []
    for tile in range(MAIN_TILES):
        spread = zero
        for part in range(GROUPS_TILE):
            tap = tile * GROUPS_TILE + part
            if tap < TAPS:
                spread = jnp.where(group == part, columns[tap], spread)
        mains.append(tiled * spread)
    spread = zero
    for tap in range(TAPS):
        spread = jnp.where(lane // 4 == tap, columns[tap], spread)
    corner = lax.rem(lane, 4)

    def tap_at(tap):
        return jnp.broadcast_to(pad[0, :, tap : tap + 1], (BASE_PAD, LANES))

    outer = jnp.where(
        corner == 0,
        tap_at(0),
        jnp.where(corner == 1, tap_at(1), jnp.where(corner == 2, tap_at(TAPS - 2), tap_at(TAPS - 1))),
    )
    inner = jnp.where(corner == 1, tap_at(0), jnp.where(corner == 2, tap_at(TAPS - 1), 0.0))
    outer = outer * spread
    inner = inner * spread
    for tile in range(MAIN_TILES):
        base_ref[:, tile * LANES : (tile + 1) * LANES] = mains[tile]
    base_ref[:, MAIN : MAIN + LANES] = outer
    base_ref[:, MAIN + LANES :] = inner
    rows = high_ref.shape[0] // BASE_PAD

    def line_weights(line):
        tap = spot - (line - 1)
        inside = (tap >= 0) & (tap < TAPS)
        tiles = [
            jnp.where(inside, pltpu.roll(main, (line - 1) % LANES, 1), 0.0) for main in mains
        ]
        if line == 0:
            tiles.append(jnp.where(corner < 2, inner, 0.0))
        elif line == rows - 1:
            tiles.append(jnp.where(corner >= 2, inner, 0.0))
        else:
            tiles.append(zero)
        return jnp.concatenate(tiles, axis=1)

    for line in range(0, rows, 2):
        both = jnp.concatenate([line_weights(line), line_weights(line + 1)], axis=0)
        high, low = split_two(both)
        where = pl.ds(line * BASE_PAD, 2 * BASE_PAD)
        high_ref[where, :] = high
        low_ref[where, :] = low


def edges_of(near_ref, far_ref):
    even = even_stripe()
    near = near_ref[...]
    far = far_ref[...]
    return jnp.where(even, far, near), jnp.where(even, near, far)


def fill_extended(ext, highs, lows, cores, pieces, near_ref, far_ref):
    rows, half = pieces[0].shape
    wide = half * cores
    fold = wide // 2
    ext[:, 0:LANES] = jnp.zeros((ext.shape[0], LANES), F32)
    ext[:, LANES + wide :] = jnp.zeros((ext.shape[0], LANES), F32)
    me = lax.axis_index("exp")
    for step in range(cores):
        start = lax.rem(me + step, cores) * half + LANES
        ext[8 : 8 + rows, pl.ds(pl.multiple_of(start, LANES), half)] = pieces[step][...]
    top, bottom = edges_of(near_ref, far_ref)
    for side in range(2):
        where = pl.ds(LANES + side * fold, fold)
        ext[0:8, where] = top[8 * side : 8 * side + 8]
        ext[8 + rows : 16 + rows, where] = bottom[8 * side : 8 * side + 8]
        spare = [
            top[16 + side : 17 + side],
            top[18 + side : 19 + side],
            bottom[16 + side : 17 + side],
            bottom[18 + side : 19 + side],
        ]
        ext[16 + rows : 24 + rows, where] = jnp.concatenate(spare + spare, axis=0)
    main = slice(0, GROUP)
    highs[main], lows[main] = split_two(ext[main])
    extra = ext[GROUP : GROUP + 8]
    span = extra.shape[1]
    early = lax.broadcasted_iota(jnp.int32, extra.shape, 0) < 4
    ahead = [extra] + [pltpu.roll(extra, span - part, 1) for part in range(1, 4)]
    lines = jnp.concatenate(
        [jnp.where(early, ahead[0], ahead[1]), jnp.where(early, ahead[2], ahead[3])], axis=0
    )
    highs[GROUP:], lows[GROUP:] = split_two(lines)


def spread_window(shifted, put):
    for tap in range(TAPS):
        put(tap * GROUP, shifted(tap, slice(0, GROUP)))
    for quad in range(MAIN_TILES):
        put(MAIN + 16 * quad, shifted(4 * quad, slice(GROUP, GROUP + 16)))


def clear_spare(refs):
    for ref in refs:
        wide = ref.shape[1]
        ref[TAPS * GROUP : MAIN] = jnp.zeros((MAIN - TAPS * GROUP, wide), BF16)
        ref[MAIN + EXTRA_ROWS :] = jnp.zeros((LANES - EXTRA_ROWS, wide), BF16)


def back_profile(horiz):
    steady = jnp.ones_like(horiz)
    square = 0.5 * (3.0 * horiz * horiz - 1.0)
    return [steady, horiz, steady, horiz, square, steady, horiz]


def fit_kernel(cores, stripes, *refs):
    pieces = refs[:cores]
    (
        near_ref,
        far_ref,
        science_ref,
        good_ref,
        odd_ref,
        high_ref,
        low_ref,
        out_ref,
        ext,
        highs,
        lows,
        xhigh,
        xlow,
    ) = refs[cores:]
    rows = pieces[0].shape[0]
    wide = science_ref.shape[2]
    pairs = wide // (4 * STAMP_W)
    fill_extended(ext, highs, lows, cores, pieces, near_ref, far_ref)
    clear_spare((xhigh, xlow))
    lane = lane_id(1)
    lane_ext = lane_id(highs.shape[0])
    first_row = lax.axis_index("stripe") * rows

    def odd_of(stamp, height):
        return jnp.broadcast_to(odd_ref[stamp : stamp + 1, :] == 1, (height, LANES))

    def window(source, stamp, offset):
        left = source[:, stamp * LANES : (stamp + 1) * LANES]
        centre = source[:, (stamp + 1) * LANES : (stamp + 2) * LANES]
        right = source[:, (stamp + 2) * LANES : (stamp + 3) * LANES]
        odd = jnp.where(lane_ext < HALF, right, centre)
        even = jnp.where(lane_ext >= LANES - HALF, left, centre)
        odd = pltpu.roll(odd, (HALF + STAMP_W + offset) % LANES, 1)
        even = pltpu.roll(even, HALF + offset, 1)
        return jnp.where(odd_of(stamp, source.shape[0]), odd, even)

    def picked(values, stamp, upper):
        moved = pltpu.roll(values, STAMP_W, 1)
        odd = odd_of(stamp, values.shape[0])
        return jnp.where(odd, values, moved) if upper else jnp.where(odd, moved, values)

    total = jnp.zeros((FIT_ROWS, FIT_ROWS), F32)
    chunk = 2
    for start in range(0, pairs, chunk):
        for pair in range(start, start + chunk):
            columns = slice(pair * LANES, (pair + 1) * LANES)
            for source, target in ((highs, xhigh), (lows, xlow)):
                first = window(source, 2 * pair, 0)
                second = window(source, 2 * pair + 1, STAMP_W)

                def shifted(tap, lines):
                    a, b = first[lines], second[lines]
                    if tap:
                        a = pltpu.roll(a, LANES - tap, 1)
                        b = pltpu.roll(b, LANES - tap, 1)
                    return jnp.where(lane_id(a.shape[0]) < STAMP_W, a, b)

                def put(place, values):
                    target[place : place + values.shape[0], columns] = values

                spread_window(shifted, put)
        span = slice(start * LANES, (start + chunk) * LANES)
        weights_high = high_ref[...]
        weights_low = low_ref[...]
        bases = (
            jnp.dot(weights_high, xhigh[:, span], preferred_element_type=F32)
            + jnp.dot(weights_low, xhigh[:, span], preferred_element_type=F32)
            + jnp.dot(weights_high, xlow[:, span], preferred_element_type=F32)
        )
        horiz_parts, science_parts, good_parts = [], [], []
        for pair in range(start, start + chunk):
            low_half = lane < STAMP_W
            odd = jnp.where(
                low_half, odd_ref[2 * pair : 2 * pair + 1], odd_ref[2 * pair + 1 : 2 * pair + 2] + 1
            )
            horiz_parts.append(position(4 * pair * STAMP_W + odd * STAMP_W + lane, wide))
            for source, parts in ((science_ref, science_parts), (good_ref, good_parts)):
                a = source[0, :, 2 * pair * LANES : (2 * pair + 1) * LANES]
                b = source[0, :, (2 * pair + 1) * LANES : (2 * pair + 2) * LANES]
                a = picked(a, 2 * pair, False)
                b = picked(b, 2 * pair + 1, True)
                parts.append(jnp.where(lane_id(rows) < STAMP_W, a, b))
        horiz = jnp.concatenate(horiz_parts, axis=1)
        good = jnp.concatenate(good_parts, axis=1)
        target = good * jnp.concatenate(science_parts, axis=1)
        profile = jnp.concatenate(back_profile(horiz), axis=0)
        for line in range(rows):
            keep = good[line : line + 1]
            own = bases[line * BASE_PAD : (line + 1) * BASE_PAD] * keep
            vert = position(jnp.full((1, chunk * LANES), first_row + line, jnp.int32), rows * stripes)
            square = 0.5 * (3.0 * vert * vert - 1.0)
            steady = jnp.ones_like(vert)
            scale = jnp.concatenate([steady, steady, vert, vert, steady, square, square], axis=0)
            ground = profile * scale * keep
            design = jnp.concatenate(
                [own, own * horiz, own * vert, ground, target[line : line + 1]], axis=0
            ).astype(BF16)
            total = total + lax.dot_general(
                design, design, (((1,), (1,)), ((), ())), preferred_element_type=F32
            )
    out_ref[...] = jnp.concatenate(
        [total, jnp.zeros((FIT_ROWS, LANES - FIT_ROWS), F32)], axis=1
    )


def panels():
    out = []
    for term in range(3):
        start = term * BASE_PAD
        out += [(start, 8), (start + 8, 8), (start + 16, BASES - 16)]
    return out + [(3 * BASE_PAD, BACK)]


def solve_rows(matrix):
    sub = row_id(8)
    tiles = [matrix[start : start + 8] for start in range(0, FIT_ROWS, 8)]

    def spread(tile, spot):
        return jnp.broadcast_to(tile[spot : spot + 1], (8, LANES))

    for start, size in panels():
        home = start // 8
        columns = [
            [jnp.broadcast_to(tile[:, start + j : start + j + 1], (8, LANES)) for tile in tiles]
            for j in range(size)
        ]
        corner = [column[home] for column in columns]
        rows = tiles[home]
        for spot in range(size):
            keep = sub == spot
            inverse = 1.0 / spread(corner[spot], spot)
            others = jnp.where(keep, 0.0, corner[spot])
            scaled = spread(rows, spot) * inverse
            rows = jnp.where(keep, scaled, rows - others * scaled)
            for j in range(spot + 1, size):
                scaled = spread(corner[j], spot) * inverse
                corner[j] = jnp.where(keep, scaled, corner[j] - others * scaled)
        for place in range(len(tiles)):
            if place == home:
                tiles[place] = rows
                continue
            change = columns[0][place] * spread(rows, 0)
            for j in range(1, size):
                change = change + columns[j][place] * spread(rows, j)
            tiles[place] = tiles[place] - change
    line = row_id(FIT_ROWS)
    used = (line >= 3 * BASE_PAD) | (lax.rem(line, BASE_PAD) < BASES)
    right = jnp.concatenate(tiles, axis=0)[:, FIT_ROWS - 1 : FIT_ROWS]
    return jnp.where(used, jnp.broadcast_to(right, (FIT_ROWS, LANES)), 0.0)


def spread_kernel(cores, *refs):
    pieces = refs[:cores]
    near_ref, far_ref, after_ref, xhigh, xlow, ext, highs, lows = refs[cores:]
    wide = xhigh.shape[1]
    fill_extended(ext, highs, lows, cores, pieces, near_ref, far_ref)
    clear_spare((xhigh, xlow))
    for source, target in ((highs, xhigh), (lows, xlow)):

        def shifted(tap, lines):
            start = LANES - HALF + tap
            return source[lines, start : start + wide]

        def put(place, values):
            target[place : place + values.shape[0]] = values

        spread_window(shifted, put)


def model_kernel(
    stripes,
    normal_ref,
    xhigh,
    xlow,
    near_ref,
    far_ref,
    science_ref,
    good_ref,
    base_ref,
    out_ref,
    coef_ref,
):
    rows = science_ref.shape[1]
    wide = science_ref.shape[2]
    top, bottom = edges_of(near_ref, far_ref)
    coef = solve_rows(normal_ref[...])
    lane = lane_id(FIT_ROWS)
    home = jnp.where(
        lane < 3 * BASES, lax.rem(lane, 3) * BASE_PAD + lane // 3, lane + 3 * (BASE_PAD - BASES)
    )
    flat = jnp.sum(jnp.where(row_id(FIT_ROWS) == home, coef, 0.0), axis=0, keepdims=True)
    coef_ref[...] = flat[:, : coef_ref.shape[1]]

    line = row_id(BASE_PAD)
    lane = lane_id(BASE_PAD)
    spot = lax.rem(lane, GROUP)
    shift = jnp.where(line == rows + 1, -2, line - 1)
    tap = spot - shift
    inside = (tap >= 0) & (tap < TAPS)
    corner = lax.rem(lane, 4)
    blocks = []
    for term in range(3):
        share = coef[term * BASE_PAD : (term + 1) * BASE_PAD]
        parts = []
        for tile in range(MAIN_TILES + 2):
            mixed = base_ref[:, tile * LANES : (tile + 1) * LANES] * share
            parts.append(jnp.broadcast_to(jnp.sum(mixed, axis=0, keepdims=True), (BASE_PAD, LANES)))
        wanted = []
        for tile in range(MAIN_TILES):
            moved = jnp.concatenate(
                [
                    pltpu.roll(
                        pltpu.roll(parts[tile][:8], (start - 1) % LANES, 1), 0, 1, stride=1, stride_axis=0
                    )
                    for start in range(0, BASE_PAD, 8)
                ],
                axis=0,
            )
            moved = jnp.where(line == rows + 1, pltpu.roll(parts[tile], LANES - 2, 1), moved)
            wanted.append(jnp.where(inside, moved, 0.0))
        outer, inner = parts[MAIN_TILES], parts[MAIN_TILES + 1]
        spare = jnp.where((line == rows + 1) & (corner < 2), outer, 0.0)
        spare = jnp.where((line == 0) & (corner < 2), inner, spare)
        spare = jnp.where((line == rows - 1) & (corner >= 2), inner, spare)
        spare = jnp.where((line == rows) & (corner >= 2), outer, spare)
        wanted.append(spare)
        blocks.append(jnp.concatenate(wanted, axis=1))
    blocks.append(jnp.zeros((8, DEPTH), F32))
    kernel_high, kernel_low = split_two(jnp.concatenate(blocks, axis=0))
    kernel_gap = kernel_high.shape[0]
    kernel_both = jnp.concatenate([kernel_high, kernel_low], axis=0)
    level = [coef[3 * BASE_PAD + m : 3 * BASE_PAD + m + 1, 0:1] for m in range(BACK)]
    first_row = lax.axis_index("stripe") * rows
    vert_line = jnp.where(line == rows + 1, -1, line)
    vert = position(first_row + vert_line, rows * stripes)[:, 0:1]
    vert_square = 0.5 * (3.0 * vert * vert - 1.0)
    chunk = min(4 * LANES, wide)
    outs = []
    for start in range(0, wide, chunk):
        span = slice(start, start + chunk)
        both = jnp.dot(kernel_both, xhigh[:, span], preferred_element_type=F32)
        lower = jnp.dot(kernel_high, xlow[:, span], preferred_element_type=F32)
        sums = both[: 3 * BASE_PAD] + (both[kernel_gap : kernel_gap + 3 * BASE_PAD] + lower[: 3 * BASE_PAD])
        horiz = position(start + lax.broadcasted_iota(jnp.int32, (1, chunk), 1), wide)
        horiz_square = 0.5 * (3.0 * horiz * horiz - 1.0)
        model = (
            sums[:BASE_PAD]
            + horiz * sums[BASE_PAD : 2 * BASE_PAD]
            + vert * sums[2 * BASE_PAD :]
            + (level[0] + level[1] * horiz + level[4] * horiz_square)
            + vert * (level[2] + level[3] * horiz)
            + vert_square * (level[5] + level[6] * horiz)
        )
        outs.append(model)
    model = jnp.concatenate(outs, axis=1)
    own = good_ref[0] * (science_ref[0] - model[:rows])

    def halo(edge, spot):
        science = jnp.concatenate([edge[20:21], edge[21:22]], axis=1)
        good = jnp.concatenate([edge[22:23], edge[23:24]], axis=1)
        return good * (science - model[spot : spot + 1])

    above_row = halo(top, rows + 1)
    below_row = halo(bottom, rows)
    lines = lax.broadcasted_iota(jnp.int32, (rows, wide), 0)
    spots = lax.broadcasted_iota(jnp.int32, (rows, wide), 1)
    above = jnp.where(lines == 0, above_row, pltpu.roll(own, 1, 0))
    below = jnp.where(lines == rows - 1, below_row, pltpu.roll(own, rows - 1, 0))
    before = jnp.where(spots == 0, 0.0, pltpu.roll(own, 1, 1))
    after = jnp.where(spots == wide - 1, 0.0, pltpu.roll(own, wide - 1, 1))
    out_ref[0] = 4.0 * own - (below + above + after + before)


def whole_vmem(count):
    return [pl.BlockSpec(memory_space=pltpu.VMEM)] * count


def summed(values, axis):
    count = lax.axis_size(axis)
    if count & (count - 1):
        return lax.psum(values, axis)
    step = 1
    while step < count:
        values = values + lax.ppermute(values, axis, [(i, i ^ step) for i in range(count)])
        step *= 2
    return values


def shards(template, exposure, cosmic_mask, stamp_blocks, row_filters, col_filters):
    arguments = (template, exposure, cosmic_mask, stamp_blocks, row_filters, col_filters)
    rows, half = template.shape
    wide = exposure.shape[2]
    cores = lax.axis_size("exp")
    stripes = lax.axis_size("stripe")
    params = pltpu.CompilerParams(vmem_limit_bytes=24 * 1024 * 1024)
    pieces = [template] + [
        lax.ppermute(template, "exp", [((i + step) % cores, i) for i in range(cores)])
        for step in range(1, cores)
    ]
    weight_shape = jax.ShapeDtypeStruct((rows * BASE_PAD, DEPTH), BF16)
    stamps = stamp_blocks.shape[1]
    template_in, science, good, odd, high, low, base = pl.pallas_call(
        load_kernel,
        out_shape=(
            jax.ShapeDtypeStruct(template.shape, F32),
            jax.ShapeDtypeStruct(exposure.shape, F32),
            jax.ShapeDtypeStruct(exposure.shape, F32),
            jax.ShapeDtypeStruct((stamps, LANES), jnp.int32),
            weight_shape,
            weight_shape,
            jax.ShapeDtypeStruct((BASE_PAD, DEPTH + LANES), F32),
        ),
        in_specs=[pl.BlockSpec(memory_space=pltpu.HBM)] * 6,
        out_specs=tuple(whole_vmem(7)),
        scratch_shapes=[
            pltpu.VMEM((2, BASE_PAD, LANES), F32),
            pltpu.VMEM(row_filters.shape, F32),
            pltpu.VMEM(col_filters.shape, F32),
            pltpu.VMEM(cosmic_mask.shape, jnp.int32),
            pltpu.SMEM(stamp_blocks.shape, jnp.int32),
            pltpu.SemaphoreType.DMA((6,)),
        ],
        compiler_params=params,
        name="load",
    )(*[pltpu.with_memory_space_constraint(array, pltpu.HBM) for array in arguments])
    pieces = [template_in] + pieces[1:]
    edge_shape = jax.ShapeDtypeStruct((24, wide // 2), F32)
    near, far = pl.pallas_call(
        functools.partial(edge_kernel, cores),
        out_shape=(edge_shape, edge_shape),
        in_specs=whole_vmem(cores + 2),
        out_specs=tuple(whole_vmem(2)),
        scratch_shapes=[pltpu.VMEM((rows, wide), F32)],
        compiler_params=params,
        name="edges",
    )(*pieces, science, good)
    near_pairs = [(i, i + 1) for i in range(0, stripes - 1, 2)]
    far_pairs = [(i, i + 1) for i in range(1, stripes - 1, 2)]

    def swapped(values, couples):
        return lax.ppermute(values, "stripe", couples + [(b, a) for a, b in couples])

    far = swapped(far, far_pairs)
    near = swapped(near, near_pairs)
    ext_shapes = [
        pltpu.VMEM((rows + 24, wide + 2 * LANES), F32),
        pltpu.VMEM((GROUP + 16, wide + 2 * LANES), BF16),
        pltpu.VMEM((GROUP + 16, wide + 2 * LANES), BF16),
    ]
    normal = pl.pallas_call(
        functools.partial(fit_kernel, cores, stripes),
        out_shape=jax.ShapeDtypeStruct((FIT_ROWS, LANES), F32),
        in_specs=whole_vmem(cores + 7),
        out_specs=pl.BlockSpec(memory_space=pltpu.VMEM),
        scratch_shapes=ext_shapes
        + [
            pltpu.VMEM((DEPTH, wide // 2), BF16),
            pltpu.VMEM((DEPTH, wide // 2), BF16),
        ],
        compiler_params=params,
        name="fit",
    )(*pieces, near, far, science, good, odd, high, low)
    wide_shape = jax.ShapeDtypeStruct((DEPTH, wide), BF16)
    xhigh, xlow = pl.pallas_call(
        functools.partial(spread_kernel, cores),
        out_shape=(wide_shape, wide_shape),
        in_specs=whole_vmem(cores + 3),
        out_specs=tuple(whole_vmem(2)),
        scratch_shapes=ext_shapes,
        compiler_params=params,
        name="spread",
    )(*pieces, near, far, normal)
    normal = summed(normal, "stripe")
    filtered, coef = pl.pallas_call(
        functools.partial(model_kernel, stripes),
        out_shape=(
            jax.ShapeDtypeStruct(exposure.shape, F32),
            jax.ShapeDtypeStruct((1, 3 * BASES + BACK), F32),
        ),
        in_specs=whole_vmem(8),
        out_specs=tuple(whole_vmem(2)),
        compiler_params=params,
        name="model",
    )(normal, xhigh, xlow, near, far, science, good, base)
    return filtered, coef


def solution(mesh):
    placed = (
        P(("groups", "stripe"), "exp"),
        P(("groups", "exp"), "stripe", None),
        P(("groups", "exp"), "stripe", None),
        P(("groups", "stripe"), None),
        P(),
        P(),
    )
    return jax.shard_map(
        shards,
        mesh=mesh,
        in_specs=placed,
        out_specs=(P(("groups", "exp"), "stripe", None), P(("groups", "exp"), None)),
        check_vma=False,
    )
```

```python
import functools

import jax
import jax.numpy as jnp
from jax import lax
from jax.experimental import pallas as pl
from jax.experimental.pallas import tpu as pltpu
from jax.sharding import PartitionSpec as P

HALF = 9
TAPS = 2 * HALF + 1
BASES = 19
STAMP_W = 64
LANES = 128
BASE_PAD = 24
BACK = 7
FIT_ROWS = 3 * BASE_PAD + BACK + 1
REACH = HALF + 1
GROUP = 32
GROUPS_TILE = LANES // GROUP
MAIN_TILES = 5
MAIN = MAIN_TILES * LANES
DEPTH = MAIN + LANES
EXTRA_ROWS = 80
NEAR_AT = TAPS * 16
NEAR_EXTRA_AT = NEAR_AT + 160
EARLY = NEAR_EXTRA_AT + 48
FAR_EXTRA_AT = 160
LATE = 2 * LANES
LATE_ROWS = -(-HALF * BASE_PAD // 16) * 16
F32 = jnp.float32
BF16 = jnp.bfloat16


def lane_id(rows):
    return lax.broadcasted_iota(jnp.int32, (rows, LANES), 1)


def row_id(rows):
    return lax.broadcasted_iota(jnp.int32, (rows, LANES), 0)


def split_two(values):
    high = values.astype(BF16)
    low = (values - high.astype(F32)).astype(BF16)
    return high, low


def position(index, total):
    return (2.0 * index.astype(F32) + 1.0) / total - 1.0


def even_stripe():
    return lax.rem(lax.axis_index("stripe"), 2) == 0


def edge_kernel(cores, toward_near, *refs):
    pieces = refs[:cores]
    science_ref, good_ref = refs[cores : cores + 2]
    edge_ref, ext = refs[-2:]
    rows, half = pieces[0].shape
    wide = science_ref.shape[2]
    me = lax.axis_index("exp")
    for step in range(cores):
        start = lax.rem(me + step, cores) * half
        ext[:, pl.ds(pl.multiple_of(start, LANES), half)] = pieces[step][...]
    fold = wide // 2
    low_first = rows - 8

    def edge(first, extra, outer):
        parts = [ext[first : first + 8, :fold], ext[first : first + 8, fold:]]
        tail = []
        for line in (extra, extra + 1):
            tail += [ext[line : line + 1, :fold], ext[line : line + 1, fold:]]
        science = science_ref[0, outer : outer + 1, :]
        good = good_ref[0, outer : outer + 1, :]
        for line in (science, good):
            tail += [line[:, :fold], line[:, fold:]]
        return jnp.concatenate(parts + tail, axis=0)

    bottom = edge(low_first, rows - REACH, rows - 1)
    top = edge(0, 8, 0)
    edge_ref[...] = jnp.where(even_stripe() == toward_near, bottom, top)


def load_kernel(
    template_hbm,
    science_hbm,
    good_hbm,
    row_hbm,
    col_hbm,
    stamps_hbm,
    template_ref,
    science_ref,
    good_ref,
    row_ref,
    col_ref,
    odd_ref,
    mask_ref,
    stamps_ref,
    sems,
):
    moves = [
        pltpu.make_async_copy(source, target, sems.at[spot])
        for spot, (source, target) in enumerate(
            [
                (science_hbm, science_ref),
                (good_hbm, mask_ref),
                (template_hbm, template_ref),
                (row_hbm, row_ref),
                (col_hbm, col_ref),
                (stamps_hbm, stamps_ref),
            ]
        )
    ]
    for move in moves:
        move.start()
    for move in moves:
        move.wait()
    good_ref[...] = mask_ref[...].astype(F32)
    odd_ref[...] = jnp.concatenate(
        [
            jnp.full((1, LANES), lax.rem(stamps_ref[0, stamp], 2), jnp.int32)
            for stamp in range(odd_ref.shape[0])
        ],
        axis=0,
    )


def weight_kernel(
    row_ref, col_ref, high_ref, low_ref, late_high_ref, late_low_ref, base_ref, pad
):
    pad[...] = jnp.zeros_like(pad)
    pad[0, 0:BASES, 0:TAPS] = row_ref[...]
    pad[1, 0:BASES, 0:TAPS] = col_ref[...]
    row = pad[0]
    lane = lane_id(BASE_PAD)
    group = lane // GROUP
    tiled = row
    for part in range(1, GROUPS_TILE):
        tiled = tiled + pltpu.roll(row, part * GROUP, 1)
    columns = [
        jnp.broadcast_to(pad[1, :, tap : tap + 1], (BASE_PAD, LANES)) for tap in range(TAPS)
    ]
    zero = jnp.zeros((BASE_PAD, LANES), F32)
    mains = []
    for tile in range(MAIN_TILES):
        spread = zero
        for part in range(GROUPS_TILE):
            tap = tile * GROUPS_TILE + part
            if tap < TAPS:
                spread = jnp.where(group == part, columns[tap], spread)
        mains.append(tiled * spread)
    spread = zero
    for tap in range(TAPS):
        spread = jnp.where(lane // 4 == tap, columns[tap], spread)
    corner = lax.rem(lane, 4)

    def tap_at(tap):
        return jnp.broadcast_to(pad[0, :, tap : tap + 1], (BASE_PAD, LANES))

    outer = jnp.where(
        corner == 0,
        tap_at(0),
        jnp.where(corner == 1, tap_at(1), jnp.where(corner == 2, tap_at(TAPS - 2), tap_at(TAPS - 1))),
    )
    inner = jnp.where(corner == 1, tap_at(0), jnp.where(corner == 2, tap_at(TAPS - 1), 0.0))
    outer = outer * spread
    inner = inner * spread
    for tile in range(MAIN_TILES):
        base_ref[:, tile * LANES : (tile + 1) * LANES] = mains[tile]
    base_ref[:, MAIN : MAIN + LANES] = outer
    base_ref[:, MAIN + LANES :] = inner
    rows = high_ref.shape[0] // BASE_PAD
    even = even_stripe()
    first_tap, last_tap = tap_at(0), tap_at(TAPS - 1)

    def column_tile(tap_of):
        spread = zero
        begin = 0
        for end in range(1, LANES + 1):
            if end < LANES and tap_of(end) == tap_of(begin):
                continue
            if tap_of(begin) < TAPS:
                spread = jnp.where((lane >= begin) & (lane < end), columns[tap_of(begin)], spread)
            begin = end
        return spread

    def early_tap(place):
        if place < NEAR_AT:
            return place // 16
        return (place - NEAR_AT) // 8 if place < NEAR_EXTRA_AT else (place - NEAR_EXTRA_AT) // 2

    def late_tap(place):
        return place // 8 if place < FAR_EXTRA_AT else (place - FAR_EXTRA_AT) // 2

    early_tiles = [
        column_tile(lambda spot, tile=tile: early_tap(tile * LANES + spot))
        for tile in range(EARLY // LANES)
    ]
    late_tiles = [
        column_tile(lambda spot, tile=tile: late_tap(tile * LANES + spot))
        for tile in range(LATE // LANES)
    ]

    def repeats(period):
        blocks = []
        for start in range(0, TAPS, period):
            block = pltpu.roll(row, (LANES - start) % LANES, 1) if start else row
            block = jnp.where(lane < period, block, 0.0)
            size = period
            while size < LANES:
                block = block + pltpu.roll(block, size, 1)
                size *= 2
            blocks.append(block)
        return blocks

    def window(blocks, period, first):
        block, move = first // period, first % period
        here = blocks[block] if 0 <= block < len(blocks) else None
        beyond = blocks[block + 1] if 0 <= block + 1 < len(blocks) else None
        if move == 0:
            return zero if here is None else here
        ready = lax.rem(lane, period) < period - move
        parts = [zero if part is None else pltpu.roll(part, LANES - move, 1) for part in (here, beyond)]
        return jnp.where(ready, parts[0], parts[1])

    by_sixteen, by_eight = repeats(16), repeats(8)
    own_rows = [window(by_sixteen, 16, HALF - line) for line in range(rows)]
    top_rows = [window(by_eight, 8, 1 - line) for line in range(rows)]
    bottom_rows = [window(by_eight, 8, rows + HALF - line) for line in range(rows)]

    parity = lax.rem(lane, 2)

    def corner_taps(upper, lower, is_upper):
        top = jnp.where(parity == 1, first_tap, 0.0) if upper else zero
        bottom = jnp.where(parity == 0, last_tap, 0.0) if lower else zero
        return jnp.where(is_upper, top, bottom)

    near_is_top = ~even
    early_rows, late_rows = [], []
    for spot in range(rows):
        odd_line = spot + rows - HALF if spot < HALF else spot - HALF
        own = jnp.where(even, own_rows[spot], own_rows[odd_line])
        side = jnp.where(even, bottom_rows[spot], top_rows[odd_line])
        extra = zero
        if spot >= HALF:
            extra = corner_taps(spot == HALF, spot == rows - 1, near_is_top)
        tiles = [
            own,
            own,
            jnp.where(lane < NEAR_AT - 2 * LANES, own, side),
            jnp.where(lane < NEAR_EXTRA_AT - 3 * LANES, side, extra),
        ]
        early_rows.append(
            jnp.concatenate([mine * tile for mine, tile in zip(tiles, early_tiles)], axis=1)
        )
        if spot < HALF:
            side = jnp.where(even, top_rows[spot], bottom_rows[odd_line])
            extra = corner_taps(spot == 0, spot == HALF - 1, even)
            tiles = [side, jnp.where(lane < FAR_EXTRA_AT - LANES, side, extra)]
            late_rows.append(
                jnp.concatenate([mine * tile for mine, tile in zip(tiles, late_tiles)], axis=1)
            )
    for spot in range(0, rows, 2):
        where = pl.ds(spot * BASE_PAD, 2 * BASE_PAD)
        high_ref[where, :], low_ref[where, :] = split_two(
            jnp.concatenate(early_rows[spot : spot + 2], axis=0)
        )
    spare = late_high_ref.shape[0] - HALF * BASE_PAD
    late_rows.append(jnp.zeros((spare, LATE), F32))
    late_high_ref[...], late_low_ref[...] = split_two(jnp.concatenate(late_rows, axis=0))


def edges_of(near_ref, far_ref):
    even = even_stripe()
    near = near_ref[...]
    far = far_ref[...]
    return jnp.where(even, far, near), jnp.where(even, near, far)


def fill_extended(ext, highs, lows, cores, pieces, near_ref, far_ref):
    rows, half = pieces[0].shape
    wide = half * cores
    fold = wide // 2
    ext[:, 0:LANES] = jnp.zeros((ext.shape[0], LANES), F32)
    ext[:, LANES + wide :] = jnp.zeros((ext.shape[0], LANES), F32)
    me = lax.axis_index("exp")
    for step in range(cores):
        start = lax.rem(me + step, cores) * half + LANES
        ext[8 : 8 + rows, pl.ds(pl.multiple_of(start, LANES), half)] = pieces[step][...]
    top, bottom = edges_of(near_ref, far_ref)
    for side in range(2):
        where = pl.ds(LANES + side * fold, fold)
        ext[0:8, where] = top[8 * side : 8 * side + 8]
        ext[8 + rows : 16 + rows, where] = bottom[8 * side : 8 * side + 8]
        spare = [
            top[16 + side : 17 + side],
            top[18 + side : 19 + side],
            bottom[16 + side : 17 + side],
            bottom[18 + side : 19 + side],
        ]
        ext[16 + rows : 24 + rows, where] = jnp.concatenate(spare + spare, axis=0)
    main = slice(0, GROUP)
    highs[main], lows[main] = split_two(ext[main])
    extra = ext[GROUP : GROUP + 8]
    span = extra.shape[1]
    early = lax.broadcasted_iota(jnp.int32, extra.shape, 0) < 4
    ahead = [extra] + [pltpu.roll(extra, span - part, 1) for part in range(1, 4)]
    lines = jnp.concatenate(
        [jnp.where(early, ahead[0], ahead[1]), jnp.where(early, ahead[2], ahead[3])], axis=0
    )
    highs[GROUP:], lows[GROUP:] = split_two(lines)


def spread_window(shifted, put):
    for tap in range(TAPS):
        put(tap * GROUP, shifted(tap, slice(0, GROUP)))
    for quad in range(MAIN_TILES):
        put(MAIN + 16 * quad, shifted(4 * quad, slice(GROUP, GROUP + 16)))


def clear_spare(refs):
    for ref in refs:
        wide = ref.shape[1]
        ref[TAPS * GROUP : MAIN] = jnp.zeros((MAIN - TAPS * GROUP, wide), BF16)
        ref[MAIN + EXTRA_ROWS :] = jnp.zeros((LANES - EXTRA_ROWS, wide), BF16)


def back_profile(horiz):
    steady = jnp.ones_like(horiz)
    square = 0.5 * (3.0 * horiz * horiz - 1.0)
    return [steady, horiz, steady, horiz, square, steady, horiz]


def put_halves(target, edge_ref, rows, first):
    fold = edge_ref.shape[1]
    for side in range(2):
        where = pl.ds(LANES + side * fold, fold)
        target[first : first + 8, where] = edge_ref[8 * side : 8 * side + 8]
        for line in range(2):
            spot = 16 + 2 * line + side
            target[rows + line : rows + line + 1, where] = edge_ref[spot : spot + 1]


def paired(values):
    span = values.shape[1]
    return jnp.concatenate([values, pltpu.roll(values, span - 1, 1)], axis=0)


def corner_block(lines):
    span = lines.shape[1]
    parts = [lines] + [pltpu.roll(lines, span - move, 1) for move in range(1, 8)]
    return jnp.concatenate(parts, axis=0)


def odd_rows(odd_ref, stamp, height):
    return jnp.broadcast_to(odd_ref[stamp : stamp + 1, :] == 1, (height, LANES))


def stamp_window(source, odd_ref, stamp, offset):
    height = source.shape[0]
    lane = lane_id(height)
    left = source[:, stamp * LANES : (stamp + 1) * LANES]
    centre = source[:, (stamp + 1) * LANES : (stamp + 2) * LANES]
    right = source[:, (stamp + 2) * LANES : (stamp + 3) * LANES]
    odd = jnp.where(lane < LANES // 4, right, centre)
    even = jnp.where(lane >= LANES - HALF, left, centre)
    odd = pltpu.roll(odd, (HALF + STAMP_W + offset) % LANES, 1)
    even = pltpu.roll(even, HALF + offset, 1)
    return jnp.where(odd_rows(odd_ref, stamp, height), odd, even)


def stamp_shifts(sources, targets, odd_ref, pair, moves):
    columns = slice(pair * LANES, (pair + 1) * LANES)
    for source, target in zip(sources, targets):
        first = stamp_window(source, odd_ref, 2 * pair, 0)
        second = stamp_window(source, odd_ref, 2 * pair + 1, STAMP_W)
        for spot, (tile, move) in enumerate(moves):
            a, b = first[16 * tile : 16 * tile + 16], second[16 * tile : 16 * tile + 16]
            if move:
                a = pltpu.roll(a, LANES - move, 1)
                b = pltpu.roll(b, LANES - move, 1)
            target[16 * spot : 16 * spot + 16, columns] = jnp.where(
                lane_id(16) < STAMP_W, a, b
            )


def three_products(high, low, xhigh, xlow):
    return (
        jnp.dot(high, xhigh, preferred_element_type=F32)
        + jnp.dot(low, xhigh, preferred_element_type=F32)
        + jnp.dot(high, xlow, preferred_element_type=F32)
    )


def design_line(bases, keep, target, horiz, profile, row, region_rows):
    own = bases * keep
    vert = position(jnp.full(horiz.shape, row, jnp.int32), region_rows)
    square = 0.5 * (3.0 * vert * vert - 1.0)
    steady = jnp.ones_like(vert)
    scale = jnp.concatenate([steady, steady, vert, vert, steady, square, square], axis=0)
    return jnp.concatenate(
        [own, own * horiz, own * vert, profile * scale * keep, target], axis=0
    ).astype(BF16)


def gram(design):
    return lax.dot_general(design, design, (((1,), (1,)), ((), ())), preferred_element_type=F32)


def early_kernel(cores, stripes, *refs):
    pieces = refs[:cores]
    (
        near_ref,
        science_ref,
        good_ref,
        odd_ref,
        high_ref,
        low_ref,
        total_ref,
        late_ref,
        aux_ref,
        ext,
        highs,
        lows,
        xhigh,
        xlow,
        bases,
    ) = refs[cores:]
    rows, half = pieces[0].shape
    wide = science_ref.shape[2]
    pairs = wide // (4 * STAMP_W)
    me = lax.axis_index("exp")
    ext[:, 0:LANES] = jnp.zeros((ext.shape[0], LANES), F32)
    ext[:, LANES + wide :] = jnp.zeros((ext.shape[0], LANES), F32)
    for step in range(cores):
        start = lax.rem(me + step, cores) * half + LANES
        ext[0:rows, pl.ds(pl.multiple_of(start, LANES), half)] = pieces[step][...]
    put_halves(ext, near_ref, rows + 8, rows)
    lines = jnp.concatenate(
        [ext[0:rows], paired(ext[rows : rows + 8]), corner_block(ext[rows + 8 : rows + 10])], axis=0
    )
    highs[...], lows[...] = split_two(lines)
    moves = [(0, tap) for tap in range(TAPS)]
    moves += [(1, 2 * step) for step in range(10)]
    moves += [(2, 8 * step) for step in range(3)]
    lane = lane_id(1)
    for pair in range(pairs):
        columns = slice(pair * LANES, (pair + 1) * LANES)
        stamp_shifts((highs, lows), (xhigh, xlow), odd_ref, pair, moves)
        odd = jnp.where(
            lane < STAMP_W,
            odd_ref[2 * pair : 2 * pair + 1],
            odd_ref[2 * pair + 1 : 2 * pair + 2] + 1,
        )
        horiz = position(4 * pair * STAMP_W + odd * STAMP_W + lane, wide)
        aux_ref[2 * rows : 2 * rows + 8, columns] = jnp.broadcast_to(horiz, (8, LANES))
        picked = []
        for source in (good_ref, science_ref):
            lower = source[0, :, 2 * pair * LANES : (2 * pair + 1) * LANES]
            upper = source[0, :, (2 * pair + 1) * LANES : (2 * pair + 2) * LANES]
            lower = jnp.where(
                odd_rows(odd_ref, 2 * pair, rows), pltpu.roll(lower, STAMP_W, 1), lower
            )
            upper = jnp.where(
                odd_rows(odd_ref, 2 * pair + 1, rows), upper, pltpu.roll(upper, STAMP_W, 1)
            )
            picked.append(jnp.where(lane_id(rows) < STAMP_W, lower, upper))
        aux_ref[0:rows, columns] = picked[0]
        aux_ref[rows : 2 * rows, columns] = picked[0] * picked[1]
    split = HALF * BASE_PAD
    chunk = 2 * LANES
    for start in range(0, wide // 2, chunk):
        span = slice(start, start + chunk)
        values = three_products(high_ref[...], low_ref[...], xhigh[:, span], xlow[:, span])
        late_ref[:, span] = values[:split]
        bases[:, span] = values[split:]
    horiz = aux_ref[2 * rows : 2 * rows + 1]
    profile = jnp.concatenate(back_profile(horiz), axis=0)
    first_line = jnp.where(even_stripe(), HALF, 0)
    first_row = lax.axis_index("stripe") * rows
    total = jnp.zeros((FIT_ROWS, FIT_ROWS), F32)
    for spot in range(rows - HALF):
        line = first_line + spot
        design = design_line(
            bases[spot * BASE_PAD : (spot + 1) * BASE_PAD],
            aux_ref[pl.ds(line, 1), :],
            aux_ref[pl.ds(rows + line, 1), :],
            horiz,
            profile,
            first_row + line,
            rows * stripes,
        )
        total = total + gram(design)
    total_ref[...] = jnp.concatenate(
        [total, jnp.zeros((FIT_ROWS, LANES - FIT_ROWS), F32)], axis=1
    )


def late_kernel(stripes, rows, *refs):
    (
        far_ref,
        odd_ref,
        high_ref,
        low_ref,
        total_ref,
        early_ref,
        aux_ref,
        out_ref,
        ext,
        highs,
        lows,
        xhigh,
        xlow,
        bases,
    ) = refs
    width = early_ref.shape[1]
    pairs = width // LANES
    ext[:, 0:LANES] = jnp.zeros((ext.shape[0], LANES), F32)
    ext[:, ext.shape[1] - LANES :] = jnp.zeros((ext.shape[0], LANES), F32)
    put_halves(ext, far_ref, 8, 0)
    lines = jnp.concatenate([paired(ext[0:8]), corner_block(ext[8:10])], axis=0)
    highs[...], lows[...] = split_two(lines)
    moves = [(0, 2 * step) for step in range(10)] + [(1, 8 * step) for step in range(3)]
    used = 16 * len(moves)
    for ref in (xhigh, xlow):
        ref[used:] = jnp.zeros((LATE - used, width), BF16)
    split = HALF * BASE_PAD
    chunk = 2 * LANES
    for start in range(0, width, chunk):
        span = slice(start, start + chunk)
        for pair in range(start // LANES, (start + chunk) // LANES):
            stamp_shifts((highs, lows), (xhigh, xlow), odd_ref, pair, moves)
        values = three_products(high_ref[...], low_ref[...], xhigh[:, span], xlow[:, span])
        bases[:, span] = early_ref[:, span] + values[:split]
    horiz = aux_ref[2 * rows : 2 * rows + 1]
    profile = jnp.concatenate(back_profile(horiz), axis=0)
    first_line = jnp.where(even_stripe(), 0, rows - HALF)
    first_row = lax.axis_index("stripe") * rows
    stack = 3
    total = jnp.zeros((stack * FIT_ROWS, stack * FIT_ROWS), F32)
    for begin in range(0, HALF, stack):
        designs = []
        for spot in range(begin, begin + stack):
            line = first_line + spot
            designs.append(
                design_line(
                    bases[spot * BASE_PAD : (spot + 1) * BASE_PAD],
                    aux_ref[pl.ds(line, 1), :],
                    aux_ref[pl.ds(rows + line, 1), :],
                    horiz,
                    profile,
                    first_row + line,
                    rows * stripes,
                )
            )
        total = total + gram(jnp.concatenate(designs, axis=0))
    own = total_ref[:, :FIT_ROWS]
    for spot in range(stack):
        where = slice(spot * FIT_ROWS, (spot + 1) * FIT_ROWS)
        own = own + total[where, where]
    out_ref[...] = jnp.concatenate([own, jnp.zeros((FIT_ROWS, LANES - FIT_ROWS), F32)], axis=1)


def panels():
    out = []
    for term in range(3):
        start = term * BASE_PAD
        out += [(start, 8), (start + 8, 8), (start + 16, BASES - 16)]
    return out + [(3 * BASE_PAD, BACK)]


def solve_rows(matrix):
    sub = row_id(8)
    tiles = [matrix[start : start + 8] for start in range(0, FIT_ROWS, 8)]

    def spread(tile, spot):
        return jnp.broadcast_to(tile[spot : spot + 1], (8, LANES))

    for start, size in panels():
        home = start // 8
        columns = [
            [jnp.broadcast_to(tile[:, start + j : start + j + 1], (8, LANES)) for tile in tiles]
            for j in range(size)
        ]
        corner = [column[home] for column in columns]
        rows = tiles[home]
        for spot in range(size):
            keep = sub == spot
            inverse = 1.0 / spread(corner[spot], spot)
            others = jnp.where(keep, 0.0, corner[spot])
            scaled = spread(rows, spot) * inverse
            rows = jnp.where(keep, scaled, rows - others * scaled)
            for j in range(spot + 1, size):
                scaled = spread(corner[j], spot) * inverse
                corner[j] = jnp.where(keep, scaled, corner[j] - others * scaled)
        for place in range(len(tiles)):
            if place == home:
                tiles[place] = rows
                continue
            change = columns[0][place] * spread(rows, 0)
            for j in range(1, size):
                change = change + columns[j][place] * spread(rows, j)
            tiles[place] = tiles[place] - change
    line = row_id(FIT_ROWS)
    used = (line >= 3 * BASE_PAD) | (lax.rem(line, BASE_PAD) < BASES)
    right = jnp.concatenate(tiles, axis=0)[:, FIT_ROWS - 1 : FIT_ROWS]
    return jnp.where(used, jnp.broadcast_to(right, (FIT_ROWS, LANES)), 0.0)


def spread_kernel(cores, *refs):
    pieces = refs[:cores]
    far_ref, near_ref, after_ref, xhigh, xlow, ext, highs, lows = refs[cores:]
    wide = xhigh.shape[1]
    fill_extended(ext, highs, lows, cores, pieces, near_ref, far_ref)
    clear_spare((xhigh, xlow))
    for source, target in ((highs, xhigh), (lows, xlow)):

        def shifted(tap, lines):
            start = LANES - HALF + tap
            return source[lines, start : start + wide]

        def put(place, values):
            target[place : place + values.shape[0]] = values

        spread_window(shifted, put)


def model_kernel(
    stripes,
    normal_ref,
    xhigh,
    xlow,
    far_ref,
    near_ref,
    science_ref,
    good_ref,
    base_ref,
    out_ref,
    coef_ref,
):
    rows = science_ref.shape[1]
    wide = science_ref.shape[2]
    top, bottom = edges_of(near_ref, far_ref)
    coef = solve_rows(normal_ref[...])
    lane = lane_id(FIT_ROWS)
    home = jnp.where(
        lane < 3 * BASES, lax.rem(lane, 3) * BASE_PAD + lane // 3, lane + 3 * (BASE_PAD - BASES)
    )
    flat = jnp.sum(jnp.where(row_id(FIT_ROWS) == home, coef, 0.0), axis=0, keepdims=True)
    coef_ref[...] = flat[:, : coef_ref.shape[1]]

    line = row_id(BASE_PAD)
    lane = lane_id(BASE_PAD)
    spot = lax.rem(lane, GROUP)
    shift = jnp.where(line == rows + 1, -2, line - 1)
    tap = spot - shift
    inside = (tap >= 0) & (tap < TAPS)
    corner = lax.rem(lane, 4)
    blocks = []
    for term in range(3):
        share = coef[term * BASE_PAD : (term + 1) * BASE_PAD]
        parts = []
        for tile in range(MAIN_TILES + 2):
            mixed = base_ref[:, tile * LANES : (tile + 1) * LANES] * share
            parts.append(jnp.broadcast_to(jnp.sum(mixed, axis=0, keepdims=True), (BASE_PAD, LANES)))
        wanted = []
        for tile in range(MAIN_TILES):
            moved = jnp.concatenate(
                [
                    pltpu.roll(
                        pltpu.roll(parts[tile][:8], (start - 1) % LANES, 1), 0, 1, stride=1, stride_axis=0
                    )
                    for start in range(0, BASE_PAD, 8)
                ],
                axis=0,
            )
            moved = jnp.where(line == rows + 1, pltpu.roll(parts[tile], LANES - 2, 1), moved)
            wanted.append(jnp.where(inside, moved, 0.0))
        outer, inner = parts[MAIN_TILES], parts[MAIN_TILES + 1]
        spare = jnp.where((line == rows + 1) & (corner < 2), outer, 0.0)
        spare = jnp.where((line == 0) & (corner < 2), inner, spare)
        spare = jnp.where((line == rows - 1) & (corner >= 2), inner, spare)
        spare = jnp.where((line == rows) & (corner >= 2), outer, spare)
        wanted.append(spare)
        blocks.append(jnp.concatenate(wanted, axis=1))
    blocks.append(jnp.zeros((8, DEPTH), F32))
    kernel_high, kernel_low = split_two(jnp.concatenate(blocks, axis=0))
    kernel_gap = kernel_high.shape[0]
    kernel_both = jnp.concatenate([kernel_high, kernel_low], axis=0)
    level = [coef[3 * BASE_PAD + m : 3 * BASE_PAD + m + 1, 0:1] for m in range(BACK)]
    first_row = lax.axis_index("stripe") * rows
    vert_line = jnp.where(line == rows + 1, -1, line)
    vert = position(first_row + vert_line, rows * stripes)[:, 0:1]
    vert_square = 0.5 * (3.0 * vert * vert - 1.0)
    chunk = min(4 * LANES, wide)
    outs = []
    for start in range(0, wide, chunk):
        span = slice(start, start + chunk)
        both = jnp.dot(kernel_both, xhigh[:, span], preferred_element_type=F32)
        lower = jnp.dot(kernel_high, xlow[:, span], preferred_element_type=F32)
        sums = both[: 3 * BASE_PAD] + (both[kernel_gap : kernel_gap + 3 * BASE_PAD] + lower[: 3 * BASE_PAD])
        horiz = position(start + lax.broadcasted_iota(jnp.int32, (1, chunk), 1), wide)
        horiz_square = 0.5 * (3.0 * horiz * horiz - 1.0)
        model = (
            sums[:BASE_PAD]
            + horiz * sums[BASE_PAD : 2 * BASE_PAD]
            + vert * sums[2 * BASE_PAD :]
            + (level[0] + level[1] * horiz + level[4] * horiz_square)
            + vert * (level[2] + level[3] * horiz)
            + vert_square * (level[5] + level[6] * horiz)
        )
        outs.append(model)
    model = jnp.concatenate(outs, axis=1)
    own = good_ref[0] * (science_ref[0] - model[:rows])

    def halo(edge, spot):
        science = jnp.concatenate([edge[20:21], edge[21:22]], axis=1)
        good = jnp.concatenate([edge[22:23], edge[23:24]], axis=1)
        return good * (science - model[spot : spot + 1])

    above_row = halo(top, rows + 1)
    below_row = halo(bottom, rows)
    lines = lax.broadcasted_iota(jnp.int32, (rows, wide), 0)
    spots = lax.broadcasted_iota(jnp.int32, (rows, wide), 1)
    above = jnp.where(lines == 0, above_row, pltpu.roll(own, 1, 0))
    below = jnp.where(lines == rows - 1, below_row, pltpu.roll(own, rows - 1, 0))
    before = jnp.where(spots == 0, 0.0, pltpu.roll(own, 1, 1))
    after = jnp.where(spots == wide - 1, 0.0, pltpu.roll(own, wide - 1, 1))
    out_ref[0] = 4.0 * own - (below + above + after + before)


def whole_vmem(count):
    return [pl.BlockSpec(memory_space=pltpu.VMEM)] * count


def summed(values, axis):
    count = lax.axis_size(axis)
    if count & (count - 1):
        return lax.psum(values, axis)
    step = 1
    while step < count:
        values = values + lax.ppermute(values, axis, [(i, i ^ step) for i in range(count)])
        step *= 2
    return values


def shards(template, exposure, cosmic_mask, stamp_blocks, row_filters, col_filters):
    arguments = (template, exposure, cosmic_mask, row_filters, col_filters, stamp_blocks)
    rows, half = template.shape
    wide = exposure.shape[2]
    cores = lax.axis_size("exp")
    stripes = lax.axis_size("stripe")
    params = pltpu.CompilerParams(vmem_limit_bytes=24 * 1024 * 1024)
    pieces = [template] + [
        lax.ppermute(template, "exp", [((i + step) % cores, i) for i in range(cores)])
        for step in range(1, cores)
    ]
    stamps = stamp_blocks.shape[1]
    template_in, science, good, row_in, col_in, odd = pl.pallas_call(
        load_kernel,
        out_shape=(
            jax.ShapeDtypeStruct(template.shape, F32),
            jax.ShapeDtypeStruct(exposure.shape, F32),
            jax.ShapeDtypeStruct(exposure.shape, F32),
            jax.ShapeDtypeStruct(row_filters.shape, F32),
            jax.ShapeDtypeStruct(col_filters.shape, F32),
            jax.ShapeDtypeStruct((stamps, LANES), jnp.int32),
        ),
        in_specs=[pl.BlockSpec(memory_space=pltpu.HBM)] * 6,
        out_specs=tuple(whole_vmem(6)),
        scratch_shapes=[
            pltpu.VMEM(cosmic_mask.shape, jnp.int32),
            pltpu.SMEM(stamp_blocks.shape, jnp.int32),
            pltpu.SemaphoreType.DMA((6,)),
        ],
        compiler_params=params,
        name="load",
    )(*[pltpu.with_memory_space_constraint(array, pltpu.HBM) for array in arguments])
    pieces = [template_in] + pieces[1:]
    edge_shape = jax.ShapeDtypeStruct((24, wide // 2), F32)

    def edge(toward_near, *others):
        return pl.pallas_call(
            functools.partial(edge_kernel, cores, toward_near),
            out_shape=edge_shape,
            in_specs=whole_vmem(cores + 2 + len(others)),
            out_specs=pl.BlockSpec(memory_space=pltpu.VMEM),
            scratch_shapes=[pltpu.VMEM((rows, wide), F32)],
            compiler_params=params,
            name="edges",
        )(*pieces, science, good, *others)

    far = edge(False)
    near = edge(True)
    near_pairs = [(i, i + 1) for i in range(0, stripes - 1, 2)]
    far_pairs = [(i, i + 1) for i in range(1, stripes - 1, 2)]

    def swapped(values, couples):
        return lax.ppermute(values, "stripe", couples + [(b, a) for a, b in couples])

    far = swapped(far, far_pairs)
    near = swapped(near, near_pairs)
    early_shape = jax.ShapeDtypeStruct((rows * BASE_PAD, EARLY), BF16)
    late_shape = jax.ShapeDtypeStruct((LATE_ROWS, LATE), BF16)
    high, low, late_high, late_low, base = pl.pallas_call(
        weight_kernel,
        out_shape=(
            early_shape,
            early_shape,
            late_shape,
            late_shape,
            jax.ShapeDtypeStruct((BASE_PAD, DEPTH + LANES), F32),
        ),
        in_specs=whole_vmem(2),
        out_specs=tuple(whole_vmem(5)),
        scratch_shapes=[pltpu.VMEM((2, BASE_PAD, LANES), F32)],
        compiler_params=params,
        name="weights",
    )(row_in, col_in)
    width = wide // 2
    reach = wide + 2 * LANES
    normal_shape = jax.ShapeDtypeStruct((FIT_ROWS, LANES), F32)
    part, kept, aux = pl.pallas_call(
        functools.partial(early_kernel, cores, stripes),
        out_shape=(
            normal_shape,
            jax.ShapeDtypeStruct((HALF * BASE_PAD, width), F32),
            jax.ShapeDtypeStruct((2 * rows + 8, width), F32),
        ),
        in_specs=whole_vmem(cores + 6),
        out_specs=tuple(whole_vmem(3)),
        scratch_shapes=[
            pltpu.VMEM((rows + 16, reach), F32),
            pltpu.VMEM((rows + 32, reach), BF16),
            pltpu.VMEM((rows + 32, reach), BF16),
            pltpu.VMEM((EARLY, width), BF16),
            pltpu.VMEM((EARLY, width), BF16),
            pltpu.VMEM(((rows - HALF) * BASE_PAD, width), F32),
        ],
        compiler_params=params,
        name="early",
    )(*pieces, near, science, good, odd, high, low)
    normal = pl.pallas_call(
        functools.partial(late_kernel, stripes, rows),
        out_shape=normal_shape,
        in_specs=whole_vmem(7),
        out_specs=pl.BlockSpec(memory_space=pltpu.VMEM),
        scratch_shapes=[
            pltpu.VMEM((16, reach), F32),
            pltpu.VMEM((32, reach), BF16),
            pltpu.VMEM((32, reach), BF16),
            pltpu.VMEM((LATE, width), BF16),
            pltpu.VMEM((LATE, width), BF16),
            pltpu.VMEM((HALF * BASE_PAD, width), F32),
        ],
        compiler_params=params,
        name="late",
    )(far, odd, late_high, late_low, part, kept, aux)
    ext_shapes = [
        pltpu.VMEM((rows + 24, wide + 2 * LANES), F32),
        pltpu.VMEM((GROUP + 16, wide + 2 * LANES), BF16),
        pltpu.VMEM((GROUP + 16, wide + 2 * LANES), BF16),
    ]
    wide_shape = jax.ShapeDtypeStruct((DEPTH, wide), BF16)
    xhigh, xlow = pl.pallas_call(
        functools.partial(spread_kernel, cores),
        out_shape=(wide_shape, wide_shape),
        in_specs=whole_vmem(cores + 3),
        out_specs=tuple(whole_vmem(2)),
        scratch_shapes=ext_shapes,
        compiler_params=params,
        name="spread",
    )(*pieces, far, near, normal)
    normal = summed(normal, "stripe")
    filtered, coef = pl.pallas_call(
        functools.partial(model_kernel, stripes),
        out_shape=(
            jax.ShapeDtypeStruct(exposure.shape, F32),
            jax.ShapeDtypeStruct((1, 3 * BASES + BACK), F32),
        ),
        in_specs=whole_vmem(8),
        out_specs=tuple(whole_vmem(2)),
        compiler_params=params,
        name="model",
    )(normal, xhigh, xlow, far, near, science, good, base)
    return filtered, coef


def solution(mesh):
    placed = (
        P(("groups", "stripe"), "exp"),
        P(("groups", "exp"), "stripe", None),
        P(("groups", "exp"), "stripe", None),
        P(("groups", "stripe"), None),
        P(),
        P(),
    )
    return jax.shard_map(
        shards,
        mesh=mesh,
        in_specs=placed,
        out_specs=(P(("groups", "exp"), "stripe", None), P(("groups", "exp"), None)),
        check_vma=False,
    )
```

```python
import functools

import jax
import jax.numpy as jnp
from jax import lax
from jax.experimental import pallas as pl
from jax.experimental.pallas import tpu as pltpu
from jax.sharding import PartitionSpec as P

HALF = 9
TAPS = 2 * HALF + 1
BASES = 19
STAMP_W = 64
LANES = 128
BASE_PAD = 24
BACK = 7
FIT_ROWS = 3 * BASE_PAD + BACK + 1
REACH = HALF + 1
GROUP = 32
GROUPS_TILE = LANES // GROUP
MAIN_TILES = 5
MAIN = MAIN_TILES * LANES
DEPTH = MAIN + LANES
EXTRA_ROWS = 80
NEAR_AT = TAPS * 16
NEAR_EXTRA_AT = NEAR_AT + 160
EARLY = NEAR_EXTRA_AT + 48
FAR_EXTRA_AT = 160
LATE = 2 * LANES
LATE_ROWS = -(-HALF * BASE_PAD // 16) * 16
F32 = jnp.float32
BF16 = jnp.bfloat16


def lane_id(rows):
    return lax.broadcasted_iota(jnp.int32, (rows, LANES), 1)


def row_id(rows):
    return lax.broadcasted_iota(jnp.int32, (rows, LANES), 0)


def split_two(values):
    high = values.astype(BF16)
    low = (values - high.astype(F32)).astype(BF16)
    return high, low


def position(index, total):
    return (2.0 * index.astype(F32) + 1.0) / total - 1.0


def even_stripe():
    return lax.rem(lax.axis_index("stripe"), 2) == 0


def edge_kernel(cores, toward_near, *refs):
    pieces = refs[:cores]
    science_ref, good_ref = refs[cores : cores + 2]
    edge_ref, ext = refs[-2:]
    rows, half = pieces[0].shape
    wide = science_ref.shape[2]
    me = lax.axis_index("exp")
    for step in range(cores):
        start = lax.rem(me + step, cores) * half
        ext[:, pl.ds(pl.multiple_of(start, LANES), half)] = pieces[step][...]
    fold = wide // 2
    low_first = rows - 8

    def edge(first, extra, outer):
        parts = [ext[first : first + 8, :fold], ext[first : first + 8, fold:]]
        tail = []
        for line in (extra, extra + 1):
            tail += [ext[line : line + 1, :fold], ext[line : line + 1, fold:]]
        science = science_ref[0, outer : outer + 1, :]
        good = good_ref[0, outer : outer + 1, :]
        for line in (science, good):
            tail += [line[:, :fold], line[:, fold:]]
        return jnp.concatenate(parts + tail, axis=0)

    bottom = edge(low_first, rows - REACH, rows - 1)
    top = edge(0, 8, 0)
    edge_ref[...] = jnp.where(even_stripe() == toward_near, bottom, top)


def load_kernel(
    template_hbm,
    science_hbm,
    good_hbm,
    row_hbm,
    col_hbm,
    stamps_hbm,
    template_ref,
    science_ref,
    good_ref,
    row_ref,
    col_ref,
    odd_ref,
    mask_ref,
    stamps_ref,
    sems,
):
    moves = [
        pltpu.make_async_copy(source, target, sems.at[spot])
        for spot, (source, target) in enumerate(
            [
                (science_hbm, science_ref),
                (good_hbm, mask_ref),
                (template_hbm, template_ref),
                (row_hbm, row_ref),
                (col_hbm, col_ref),
                (stamps_hbm, stamps_ref),
            ]
        )
    ]
    for move in moves:
        move.start()
    for move in moves:
        move.wait()
    good_ref[...] = mask_ref[...].astype(F32)
    odd_ref[...] = jnp.concatenate(
        [
            jnp.full((1, LANES), lax.rem(stamps_ref[0, stamp], 2), jnp.int32)
            for stamp in range(odd_ref.shape[0])
        ],
        axis=0,
    )


def weight_kernel(
    row_ref, col_ref, high_ref, low_ref, late_high_ref, late_low_ref, base_ref, pad
):
    pad[...] = jnp.zeros_like(pad)
    pad[0, 0:BASES, 0:TAPS] = row_ref[...]
    pad[1, 0:BASES, 0:TAPS] = col_ref[...]
    row = pad[0]
    lane = lane_id(BASE_PAD)
    group = lane // GROUP
    tiled = row
    for part in range(1, GROUPS_TILE):
        tiled = tiled + pltpu.roll(row, part * GROUP, 1)
    columns = [
        jnp.broadcast_to(pad[1, :, tap : tap + 1], (BASE_PAD, LANES)) for tap in range(TAPS)
    ]
    zero = jnp.zeros((BASE_PAD, LANES), F32)
    mains = []
    for tile in range(MAIN_TILES):
        spread = zero
        for part in range(GROUPS_TILE):
            tap = tile * GROUPS_TILE + part
            if tap < TAPS:
                spread = jnp.where(group == part, columns[tap], spread)
        mains.append(tiled * spread)
    spread = zero
    for tap in range(TAPS):
        spread = jnp.where(lane // 4 == tap, columns[tap], spread)
    corner = lax.rem(lane, 4)

    def tap_at(tap):
        return jnp.broadcast_to(pad[0, :, tap : tap + 1], (BASE_PAD, LANES))

    outer = jnp.where(
        corner == 0,
        tap_at(0),
        jnp.where(corner == 1, tap_at(1), jnp.where(corner == 2, tap_at(TAPS - 2), tap_at(TAPS - 1))),
    )
    inner = jnp.where(corner == 1, tap_at(0), jnp.where(corner == 2, tap_at(TAPS - 1), 0.0))
    outer = outer * spread
    inner = inner * spread
    for tile in range(MAIN_TILES):
        base_ref[:, tile * LANES : (tile + 1) * LANES] = mains[tile]
    base_ref[:, MAIN : MAIN + LANES] = outer
    base_ref[:, MAIN + LANES :] = inner
    rows = high_ref.shape[0] // BASE_PAD
    even = even_stripe()
    first_tap, last_tap = tap_at(0), tap_at(TAPS - 1)

    def column_tile(tap_of):
        spread = zero
        begin = 0
        for end in range(1, LANES + 1):
            if end < LANES and tap_of(end) == tap_of(begin):
                continue
            if tap_of(begin) < TAPS:
                spread = jnp.where((lane >= begin) & (lane < end), columns[tap_of(begin)], spread)
            begin = end
        return spread

    def early_tap(place):
        if place < NEAR_AT:
            return place // 16
        return (place - NEAR_AT) // 8 if place < NEAR_EXTRA_AT else (place - NEAR_EXTRA_AT) // 2

    def late_tap(place):
        return place // 8 if place < FAR_EXTRA_AT else (place - FAR_EXTRA_AT) // 2

    early_tiles = [
        column_tile(lambda spot, tile=tile: early_tap(tile * LANES + spot))
        for tile in range(EARLY // LANES)
    ]
    late_tiles = [
        column_tile(lambda spot, tile=tile: late_tap(tile * LANES + spot))
        for tile in range(LATE // LANES)
    ]

    def repeats(period):
        blocks = []
        for start in range(0, TAPS, period):
            block = pltpu.roll(row, (LANES - start) % LANES, 1) if start else row
            block = jnp.where(lane < period, block, 0.0)
            size = period
            while size < LANES:
                block = block + pltpu.roll(block, size, 1)
                size *= 2
            blocks.append(block)
        return blocks

    def window(blocks, period, first):
        block, move = first // period, first % period
        here = blocks[block] if 0 <= block < len(blocks) else None
        beyond = blocks[block + 1] if 0 <= block + 1 < len(blocks) else None
        if move == 0:
            return zero if here is None else here
        ready = lax.rem(lane, period) < period - move
        parts = [zero if part is None else pltpu.roll(part, LANES - move, 1) for part in (here, beyond)]
        return jnp.where(ready, parts[0], parts[1])

    by_sixteen, by_eight = repeats(16), repeats(8)
    own_rows = [window(by_sixteen, 16, HALF - line) for line in range(rows)]
    top_rows = [window(by_eight, 8, 1 - line) for line in range(rows)]
    bottom_rows = [window(by_eight, 8, rows + HALF - line) for line in range(rows)]

    parity = lax.rem(lane, 2)

    def corner_taps(upper, lower, is_upper):
        top = jnp.where(parity == 1, first_tap, 0.0) if upper else zero
        bottom = jnp.where(parity == 0, last_tap, 0.0) if lower else zero
        return jnp.where(is_upper, top, bottom)

    near_is_top = ~even
    early_rows, late_rows = [], []
    for spot in range(rows):
        odd_line = spot + rows - HALF if spot < HALF else spot - HALF
        own = jnp.where(even, own_rows[spot], own_rows[odd_line])
        side = jnp.where(even, bottom_rows[spot], top_rows[odd_line])
        extra = zero
        if spot >= HALF:
            extra = corner_taps(spot == HALF, spot == rows - 1, near_is_top)
        tiles = [
            own,
            own,
            jnp.where(lane < NEAR_AT - 2 * LANES, own, side),
            jnp.where(lane < NEAR_EXTRA_AT - 3 * LANES, side, extra),
        ]
        early_rows.append(
            jnp.concatenate([mine * tile for mine, tile in zip(tiles, early_tiles)], axis=1)
        )
        if spot < HALF:
            side = jnp.where(even, top_rows[spot], bottom_rows[odd_line])
            extra = corner_taps(spot == 0, spot == HALF - 1, even)
            tiles = [side, jnp.where(lane < FAR_EXTRA_AT - LANES, side, extra)]
            late_rows.append(
                jnp.concatenate([mine * tile for mine, tile in zip(tiles, late_tiles)], axis=1)
            )
    for spot in range(0, rows, 2):
        where = pl.ds(spot * BASE_PAD, 2 * BASE_PAD)
        high_ref[where, :], low_ref[where, :] = split_two(
            jnp.concatenate(early_rows[spot : spot + 2], axis=0)
        )
    spare = late_high_ref.shape[0] - HALF * BASE_PAD
    late_rows.append(jnp.zeros((spare, LATE), F32))
    late_high_ref[...], late_low_ref[...] = split_two(jnp.concatenate(late_rows, axis=0))


def edges_of(near_ref, far_ref):
    even = even_stripe()
    near = near_ref[...]
    far = far_ref[...]
    return jnp.where(even, far, near), jnp.where(even, near, far)


def fill_extended(ext, highs, lows, cores, pieces, near_ref, far_ref):
    rows, half = pieces[0].shape
    wide = half * cores
    fold = wide // 2
    ext[:, 0:LANES] = jnp.zeros((ext.shape[0], LANES), F32)
    ext[:, LANES + wide :] = jnp.zeros((ext.shape[0], LANES), F32)
    me = lax.axis_index("exp")
    for step in range(cores):
        start = lax.rem(me + step, cores) * half + LANES
        ext[8 : 8 + rows, pl.ds(pl.multiple_of(start, LANES), half)] = pieces[step][...]
    top, bottom = edges_of(near_ref, far_ref)
    for side in range(2):
        where = pl.ds(LANES + side * fold, fold)
        ext[0:8, where] = top[8 * side : 8 * side + 8]
        ext[8 + rows : 16 + rows, where] = bottom[8 * side : 8 * side + 8]
        spare = [
            top[16 + side : 17 + side],
            top[18 + side : 19 + side],
            bottom[16 + side : 17 + side],
            bottom[18 + side : 19 + side],
        ]
        ext[16 + rows : 24 + rows, where] = jnp.concatenate(spare + spare, axis=0)
    main = slice(0, GROUP)
    highs[main], lows[main] = split_two(ext[main])
    extra = ext[GROUP : GROUP + 8]
    span = extra.shape[1]
    early = lax.broadcasted_iota(jnp.int32, extra.shape, 0) < 4
    ahead = [extra] + [pltpu.roll(extra, span - part, 1) for part in range(1, 4)]
    lines = jnp.concatenate(
        [jnp.where(early, ahead[0], ahead[1]), jnp.where(early, ahead[2], ahead[3])], axis=0
    )
    highs[GROUP:], lows[GROUP:] = split_two(lines)


def spread_window(shifted, put):
    for tap in range(TAPS):
        put(tap * GROUP, shifted(tap, slice(0, GROUP)))
    for quad in range(MAIN_TILES):
        put(MAIN + 16 * quad, shifted(4 * quad, slice(GROUP, GROUP + 16)))


def clear_spare(refs):
    for ref in refs:
        wide = ref.shape[1]
        ref[TAPS * GROUP : MAIN] = jnp.zeros((MAIN - TAPS * GROUP, wide), BF16)
        ref[MAIN + EXTRA_ROWS :] = jnp.zeros((LANES - EXTRA_ROWS, wide), BF16)


def back_profile(horiz):
    steady = jnp.ones_like(horiz)
    square = 0.5 * (3.0 * horiz * horiz - 1.0)
    return [steady, horiz, steady, horiz, square, steady, horiz]


def put_halves(target, edge_ref, rows, first):
    fold = edge_ref.shape[1]
    for side in range(2):
        where = pl.ds(LANES + side * fold, fold)
        target[first : first + 8, where] = edge_ref[8 * side : 8 * side + 8]
        for line in range(2):
            spot = 16 + 2 * line + side
            target[rows + line : rows + line + 1, where] = edge_ref[spot : spot + 1]


def paired(values):
    span = values.shape[1]
    return jnp.concatenate([values, pltpu.roll(values, span - 1, 1)], axis=0)


def corner_block(lines):
    span = lines.shape[1]
    parts = [lines] + [pltpu.roll(lines, span - move, 1) for move in range(1, 8)]
    return jnp.concatenate(parts, axis=0)


def odd_rows(odd_ref, stamp, height):
    return jnp.broadcast_to(odd_ref[stamp : stamp + 1, :] == 1, (height, LANES))


def stamp_window(source, odd_ref, stamp, offset):
    height = source.shape[0]
    lane = lane_id(height)
    left = source[:, stamp * LANES : (stamp + 1) * LANES]
    centre = source[:, (stamp + 1) * LANES : (stamp + 2) * LANES]
    right = source[:, (stamp + 2) * LANES : (stamp + 3) * LANES]
    odd = jnp.where(lane < LANES // 4, right, centre)
    even = jnp.where(lane >= LANES - HALF, left, centre)
    odd = pltpu.roll(odd, (HALF + STAMP_W + offset) % LANES, 1)
    even = pltpu.roll(even, HALF + offset, 1)
    return jnp.where(odd_rows(odd_ref, stamp, height), odd, even)


def stamp_shifts(sources, targets, odd_ref, pair, moves):
    columns = slice(pair * LANES, (pair + 1) * LANES)
    for source, target in zip(sources, targets):
        first = stamp_window(source, odd_ref, 2 * pair, 0)
        second = stamp_window(source, odd_ref, 2 * pair + 1, STAMP_W)
        for spot, (tile, move) in enumerate(moves):
            a, b = first[16 * tile : 16 * tile + 16], second[16 * tile : 16 * tile + 16]
            if move:
                a = pltpu.roll(a, LANES - move, 1)
                b = pltpu.roll(b, LANES - move, 1)
            target[16 * spot : 16 * spot + 16, columns] = jnp.where(
                lane_id(16) < STAMP_W, a, b
            )


def three_products(high, low, xhigh, xlow):
    return (
        jnp.dot(high, xhigh, preferred_element_type=F32)
        + jnp.dot(low, xhigh, preferred_element_type=F32)
        + jnp.dot(high, xlow, preferred_element_type=F32)
    )


def design_line(bases, keep, target, horiz, profile, row, region_rows):
    own = bases * keep
    vert = position(jnp.full(horiz.shape, row, jnp.int32), region_rows)
    square = 0.5 * (3.0 * vert * vert - 1.0)
    steady = jnp.ones_like(vert)
    scale = jnp.concatenate([steady, steady, vert, vert, steady, square, square], axis=0)
    return jnp.concatenate(
        [own, own * horiz, own * vert, profile * scale * keep, target], axis=0
    ).astype(BF16)


def gram(design):
    return lax.dot_general(design, design, (((1,), (1,)), ((), ())), preferred_element_type=F32)


def early_kernel(cores, stripes, *refs):
    pieces = refs[:cores]
    (
        near_ref,
        science_ref,
        good_ref,
        odd_ref,
        high_ref,
        low_ref,
        total_ref,
        late_ref,
        aux_ref,
        ext,
        highs,
        lows,
        xhigh,
        xlow,
        bases,
    ) = refs[cores:]
    rows, half = pieces[0].shape
    wide = science_ref.shape[2]
    pairs = wide // (4 * STAMP_W)
    me = lax.axis_index("exp")
    ext[:, 0:LANES] = jnp.zeros((ext.shape[0], LANES), F32)
    ext[:, LANES + wide :] = jnp.zeros((ext.shape[0], LANES), F32)
    for step in range(cores):
        start = lax.rem(me + step, cores) * half + LANES
        ext[0:rows, pl.ds(pl.multiple_of(start, LANES), half)] = pieces[step][...]
    put_halves(ext, near_ref, rows + 8, rows)
    lines = jnp.concatenate(
        [ext[0:rows], paired(ext[rows : rows + 8]), corner_block(ext[rows + 8 : rows + 10])], axis=0
    )
    highs[...], lows[...] = split_two(lines)
    moves = [(0, tap) for tap in range(TAPS)]
    moves += [(1, 2 * step) for step in range(10)]
    moves += [(2, 8 * step) for step in range(3)]
    lane = lane_id(1)
    for pair in range(pairs):
        columns = slice(pair * LANES, (pair + 1) * LANES)
        stamp_shifts((highs, lows), (xhigh, xlow), odd_ref, pair, moves)
        odd = jnp.where(
            lane < STAMP_W,
            odd_ref[2 * pair : 2 * pair + 1],
            odd_ref[2 * pair + 1 : 2 * pair + 2] + 1,
        )
        horiz = position(4 * pair * STAMP_W + odd * STAMP_W + lane, wide)
        aux_ref[2 * rows : 2 * rows + 8, columns] = jnp.broadcast_to(horiz, (8, LANES))
        picked = []
        for source in (good_ref, science_ref):
            lower = source[0, :, 2 * pair * LANES : (2 * pair + 1) * LANES]
            upper = source[0, :, (2 * pair + 1) * LANES : (2 * pair + 2) * LANES]
            lower = jnp.where(
                odd_rows(odd_ref, 2 * pair, rows), pltpu.roll(lower, STAMP_W, 1), lower
            )
            upper = jnp.where(
                odd_rows(odd_ref, 2 * pair + 1, rows), upper, pltpu.roll(upper, STAMP_W, 1)
            )
            picked.append(jnp.where(lane_id(rows) < STAMP_W, lower, upper))
        aux_ref[0:rows, columns] = picked[0]
        aux_ref[rows : 2 * rows, columns] = picked[0] * picked[1]
    split = HALF * BASE_PAD
    chunk = 2 * LANES
    for start in range(0, wide // 2, chunk):
        span = slice(start, start + chunk)
        values = three_products(high_ref[...], low_ref[...], xhigh[:, span], xlow[:, span])
        late_ref[:, span] = values[:split]
        bases[:, span] = values[split:]
    horiz = aux_ref[2 * rows : 2 * rows + 1]
    profile = jnp.concatenate(back_profile(horiz), axis=0)
    first_line = jnp.where(even_stripe(), HALF, 0)
    first_row = lax.axis_index("stripe") * rows
    total = jnp.zeros((FIT_ROWS, FIT_ROWS), F32)
    for spot in range(rows - HALF):
        line = first_line + spot
        design = design_line(
            bases[spot * BASE_PAD : (spot + 1) * BASE_PAD],
            aux_ref[pl.ds(line, 1), :],
            aux_ref[pl.ds(rows + line, 1), :],
            horiz,
            profile,
            first_row + line,
            rows * stripes,
        )
        total = total + gram(design)
    total_ref[...] = jnp.concatenate(
        [total, jnp.zeros((FIT_ROWS, LANES - FIT_ROWS), F32)], axis=1
    )


def late_kernel(stripes, rows, *refs):
    (
        far_ref,
        odd_ref,
        high_ref,
        low_ref,
        total_ref,
        early_ref,
        aux_ref,
        out_ref,
        ext,
        highs,
        lows,
        xhigh,
        xlow,
        bases,
    ) = refs
    width = early_ref.shape[1]
    pairs = width // LANES
    ext[:, 0:LANES] = jnp.zeros((ext.shape[0], LANES), F32)
    ext[:, ext.shape[1] - LANES :] = jnp.zeros((ext.shape[0], LANES), F32)
    put_halves(ext, far_ref, 8, 0)
    lines = jnp.concatenate([paired(ext[0:8]), corner_block(ext[8:10])], axis=0)
    highs[...], lows[...] = split_two(lines)
    moves = [(0, 2 * step) for step in range(10)] + [(1, 8 * step) for step in range(3)]
    used = 16 * len(moves)
    for ref in (xhigh, xlow):
        ref[used:] = jnp.zeros((LATE - used, width), BF16)
    split = HALF * BASE_PAD
    chunk = 2 * LANES
    for start in range(0, width, chunk):
        span = slice(start, start + chunk)
        for pair in range(start // LANES, (start + chunk) // LANES):
            stamp_shifts((highs, lows), (xhigh, xlow), odd_ref, pair, moves)
        values = three_products(high_ref[...], low_ref[...], xhigh[:, span], xlow[:, span])
        bases[:, span] = early_ref[:, span] + values[:split]
    horiz = aux_ref[2 * rows : 2 * rows + 1]
    profile = jnp.concatenate(back_profile(horiz), axis=0)
    first_line = jnp.where(even_stripe(), 0, rows - HALF)
    first_row = lax.axis_index("stripe") * rows
    stack = 3
    total = jnp.zeros((stack * FIT_ROWS, stack * FIT_ROWS), F32)
    for begin in range(0, HALF, stack):
        designs = []
        for spot in range(begin, begin + stack):
            line = first_line + spot
            designs.append(
                design_line(
                    bases[spot * BASE_PAD : (spot + 1) * BASE_PAD],
                    aux_ref[pl.ds(line, 1), :],
                    aux_ref[pl.ds(rows + line, 1), :],
                    horiz,
                    profile,
                    first_row + line,
                    rows * stripes,
                )
            )
        total = total + gram(jnp.concatenate(designs, axis=0))
    own = total_ref[:, :FIT_ROWS]
    for spot in range(stack):
        where = slice(spot * FIT_ROWS, (spot + 1) * FIT_ROWS)
        own = own + total[where, where]
    out_ref[...] = jnp.concatenate([own, jnp.zeros((FIT_ROWS, LANES - FIT_ROWS), F32)], axis=1)


def panels():
    out = []
    for term in range(3):
        start = term * BASE_PAD
        out += [(start, 8), (start + 8, 8), (start + 16, BASES - 16)]
    return out + [(3 * BASE_PAD, BACK)]


def solve_rows(matrix):
    sub = row_id(8)
    tiles = [matrix[start : start + 8] for start in range(0, FIT_ROWS, 8)]

    def spread(tile, spot):
        return jnp.broadcast_to(tile[spot : spot + 1], (8, LANES))

    for start, size in panels():
        home = start // 8
        columns = [
            [jnp.broadcast_to(tile[:, start + j : start + j + 1], (8, LANES)) for tile in tiles]
            for j in range(size)
        ]
        corner = [column[home] for column in columns]
        rows = tiles[home]
        for spot in range(size):
            keep = sub == spot
            inverse = 1.0 / spread(corner[spot], spot)
            others = jnp.where(keep, 0.0, corner[spot])
            scaled = spread(rows, spot) * inverse
            rows = jnp.where(keep, scaled, rows - others * scaled)
            for j in range(spot + 1, size):
                scaled = spread(corner[j], spot) * inverse
                corner[j] = jnp.where(keep, scaled, corner[j] - others * scaled)
        for place in range(len(tiles)):
            if place == home:
                tiles[place] = rows
                continue
            change = columns[0][place] * spread(rows, 0)
            for j in range(1, size):
                change = change + columns[j][place] * spread(rows, j)
            tiles[place] = tiles[place] - change
    line = row_id(FIT_ROWS)
    used = (line >= 3 * BASE_PAD) | (lax.rem(line, BASE_PAD) < BASES)
    right = jnp.concatenate(tiles, axis=0)[:, FIT_ROWS - 1 : FIT_ROWS]
    return jnp.where(used, jnp.broadcast_to(right, (FIT_ROWS, LANES)), 0.0)


def region_weights(base_ref, high_ref, low_ref, rows):
    lane = lane_id(8)
    spot = lax.rem(lane, GROUP)
    corner = lax.rem(lane, 4)
    line = row_id(8)
    mains = [base_ref[:, tile * LANES : (tile + 1) * LANES] for tile in range(MAIN_TILES)]
    outer = base_ref[:, MAIN : MAIN + LANES]
    inner = base_ref[:, MAIN + LANES :]
    blocks = [[] for _ in range(BASES)]
    for start in range(0, rows, 8):
        tap = spot - (start + line - 1)
        inside = (tap >= 0) & (tap < TAPS)
        moved = [pltpu.roll(main, (start - 1) % LANES, 1) for main in mains]
        extra = zero_row = jnp.zeros((8, LANES), F32)
        for b in range(BASES):
            tiles = []
            for main in moved:
                wide = jnp.broadcast_to(main[b : b + 1], (8, LANES))
                tiles.append(
                    jnp.where(inside, pltpu.roll(wide, 0, 1, stride=1, stride_axis=0), 0.0)
                )
            extra = zero_row
            mine = jnp.broadcast_to(inner[b : b + 1], (8, LANES))
            if start == 0:
                extra = jnp.where((line == 0) & (corner < 2), mine, extra)
            if start == rows - 8:
                extra = jnp.where((line == 7) & (corner >= 2), mine, extra)
            blocks[b].append(jnp.concatenate(tiles + [extra], axis=1))
    for b in range(BASES):
        where = pl.ds(b * rows, rows)
        high_ref[where, :], low_ref[where, :] = split_two(jnp.concatenate(blocks[b], axis=0))
    lane = lane_id(BASE_PAD)
    spot = lax.rem(lane, GROUP)
    corner = lax.rem(lane, 4)
    halos = []
    for shift, extra in ((rows - 1, corner >= 2), (-2, corner < 2)):
        tap = spot - shift
        inside = (tap >= 0) & (tap < TAPS)
        tiles = [jnp.where(inside, pltpu.roll(main, shift % LANES, 1), 0.0) for main in mains]
        halos.append(jnp.concatenate(tiles + [jnp.where(extra, outer, 0.0)], axis=1))
    where = pl.ds(BASES * rows, 2 * BASE_PAD)
    high_ref[where, :], low_ref[where, :] = split_two(jnp.concatenate(halos, axis=0))


def region_bases(highs, lows, high_ref, low_ref, first, out_ref, xhigh, xlow):
    clear_spare((xhigh, xlow))
    wide = out_ref.shape[1]
    chunk = 2 * LANES
    for start in range(0, wide, chunk):
        span = slice(start, start + chunk)
        for source, target in ((highs, xhigh), (lows, xlow)):

            def shifted(tap, lines):
                begin = first + start + LANES - HALF + tap
                return source[lines, begin : begin + chunk]

            def put(place, values):
                target[place : place + values.shape[0], span] = values

            spread_window(shifted, put)
        out_ref[:, span] = three_products(
            high_ref[...], low_ref[...], xhigh[:, span], xlow[:, span]
        )


def first_bases_kernel(cores, *refs):
    pieces = refs[:cores]
    (
        far_ref,
        near_ref,
        base_ref,
        after_ref,
        high_ref,
        low_ref,
        highs,
        lows,
        out_ref,
        ext,
        xhigh,
        xlow,
    ) = refs[cores:]
    region_weights(base_ref, high_ref, low_ref, pieces[0].shape[0])
    fill_extended(ext, highs, lows, cores, pieces, near_ref, far_ref)
    region_bases(highs, lows, high_ref, low_ref, 0, out_ref, xhigh, xlow)


def next_bases_kernel(first, highs, lows, high_ref, low_ref, after_ref, out_ref, xhigh, xlow):
    region_bases(highs, lows, high_ref, low_ref, first, out_ref, xhigh, xlow)


def add_kernel(mine_ref, other_ref, after_ref, out_ref):
    out_ref[...] = mine_ref[...] + other_ref[...]


def model_kernel(stripes, normal_ref, *refs):
    far_ref, near_ref, science_ref, good_ref, out_ref, coef_ref = refs[-6:]
    parts = refs[:-6]
    rows = science_ref.shape[1]
    wide = science_ref.shape[2]
    top, bottom = edges_of(near_ref, far_ref)
    coef = solve_rows(normal_ref[...])
    lane = lane_id(FIT_ROWS)
    home = jnp.where(
        lane < 3 * BASES, lax.rem(lane, 3) * BASE_PAD + lane // 3, lane + 3 * (BASE_PAD - BASES)
    )
    flat = jnp.sum(jnp.where(row_id(FIT_ROWS) == home, coef, 0.0), axis=0, keepdims=True)
    coef_ref[...] = flat[:, : coef_ref.shape[1]]

    def share(spot, height):
        return jnp.broadcast_to(coef[spot : spot + 1], (height, LANES))

    first_row = lax.axis_index("stripe") * rows
    vert = position(first_row + row_id(rows), rows * stripes)
    halo_vert = [
        position(jnp.full((8, LANES), first_row + line, jnp.int32), rows * stripes)
        for line in (rows, -1)
    ]
    slopes = [share(2 * BASE_PAD + b, rows) * vert for b in range(BASES)]
    halo_slopes = [
        coef[2 * BASE_PAD : 3 * BASE_PAD] * jnp.concatenate([line] * 3, axis=0) for line in halo_vert
    ]
    level = [share(3 * BASE_PAD + m, 8) for m in range(BACK)]

    def ground(here, horiz):
        square = 0.5 * (3.0 * here * here - 1.0)
        horiz_square = 0.5 * (3.0 * horiz * horiz - 1.0)
        steady = level[0] + level[1] * horiz + level[4] * horiz_square
        sloped = level[2] + level[3] * horiz
        curved = level[5] + level[6] * horiz
        if here.shape[0] > 8:
            steady, sloped, curved = (
                jnp.concatenate([part] * (here.shape[0] // 8), axis=0)
                for part in (steady, sloped, curved)
            )
        return steady + here * sloped + square * curved

    models, halos = [], [[], []]
    for part in parts:
        for start in range(0, part.shape[1], LANES):
            span = slice(start, start + LANES)
            begin = len(models) * LANES
            horiz = position(begin + lane_id(8), wide)
            total = ground(vert, horiz)
            for b in range(BASES):
                steady = share(b, 8) + share(BASE_PAD + b, 8) * horiz
                scale = jnp.concatenate([steady] * (rows // 8), axis=0) + slopes[b]
                total = total + part[b * rows : (b + 1) * rows, span] * scale
            models.append(total)
            steady = coef[:BASE_PAD] + coef[BASE_PAD : 2 * BASE_PAD] * horiz[0:1]
            for side in range(2):
                place = BASES * rows + side * BASE_PAD
                values = part[place : place + BASE_PAD, span] * (steady + halo_slopes[side])
                values = jnp.sum(values, axis=0, keepdims=True)
                halos[side].append(values + ground(halo_vert[side], horiz)[0:1])
    model = jnp.concatenate(models, axis=1)
    below_model, above_model = (jnp.concatenate(side, axis=1) for side in halos)
    own = good_ref[0] * (science_ref[0] - model)

    def halo(edge, values):
        science = jnp.concatenate([edge[20:21], edge[21:22]], axis=1)
        good = jnp.concatenate([edge[22:23], edge[23:24]], axis=1)
        return good * (science - values)

    above_row = halo(top, above_model)
    below_row = halo(bottom, below_model)
    lines = lax.broadcasted_iota(jnp.int32, (rows, wide), 0)
    spots = lax.broadcasted_iota(jnp.int32, (rows, wide), 1)
    above = jnp.where(lines == 0, above_row, pltpu.roll(own, 1, 0))
    below = jnp.where(lines == rows - 1, below_row, pltpu.roll(own, rows - 1, 0))
    before = jnp.where(spots == 0, 0.0, pltpu.roll(own, 1, 1))
    after = jnp.where(spots == wide - 1, 0.0, pltpu.roll(own, wide - 1, 1))
    out_ref[0] = 4.0 * own - (below + above + after + before)


def whole_vmem(count):
    return [pl.BlockSpec(memory_space=pltpu.VMEM)] * count


def add(values, other, after, params):
    return pl.pallas_call(
        add_kernel,
        out_shape=jax.ShapeDtypeStruct(values.shape, values.dtype),
        in_specs=whole_vmem(3),
        out_specs=pl.BlockSpec(memory_space=pltpu.VMEM),
        compiler_params=params,
        name="add",
    )(values, other, after)


def summed(values, axis, beside, params):
    count = lax.axis_size(axis)
    if count & (count - 1):
        for work in beside:
            work(values)
        return lax.psum(values, axis)
    step = 1
    waiting = list(beside)
    while step < count:
        other = lax.ppermute(values, axis, [(i, i ^ step) for i in range(count)])
        if waiting:
            values = add(values, other, waiting.pop(0)(values), params)
        else:
            values = values + other
        step *= 2
    for work in waiting:
        work(values)
    return values


def shards(template, exposure, cosmic_mask, stamp_blocks, row_filters, col_filters):
    arguments = (template, exposure, cosmic_mask, row_filters, col_filters, stamp_blocks)
    rows, half = template.shape
    wide = exposure.shape[2]
    cores = lax.axis_size("exp")
    stripes = lax.axis_size("stripe")
    params = pltpu.CompilerParams(vmem_limit_bytes=24 * 1024 * 1024)
    pieces = [template] + [
        lax.ppermute(template, "exp", [((i + step) % cores, i) for i in range(cores)])
        for step in range(1, cores)
    ]
    stamps = stamp_blocks.shape[1]
    template_in, science, good, row_in, col_in, odd = pl.pallas_call(
        load_kernel,
        out_shape=(
            jax.ShapeDtypeStruct(template.shape, F32),
            jax.ShapeDtypeStruct(exposure.shape, F32),
            jax.ShapeDtypeStruct(exposure.shape, F32),
            jax.ShapeDtypeStruct(row_filters.shape, F32),
            jax.ShapeDtypeStruct(col_filters.shape, F32),
            jax.ShapeDtypeStruct((stamps, LANES), jnp.int32),
        ),
        in_specs=[pl.BlockSpec(memory_space=pltpu.HBM)] * 6,
        out_specs=tuple(whole_vmem(6)),
        scratch_shapes=[
            pltpu.VMEM(cosmic_mask.shape, jnp.int32),
            pltpu.SMEM(stamp_blocks.shape, jnp.int32),
            pltpu.SemaphoreType.DMA((6,)),
        ],
        compiler_params=params,
        name="load",
    )(*[pltpu.with_memory_space_constraint(array, pltpu.HBM) for array in arguments])
    pieces = [template_in] + pieces[1:]
    edge_shape = jax.ShapeDtypeStruct((24, wide // 2), F32)

    def edge(toward_near, *others):
        return pl.pallas_call(
            functools.partial(edge_kernel, cores, toward_near),
            out_shape=edge_shape,
            in_specs=whole_vmem(cores + 2 + len(others)),
            out_specs=pl.BlockSpec(memory_space=pltpu.VMEM),
            scratch_shapes=[pltpu.VMEM((rows, wide), F32)],
            compiler_params=params,
            name="edges",
        )(*pieces, science, good, *others)

    far = edge(False)
    near = edge(True)
    near_pairs = [(i, i + 1) for i in range(0, stripes - 1, 2)]
    far_pairs = [(i, i + 1) for i in range(1, stripes - 1, 2)]

    def swapped(values, couples):
        return lax.ppermute(values, "stripe", couples + [(b, a) for a, b in couples])

    far = swapped(far, far_pairs)
    near = swapped(near, near_pairs)
    early_shape = jax.ShapeDtypeStruct((rows * BASE_PAD, EARLY), BF16)
    late_shape = jax.ShapeDtypeStruct((LATE_ROWS, LATE), BF16)
    high, low, late_high, late_low, base = pl.pallas_call(
        weight_kernel,
        out_shape=(
            early_shape,
            early_shape,
            late_shape,
            late_shape,
            jax.ShapeDtypeStruct((BASE_PAD, DEPTH + LANES), F32),
        ),
        in_specs=whole_vmem(2),
        out_specs=tuple(whole_vmem(5)),
        scratch_shapes=[pltpu.VMEM((2, BASE_PAD, LANES), F32)],
        compiler_params=params,
        name="weights",
    )(row_in, col_in)
    width = wide // 2
    reach = wide + 2 * LANES
    normal_shape = jax.ShapeDtypeStruct((FIT_ROWS, LANES), F32)
    part, kept, aux = pl.pallas_call(
        functools.partial(early_kernel, cores, stripes),
        out_shape=(
            normal_shape,
            jax.ShapeDtypeStruct((HALF * BASE_PAD, width), F32),
            jax.ShapeDtypeStruct((2 * rows + 8, width), F32),
        ),
        in_specs=whole_vmem(cores + 6),
        out_specs=tuple(whole_vmem(3)),
        scratch_shapes=[
            pltpu.VMEM((rows + 16, reach), F32),
            pltpu.VMEM((rows + 32, reach), BF16),
            pltpu.VMEM((rows + 32, reach), BF16),
            pltpu.VMEM((EARLY, width), BF16),
            pltpu.VMEM((EARLY, width), BF16),
            pltpu.VMEM(((rows - HALF) * BASE_PAD, width), F32),
        ],
        compiler_params=params,
        name="early",
    )(*pieces, near, science, good, odd, high, low)
    normal = pl.pallas_call(
        functools.partial(late_kernel, stripes, rows),
        out_shape=normal_shape,
        in_specs=whole_vmem(7),
        out_specs=pl.BlockSpec(memory_space=pltpu.VMEM),
        scratch_shapes=[
            pltpu.VMEM((16, reach), F32),
            pltpu.VMEM((32, reach), BF16),
            pltpu.VMEM((32, reach), BF16),
            pltpu.VMEM((LATE, width), BF16),
            pltpu.VMEM((LATE, width), BF16),
            pltpu.VMEM((HALF * BASE_PAD, width), F32),
        ],
        compiler_params=params,
        name="late",
    )(far, odd, late_high, late_low, part, kept, aux)
    region_rows = BASES * rows + 2 * BASE_PAD
    blocks = wide // (2 * LANES)
    cuts = [blocks * cut // 8 * 2 * LANES for cut in (0, 2, 5, 8)]
    weight_shape = jax.ShapeDtypeStruct((region_rows, DEPTH), BF16)
    source_shape = jax.ShapeDtypeStruct((GROUP + 16, reach), BF16)
    parts, shared = [], []

    def shift_scratch(size):
        return [pltpu.VMEM((DEPTH, size), BF16)] * 2

    def first_bases(after):
        size = cuts[1]
        *made, part = pl.pallas_call(
            functools.partial(first_bases_kernel, cores),
            out_shape=(
                weight_shape,
                weight_shape,
                source_shape,
                source_shape,
                jax.ShapeDtypeStruct((region_rows, size), F32),
            ),
            in_specs=whole_vmem(cores + 4),
            out_specs=tuple(whole_vmem(5)),
            scratch_shapes=[pltpu.VMEM((rows + 24, reach), F32)] + shift_scratch(size),
            compiler_params=params,
            name="bases",
        )(*pieces, far, near, base, after)
        shared.extend(made)
        parts.append(part)
        return part

    def next_bases(cut, after):
        size = cuts[cut + 1] - cuts[cut]
        high, low, highs, lows = shared
        part = pl.pallas_call(
            functools.partial(next_bases_kernel, cuts[cut]),
            out_shape=jax.ShapeDtypeStruct((region_rows, size), F32),
            in_specs=whole_vmem(5),
            out_specs=pl.BlockSpec(memory_space=pltpu.VMEM),
            scratch_shapes=shift_scratch(size),
            compiler_params=params,
            name="bases",
        )(highs, lows, high, low, after)
        parts.append(part)
        return part

    beside = [first_bases, functools.partial(next_bases, 1), functools.partial(next_bases, 2)]
    normal = summed(normal, "stripe", beside, params)
    filtered, coef = pl.pallas_call(
        functools.partial(model_kernel, stripes),
        out_shape=(
            jax.ShapeDtypeStruct(exposure.shape, F32),
            jax.ShapeDtypeStruct((1, 3 * BASES + BACK), F32),
        ),
        in_specs=whole_vmem(1 + len(parts) + 4),
        out_specs=tuple(whole_vmem(2)),
        compiler_params=params,
        name="model",
    )(normal, *parts, far, near, science, good)
    return filtered, coef


def solution(mesh):
    placed = (
        P(("groups", "stripe"), "exp"),
        P(("groups", "exp"), "stripe", None),
        P(("groups", "exp"), "stripe", None),
        P(("groups", "stripe"), None),
        P(),
        P(),
    )
    return jax.shard_map(
        shards,
        mesh=mesh,
        in_specs=placed,
        out_specs=(P(("groups", "exp"), "stripe", None), P(("groups", "exp"), None)),
        check_vma=False,
    )
```

```python
import functools

import jax
import jax.numpy as jnp
from jax import lax
from jax.experimental import pallas as pl
from jax.experimental.pallas import tpu as pltpu
from jax.sharding import PartitionSpec as P

HALF = 9
TAPS = 2 * HALF + 1
BASES = 19
STAMP_W = 64
LANES = 128
BASE_PAD = 24
BACK = 7
FIT_ROWS = 3 * BASE_PAD
BACK_FIRST = BASE_PAD - BASES
TARGET = BASE_PAD + BASES + BACK - BACK_FIRST
PACKED = 2 * BASE_PAD
REACH = HALF + 1
GROUP = 32
GROUPS_TILE = LANES // GROUP
MAIN_TILES = 5
MAIN = MAIN_TILES * LANES
DEPTH = MAIN + LANES
EXTRA_ROWS = 80
NEAR_AT = TAPS * 16
NEAR_EXTRA_AT = NEAR_AT + 160
EARLY = NEAR_EXTRA_AT + 48
FAR_EXTRA_AT = 160
LATE = 2 * LANES
LATE_ROWS = -(-HALF * BASE_PAD // 16) * 16
F32 = jnp.float32
BF16 = jnp.bfloat16


def lane_id(rows):
    return lax.broadcasted_iota(jnp.int32, (rows, LANES), 1)


def row_id(rows):
    return lax.broadcasted_iota(jnp.int32, (rows, LANES), 0)


def split_two(values):
    high = values.astype(BF16)
    low = (values - high.astype(F32)).astype(BF16)
    return high, low


def position(index, total):
    return (2.0 * index.astype(F32) + 1.0) / total - 1.0


def even_stripe():
    return lax.rem(lax.axis_index("stripe"), 2) == 0


def edge_kernel(cores, toward_near, *refs):
    pieces = refs[:cores]
    science_ref, good_ref = refs[cores : cores + 2]
    edge_ref, ext = refs[-2:]
    rows, half = pieces[0].shape
    wide = science_ref.shape[2]
    me = lax.axis_index("exp")
    for step in range(cores):
        start = lax.rem(me + step, cores) * half
        ext[:, pl.ds(pl.multiple_of(start, LANES), half)] = pieces[step][...]
    fold = wide // 2
    low_first = rows - 8

    def edge(first, extra, outer):
        parts = [ext[first : first + 8, :fold], ext[first : first + 8, fold:]]
        tail = []
        for line in (extra, extra + 1):
            tail += [ext[line : line + 1, :fold], ext[line : line + 1, fold:]]
        science = science_ref[0, outer : outer + 1, :]
        good = good_ref[0, outer : outer + 1, :]
        for line in (science, good):
            tail += [line[:, :fold], line[:, fold:]]
        return jnp.concatenate(parts + tail, axis=0)

    bottom = edge(low_first, rows - REACH, rows - 1)
    top = edge(0, 8, 0)
    edge_ref[...] = jnp.where(even_stripe() == toward_near, bottom, top)


def load_kernel(
    template_hbm,
    science_hbm,
    good_hbm,
    row_hbm,
    col_hbm,
    stamps_hbm,
    template_ref,
    science_ref,
    good_ref,
    row_ref,
    col_ref,
    odd_ref,
    mask_ref,
    stamps_ref,
    sems,
):
    moves = [
        pltpu.make_async_copy(source, target, sems.at[spot])
        for spot, (source, target) in enumerate(
            [
                (science_hbm, science_ref),
                (good_hbm, mask_ref),
                (template_hbm, template_ref),
                (row_hbm, row_ref),
                (col_hbm, col_ref),
                (stamps_hbm, stamps_ref),
            ]
        )
    ]
    for move in moves:
        move.start()
    for move in moves:
        move.wait()
    good_ref[...] = mask_ref[...].astype(F32)
    odd_ref[...] = jnp.concatenate(
        [
            jnp.full((1, LANES), lax.rem(stamps_ref[0, stamp], 2), jnp.int32)
            for stamp in range(odd_ref.shape[0])
        ],
        axis=0,
    )


def weight_kernel(
    row_ref, col_ref, high_ref, low_ref, late_high_ref, late_low_ref, base_ref, pad
):
    pad[...] = jnp.zeros_like(pad)
    pad[0, 0:BASES, 0:TAPS] = row_ref[...]
    pad[1, 0:BASES, 0:TAPS] = col_ref[...]
    row = pad[0]
    lane = lane_id(BASE_PAD)
    group = lane // GROUP
    tiled = row
    for part in range(1, GROUPS_TILE):
        tiled = tiled + pltpu.roll(row, part * GROUP, 1)
    columns = [
        jnp.broadcast_to(pad[1, :, tap : tap + 1], (BASE_PAD, LANES)) for tap in range(TAPS)
    ]
    zero = jnp.zeros((BASE_PAD, LANES), F32)
    mains = []
    for tile in range(MAIN_TILES):
        spread = zero
        for part in range(GROUPS_TILE):
            tap = tile * GROUPS_TILE + part
            if tap < TAPS:
                spread = jnp.where(group == part, columns[tap], spread)
        mains.append(tiled * spread)
    spread = zero
    for tap in range(TAPS):
        spread = jnp.where(lane // 4 == tap, columns[tap], spread)
    corner = lax.rem(lane, 4)

    def tap_at(tap):
        return jnp.broadcast_to(pad[0, :, tap : tap + 1], (BASE_PAD, LANES))

    outer = jnp.where(
        corner == 0,
        tap_at(0),
        jnp.where(corner == 1, tap_at(1), jnp.where(corner == 2, tap_at(TAPS - 2), tap_at(TAPS - 1))),
    )
    inner = jnp.where(corner == 1, tap_at(0), jnp.where(corner == 2, tap_at(TAPS - 1), 0.0))
    outer = outer * spread
    inner = inner * spread
    for tile in range(MAIN_TILES):
        base_ref[:, tile * LANES : (tile + 1) * LANES] = mains[tile]
    base_ref[:, MAIN : MAIN + LANES] = outer
    base_ref[:, MAIN + LANES :] = inner
    rows = high_ref.shape[0] // BASE_PAD
    even = even_stripe()
    first_tap, last_tap = tap_at(0), tap_at(TAPS - 1)

    def column_tile(tap_of):
        spread = zero
        begin = 0
        for end in range(1, LANES + 1):
            if end < LANES and tap_of(end) == tap_of(begin):
                continue
            if tap_of(begin) < TAPS:
                spread = jnp.where((lane >= begin) & (lane < end), columns[tap_of(begin)], spread)
            begin = end
        return spread

    def early_tap(place):
        if place < NEAR_AT:
            return place // 16
        return (place - NEAR_AT) // 8 if place < NEAR_EXTRA_AT else (place - NEAR_EXTRA_AT) // 2

    def late_tap(place):
        return place // 8 if place < FAR_EXTRA_AT else (place - FAR_EXTRA_AT) // 2

    early_tiles = [
        column_tile(lambda spot, tile=tile: early_tap(tile * LANES + spot))
        for tile in range(EARLY // LANES)
    ]
    late_tiles = [
        column_tile(lambda spot, tile=tile: late_tap(tile * LANES + spot))
        for tile in range(LATE // LANES)
    ]

    def repeats(period):
        blocks = []
        for start in range(0, TAPS, period):
            block = pltpu.roll(row, (LANES - start) % LANES, 1) if start else row
            block = jnp.where(lane < period, block, 0.0)
            size = period
            while size < LANES:
                block = block + pltpu.roll(block, size, 1)
                size *= 2
            blocks.append(block)
        return blocks

    def window(blocks, period, first):
        block, move = first // period, first % period
        here = blocks[block] if 0 <= block < len(blocks) else None
        beyond = blocks[block + 1] if 0 <= block + 1 < len(blocks) else None
        if move == 0:
            return zero if here is None else here
        ready = lax.rem(lane, period) < period - move
        parts = [zero if part is None else pltpu.roll(part, LANES - move, 1) for part in (here, beyond)]
        return jnp.where(ready, parts[0], parts[1])

    by_sixteen, by_eight = repeats(16), repeats(8)
    own_rows = [window(by_sixteen, 16, HALF - line) for line in range(rows)]
    top_rows = [window(by_eight, 8, 1 - line) for line in range(rows)]
    bottom_rows = [window(by_eight, 8, rows + HALF - line) for line in range(rows)]

    parity = lax.rem(lane, 2)

    def corner_taps(upper, lower, is_upper):
        top = jnp.where(parity == 1, first_tap, 0.0) if upper else zero
        bottom = jnp.where(parity == 0, last_tap, 0.0) if lower else zero
        return jnp.where(is_upper, top, bottom)

    near_is_top = ~even
    early_rows, late_rows = [], []
    for spot in range(rows):
        odd_line = spot + rows - HALF if spot < HALF else spot - HALF
        own = jnp.where(even, own_rows[spot], own_rows[odd_line])
        side = jnp.where(even, bottom_rows[spot], top_rows[odd_line])
        extra = zero
        if spot >= HALF:
            extra = corner_taps(spot == HALF, spot == rows - 1, near_is_top)
        tiles = [
            own,
            own,
            jnp.where(lane < NEAR_AT - 2 * LANES, own, side),
            jnp.where(lane < NEAR_EXTRA_AT - 3 * LANES, side, extra),
        ]
        early_rows.append(
            jnp.concatenate([mine * tile for mine, tile in zip(tiles, early_tiles)], axis=1)
        )
        if spot < HALF:
            side = jnp.where(even, top_rows[spot], bottom_rows[odd_line])
            extra = corner_taps(spot == 0, spot == HALF - 1, even)
            tiles = [side, jnp.where(lane < FAR_EXTRA_AT - LANES, side, extra)]
            late_rows.append(
                jnp.concatenate([mine * tile for mine, tile in zip(tiles, late_tiles)], axis=1)
            )
    for spot in range(0, rows, 2):
        where = pl.ds(spot * BASE_PAD, 2 * BASE_PAD)
        high_ref[where, :], low_ref[where, :] = split_two(
            jnp.concatenate(early_rows[spot : spot + 2], axis=0)
        )
    spare = late_high_ref.shape[0] - HALF * BASE_PAD
    late_rows.append(jnp.zeros((spare, LATE), F32))
    late_high_ref[...], late_low_ref[...] = split_two(jnp.concatenate(late_rows, axis=0))


def edges_of(near_ref, far_ref):
    even = even_stripe()
    near = near_ref[...]
    far = far_ref[...]
    return jnp.where(even, far, near), jnp.where(even, near, far)


def fill_extended(ext, highs, lows, cores, pieces, near_ref, far_ref):
    rows, half = pieces[0].shape
    wide = half * cores
    fold = wide // 2
    ext[:, 0:LANES] = jnp.zeros((ext.shape[0], LANES), F32)
    ext[:, LANES + wide :] = jnp.zeros((ext.shape[0], LANES), F32)
    me = lax.axis_index("exp")
    for step in range(cores):
        start = lax.rem(me + step, cores) * half + LANES
        ext[8 : 8 + rows, pl.ds(pl.multiple_of(start, LANES), half)] = pieces[step][...]
    top, bottom = edges_of(near_ref, far_ref)
    for side in range(2):
        where = pl.ds(LANES + side * fold, fold)
        ext[0:8, where] = top[8 * side : 8 * side + 8]
        ext[8 + rows : 16 + rows, where] = bottom[8 * side : 8 * side + 8]
        spare = [
            top[16 + side : 17 + side],
            top[18 + side : 19 + side],
            bottom[16 + side : 17 + side],
            bottom[18 + side : 19 + side],
        ]
        ext[16 + rows : 24 + rows, where] = jnp.concatenate(spare + spare, axis=0)
    main = slice(0, GROUP)
    highs[main], lows[main] = split_two(ext[main])
    extra = ext[GROUP : GROUP + 8]
    span = extra.shape[1]
    early = lax.broadcasted_iota(jnp.int32, extra.shape, 0) < 4
    ahead = [extra] + [pltpu.roll(extra, span - part, 1) for part in range(1, 4)]
    lines = jnp.concatenate(
        [jnp.where(early, ahead[0], ahead[1]), jnp.where(early, ahead[2], ahead[3])], axis=0
    )
    highs[GROUP:], lows[GROUP:] = split_two(lines)


def spread_window(shifted, put):
    for tap in range(TAPS):
        put(tap * GROUP, shifted(tap, slice(0, GROUP)))
    for quad in range(MAIN_TILES):
        put(MAIN + 16 * quad, shifted(4 * quad, slice(GROUP, GROUP + 16)))


def clear_spare(refs):
    for ref in refs:
        wide = ref.shape[1]
        ref[TAPS * GROUP : MAIN] = jnp.zeros((MAIN - TAPS * GROUP, wide), BF16)
        ref[MAIN + EXTRA_ROWS :] = jnp.zeros((LANES - EXTRA_ROWS, wide), BF16)


def back_profile(horiz):
    steady = jnp.ones_like(horiz)
    square = 0.5 * (3.0 * horiz * horiz - 1.0)
    return [steady, horiz, steady, horiz, square, steady, horiz]


def put_halves(target, edge_ref, rows, first):
    fold = edge_ref.shape[1]
    for side in range(2):
        where = pl.ds(LANES + side * fold, fold)
        target[first : first + 8, where] = edge_ref[8 * side : 8 * side + 8]
        for line in range(2):
            spot = 16 + 2 * line + side
            target[rows + line : rows + line + 1, where] = edge_ref[spot : spot + 1]


def paired(values):
    span = values.shape[1]
    return jnp.concatenate([values, pltpu.roll(values, span - 1, 1)], axis=0)


def corner_block(lines):
    span = lines.shape[1]
    parts = [lines] + [pltpu.roll(lines, span - move, 1) for move in range(1, 8)]
    return jnp.concatenate(parts, axis=0)


def odd_rows(odd_ref, stamp, height):
    return jnp.broadcast_to(odd_ref[stamp : stamp + 1, :] == 1, (height, LANES))


def stamp_window(source, odd_ref, stamp, offset):
    height = source.shape[0]
    lane = lane_id(height)
    left = source[:, stamp * LANES : (stamp + 1) * LANES]
    centre = source[:, (stamp + 1) * LANES : (stamp + 2) * LANES]
    right = source[:, (stamp + 2) * LANES : (stamp + 3) * LANES]
    odd = jnp.where(lane < LANES // 4, right, centre)
    even = jnp.where(lane >= LANES - HALF, left, centre)
    odd = pltpu.roll(odd, (HALF + STAMP_W + offset) % LANES, 1)
    even = pltpu.roll(even, HALF + offset, 1)
    return jnp.where(odd_rows(odd_ref, stamp, height), odd, even)


def stamp_shifts(sources, targets, odd_ref, pair, moves):
    columns = slice(pair * LANES, (pair + 1) * LANES)
    for source, target in zip(sources, targets):
        first = stamp_window(source, odd_ref, 2 * pair, 0)
        second = stamp_window(source, odd_ref, 2 * pair + 1, STAMP_W)
        for spot, (tile, move) in enumerate(moves):
            a, b = first[16 * tile : 16 * tile + 16], second[16 * tile : 16 * tile + 16]
            if move:
                a = pltpu.roll(a, LANES - move, 1)
                b = pltpu.roll(b, LANES - move, 1)
            target[16 * spot : 16 * spot + 16, columns] = jnp.where(
                lane_id(16) < STAMP_W, a, b
            )


def stamp_values(sources, odd_ref, pair, moves):
    out = []
    for source in sources:
        first = stamp_window(source, odd_ref, 2 * pair, 0)
        second = stamp_window(source, odd_ref, 2 * pair + 1, STAMP_W)
        tiles = []
        for tile, move in moves:
            a, b = first[16 * tile : 16 * tile + 16], second[16 * tile : 16 * tile + 16]
            if move:
                a = pltpu.roll(a, LANES - move, 1)
                b = pltpu.roll(b, LANES - move, 1)
            tiles.append(jnp.where(lane_id(16) < STAMP_W, a, b))
        out.append(jnp.concatenate(tiles, axis=0))
    return out


def three_products(high, low, xhigh, xlow):
    return (
        jnp.dot(high, xhigh, preferred_element_type=F32)
        + jnp.dot(low, xhigh, preferred_element_type=F32)
        + jnp.dot(high, xlow, preferred_element_type=F32)
    )


def back_rows(rows):
    empty = jnp.zeros_like(rows[0])
    lead = [empty] * (8 - BACK_FIRST)
    second = lead + rows[BACK_FIRST:]
    second += [empty] * (8 - len(second))
    return [jnp.concatenate(part, axis=0) for part in (lead + rows[:BACK_FIRST], second)]


def design_line(bases, keep, target, horiz, profiles, row, region_rows):
    own = bases * keep
    vert = position(jnp.full(horiz.shape, row, jnp.int32), region_rows)
    square = 0.5 * (3.0 * vert * vert - 1.0)
    steady = jnp.ones_like(vert)
    scales = back_rows([steady, steady, vert, vert, steady, square, square])
    first, second = (profile * scale * keep for profile, scale in zip(profiles, scales))
    spot = lax.broadcasted_iota(jnp.int32, second.shape, 0)
    second = jnp.where(spot == TARGET % 8, target, second)
    sloped = own * horiz
    return jnp.concatenate(
        [own[:16], own[16:] + first, sloped[:16], sloped[16:] + second, own * vert], axis=0
    )


def gram(lines):
    design = jnp.concatenate([line.astype(BF16) for line in lines], axis=1)
    return lax.dot_general(design, design, (((1,), (1,)), ((), ())), preferred_element_type=F32)


def early_kernel(cores, stripes, *refs):
    pieces = refs[:cores]
    (
        near_ref,
        science_ref,
        good_ref,
        odd_ref,
        high_ref,
        low_ref,
        total_ref,
        late_ref,
        aux_ref,
        ext,
        highs,
        lows,
        xhigh,
        xlow,
        bases,
    ) = refs[cores:]
    rows, half = pieces[0].shape
    wide = science_ref.shape[2]
    pairs = wide // (4 * STAMP_W)
    me = lax.axis_index("exp")
    ext[:, 0:LANES] = jnp.zeros((ext.shape[0], LANES), F32)
    ext[:, LANES + wide :] = jnp.zeros((ext.shape[0], LANES), F32)
    for step in range(cores):
        start = lax.rem(me + step, cores) * half + LANES
        ext[0:rows, pl.ds(pl.multiple_of(start, LANES), half)] = pieces[step][...]
    put_halves(ext, near_ref, rows + 8, rows)
    lines = jnp.concatenate(
        [ext[0:rows], paired(ext[rows : rows + 8]), corner_block(ext[rows + 8 : rows + 10])], axis=0
    )
    highs[...], lows[...] = split_two(lines)
    moves = [(0, tap) for tap in range(TAPS)]
    moves += [(1, 2 * step) for step in range(10)]
    moves += [(2, 8 * step) for step in range(3)]
    lane = lane_id(1)
    for pair in range(pairs):
        columns = slice(pair * LANES, (pair + 1) * LANES)
        stamp_shifts((highs, lows), (xhigh, xlow), odd_ref, pair, moves)
        odd = jnp.where(
            lane < STAMP_W,
            odd_ref[2 * pair : 2 * pair + 1],
            odd_ref[2 * pair + 1 : 2 * pair + 2] + 1,
        )
        horiz = position(4 * pair * STAMP_W + odd * STAMP_W + lane, wide)
        aux_ref[2 * rows : 2 * rows + 8, columns] = jnp.broadcast_to(horiz, (8, LANES))
        picked = []
        for source in (good_ref, science_ref):
            lower = source[0, :, 2 * pair * LANES : (2 * pair + 1) * LANES]
            upper = source[0, :, (2 * pair + 1) * LANES : (2 * pair + 2) * LANES]
            lower = jnp.where(
                odd_rows(odd_ref, 2 * pair, rows), pltpu.roll(lower, STAMP_W, 1), lower
            )
            upper = jnp.where(
                odd_rows(odd_ref, 2 * pair + 1, rows), upper, pltpu.roll(upper, STAMP_W, 1)
            )
            picked.append(jnp.where(lane_id(rows) < STAMP_W, lower, upper))
        aux_ref[0:rows, columns] = picked[0]
        aux_ref[rows : 2 * rows, columns] = picked[0] * picked[1]
    split = HALF * BASE_PAD
    chunk = 2 * LANES
    for start in range(0, wide // 2, chunk):
        span = slice(start, start + chunk)
        values = three_products(high_ref[...], low_ref[...], xhigh[:, span], xlow[:, span])
        late_ref[:, span] = values[:split]
        bases[:, span] = values[split:]
    horiz = aux_ref[2 * rows : 2 * rows + 1]
    profile = back_rows(back_profile(horiz))
    first_line = jnp.where(even_stripe(), HALF, 0)
    first_row = lax.axis_index("stripe") * rows
    designs = []
    for spot in range(rows - HALF):
        line = first_line + spot
        designs.append(design_line(
            bases[spot * BASE_PAD : (spot + 1) * BASE_PAD],
            aux_ref[pl.ds(line, 1), :],
            aux_ref[pl.ds(rows + line, 1), :],
            horiz,
            profile,
            first_row + line,
            rows * stripes,
        ))
    total = gram(designs)
    total_ref[...] = jnp.concatenate(
        [total, jnp.zeros((FIT_ROWS, LANES - FIT_ROWS), F32)], axis=1
    )


def late_kernel(stripes, rows, *refs):
    (
        far_ref,
        odd_ref,
        high_ref,
        low_ref,
        total_ref,
        early_ref,
        aux_ref,
        out_ref,
        ext,
        highs,
        lows,
        bases,
    ) = refs
    width = early_ref.shape[1]
    pairs = width // LANES
    ext[:, 0:LANES] = jnp.zeros((ext.shape[0], LANES), F32)
    ext[:, ext.shape[1] - LANES :] = jnp.zeros((ext.shape[0], LANES), F32)
    put_halves(ext, far_ref, 8, 0)
    lines = jnp.concatenate([paired(ext[0:8]), corner_block(ext[8:10])], axis=0)
    highs[...], lows[...] = split_two(lines)
    moves = [(0, 2 * step) for step in range(10)] + [(1, 8 * step) for step in range(3)]
    used = 16 * len(moves)
    split = HALF * BASE_PAD
    chunk = 4 * LANES
    for start in range(0, width, chunk):
        span = slice(start, start + chunk)
        made = [
            stamp_values((highs, lows), odd_ref, pair, moves)
            for pair in range(start // LANES, (start + chunk) // LANES)
        ]
        spare = jnp.zeros((LATE - used, chunk), BF16)
        xh, xl = (
            jnp.concatenate([jnp.concatenate([one[side] for one in made], axis=1), spare], axis=0)
            for side in range(2)
        )
        values = three_products(high_ref[...], low_ref[...], xh, xl)
        bases[:, span] = early_ref[:, span] + values[:split]
    horiz = aux_ref[2 * rows : 2 * rows + 1]
    profile = back_rows(back_profile(horiz))
    first_line = jnp.where(even_stripe(), 0, rows - HALF)
    first_row = lax.axis_index("stripe") * rows
    designs = []
    for spot in range(HALF):
        line = first_line + spot
        designs.append(
            design_line(
                bases[spot * BASE_PAD : (spot + 1) * BASE_PAD],
                aux_ref[pl.ds(line, 1), :],
                aux_ref[pl.ds(rows + line, 1), :],
                horiz,
                profile,
                first_row + line,
                rows * stripes,
            )
        )
    own = total_ref[:, :FIT_ROWS] + gram(designs)
    out_ref[...] = packed_normal(own)


def packed_normal(normal):
    room = LANES - FIT_ROWS
    last = normal[PACKED:]
    spare = jnp.zeros((BASE_PAD, 2 * room - FIT_ROWS), F32)
    return jnp.concatenate(
        [
            jnp.concatenate([normal[:BASE_PAD], last[:, :room]], axis=1),
            jnp.concatenate([normal[BASE_PAD:PACKED], last[:, room:], spare], axis=1),
        ],
        axis=0,
    )


def unpacked_normal(packed):
    room = LANES - FIT_ROWS
    lane = lane_id(BASE_PAD)
    last = jnp.where(
        lane < room,
        pltpu.roll(packed[:BASE_PAD], room, 1),
        pltpu.roll(packed[BASE_PAD:], 2 * room, 1),
    )
    values = jnp.concatenate([packed, last], axis=0)
    return jnp.where(lane_id(FIT_ROWS) < FIT_ROWS, values, 0.0)


def panels():
    out = []
    for term, used in enumerate((BASE_PAD, BASES + BACK - BACK_FIRST, BASES)):
        for start in range(0, used, 8):
            out.append((term * BASE_PAD + start, min(8, used - start)))
    return out


def tree_sum(values):
    while len(values) > 1:
        values = [sum(values[spot : spot + 2][1:], values[spot]) for spot in range(0, len(values), 2)]
    return values[0]


def solve_rows(matrix):
    sub = row_id(8)
    tiles = [matrix[start : start + 8] for start in range(0, FIT_ROWS, 8)]
    order = panels()

    def spread(tile, spot):
        return jnp.broadcast_to(tile[spot : spot + 1], (8, LANES))

    def column(tile, spot):
        return jnp.broadcast_to(tile[:, spot : spot + 1], (8, LANES))

    start, size = order[0]
    corner = [column(tiles[start // 8], start + j) for j in range(size)]
    for step, (start, size) in enumerate(order):
        home = start // 8
        columns = [
            [None if place == home else column(tile, start + j) for place, tile in enumerate(tiles)]
            for j in range(size)
        ]
        rows = tiles[home]
        following = order[step + 1] if step + 1 < len(order) else (0, 0)
        next_home = following[0] // 8
        ahead = [column(rows, following[0] + j) for j in range(following[1])]
        below = [column(tiles[next_home], following[0] + j) for j in range(following[1])]
        for spot in range(size):
            keep = sub == spot
            inverse = 1.0 / spread(corner[spot], spot)
            others = jnp.where(keep, 0.0, corner[spot])

            def eliminated(values):
                scaled = spread(values, spot) * inverse
                return jnp.where(keep, scaled, values - others * scaled)

            corner = [
                eliminated(values) if j > spot else values for j, values in enumerate(corner)
            ]
            ahead = [eliminated(values) for values in ahead]
            rows = eliminated(rows)
        if following[1]:
            corner = [
                values - tree_sum([columns[i][next_home] * spread(ahead[j], i) for i in range(size)])
                for j, values in enumerate(below)
            ]
        for place in range(len(tiles)):
            if place == home:
                tiles[place] = rows
            else:
                tiles[place] = tiles[place] - tree_sum(
                    [columns[i][place] * spread(rows, i) for i in range(size)]
                )
    line = row_id(FIT_ROWS)
    used = (line < TARGET) | ((line >= PACKED) & (line < PACKED + BASES))
    right = jnp.concatenate(tiles, axis=0)[:, TARGET : TARGET + 1]
    return jnp.where(used, jnp.broadcast_to(right, (FIT_ROWS, LANES)), 0.0)


def region_weights(base_ref, high_ref, low_ref, rows):
    lane = lane_id(8)
    spot = lax.rem(lane, GROUP)
    corner = lax.rem(lane, 4)
    line = row_id(8)
    mains = [base_ref[:, tile * LANES : (tile + 1) * LANES] for tile in range(MAIN_TILES)]
    outer = base_ref[:, MAIN : MAIN + LANES]
    inner = base_ref[:, MAIN + LANES :]
    blocks = [[] for _ in range(BASES)]
    for start in range(0, rows, 8):
        tap = spot - (start + line - 1)
        inside = (tap >= 0) & (tap < TAPS)
        moved = [pltpu.roll(main, (start - 1) % LANES, 1) for main in mains]
        extra = zero_row = jnp.zeros((8, LANES), F32)
        for b in range(BASES):
            tiles = []
            for main in moved:
                wide = jnp.broadcast_to(main[b : b + 1], (8, LANES))
                tiles.append(
                    jnp.where(inside, pltpu.roll(wide, 0, 1, stride=1, stride_axis=0), 0.0)
                )
            extra = zero_row
            mine = jnp.broadcast_to(inner[b : b + 1], (8, LANES))
            if start == 0:
                extra = jnp.where((line == 0) & (corner < 2), mine, extra)
            if start == rows - 8:
                extra = jnp.where((line == 7) & (corner >= 2), mine, extra)
            blocks[b].append(jnp.concatenate(tiles + [extra], axis=1))
    for b in range(BASES):
        where = pl.ds(b * rows, rows)
        high_ref[where, :], low_ref[where, :] = split_two(jnp.concatenate(blocks[b], axis=0))
    lane = lane_id(BASE_PAD)
    spot = lax.rem(lane, GROUP)
    corner = lax.rem(lane, 4)
    halos = []
    for shift, extra in ((rows - 1, corner >= 2), (-2, corner < 2)):
        tap = spot - shift
        inside = (tap >= 0) & (tap < TAPS)
        tiles = [jnp.where(inside, pltpu.roll(main, shift % LANES, 1), 0.0) for main in mains]
        halos.append(jnp.concatenate(tiles + [jnp.where(extra, outer, 0.0)], axis=1))
    where = pl.ds(BASES * rows, 2 * BASE_PAD)
    high_ref[where, :], low_ref[where, :] = split_two(jnp.concatenate(halos, axis=0))


def region_bases(highs, lows, high_ref, low_ref, first, out_ref, xhigh, xlow):
    clear_spare((xhigh, xlow))
    wide = out_ref.shape[1]
    chunk = 2 * LANES
    for start in range(0, wide, chunk):
        span = slice(start, start + chunk)
        for source, target in ((highs, xhigh), (lows, xlow)):

            def shifted(tap, lines):
                begin = first + start + LANES - HALF + tap
                return source[lines, begin : begin + chunk]

            def put(place, values):
                target[place : place + values.shape[0], span] = values

            spread_window(shifted, put)
        out_ref[:, span] = three_products(
            high_ref[...], low_ref[...], xhigh[:, span], xlow[:, span]
        )


def first_bases_kernel(cores, *refs):
    pieces = refs[:cores]
    (
        far_ref,
        near_ref,
        base_ref,
        after_ref,
        high_ref,
        low_ref,
        highs,
        lows,
        out_ref,
        ext,
        xhigh,
        xlow,
    ) = refs[cores:]
    region_weights(base_ref, high_ref, low_ref, pieces[0].shape[0])
    fill_extended(ext, highs, lows, cores, pieces, near_ref, far_ref)
    region_bases(highs, lows, high_ref, low_ref, 0, out_ref, xhigh, xlow)


def next_bases_kernel(first, highs, lows, high_ref, low_ref, after_ref, out_ref, xhigh, xlow):
    region_bases(highs, lows, high_ref, low_ref, first, out_ref, xhigh, xlow)


def add_kernel(mine_ref, other_ref, after_ref, out_ref):
    out_ref[...] = mine_ref[...] + other_ref[...]


def model_kernel(stripes, normal_ref, *refs):
    far_ref, near_ref, science_ref, good_ref, out_ref, coef_ref = refs[-6:]
    parts = refs[:-6]
    rows = science_ref.shape[1]
    wide = science_ref.shape[2]
    top, bottom = edges_of(near_ref, far_ref)
    coef = solve_rows(unpacked_normal(normal_ref[...]))
    lane = lane_id(FIT_ROWS)
    home = lane - 3 * BASES + jnp.where(lane < 3 * BASES + BACK_FIRST, BASES, BASE_PAD + BASES - BACK_FIRST)
    home = jnp.where(lane < 3 * BASES, lax.rem(lane, 3) * BASE_PAD + lane // 3, home)
    flat = jnp.sum(jnp.where(row_id(FIT_ROWS) == home, coef, 0.0), axis=0, keepdims=True)
    coef_ref[...] = flat[:, : coef_ref.shape[1]]

    def share(spot, height):
        return jnp.broadcast_to(coef[spot : spot + 1], (height, LANES))

    first_row = lax.axis_index("stripe") * rows
    vert = position(first_row + row_id(rows), rows * stripes)
    halo_vert = [
        position(jnp.full((8, LANES), first_row + line, jnp.int32), rows * stripes)
        for line in (rows, -1)
    ]
    slopes = [share(2 * BASE_PAD + b, rows) * vert for b in range(BASES)]
    halo_slopes = [
        coef[2 * BASE_PAD : 3 * BASE_PAD] * jnp.concatenate([line] * 3, axis=0) for line in halo_vert
    ]
    level = [
        share(BASES + m + (0 if m < BACK_FIRST else BASE_PAD - BACK_FIRST), 8) for m in range(BACK)
    ]

    def ground(here, horiz):
        square = 0.5 * (3.0 * here * here - 1.0)
        horiz_square = 0.5 * (3.0 * horiz * horiz - 1.0)
        steady = level[0] + level[1] * horiz + level[4] * horiz_square
        sloped = level[2] + level[3] * horiz
        curved = level[5] + level[6] * horiz
        if here.shape[0] > 8:
            steady, sloped, curved = (
                jnp.concatenate([part] * (here.shape[0] // 8), axis=0)
                for part in (steady, sloped, curved)
            )
        return steady + here * sloped + square * curved

    models, halos = [], [[], []]
    for part in parts:
        for start in range(0, part.shape[1], LANES):
            span = slice(start, start + LANES)
            begin = len(models) * LANES
            horiz = position(begin + lane_id(8), wide)
            total = ground(vert, horiz)
            for b in range(BASES):
                steady = share(b, 8) + share(BASE_PAD + b, 8) * horiz
                scale = jnp.concatenate([steady] * (rows // 8), axis=0) + slopes[b]
                total = total + part[b * rows : (b + 1) * rows, span] * scale
            models.append(total)
            steady = coef[:BASE_PAD] + coef[BASE_PAD : 2 * BASE_PAD] * horiz[0:1]
            for side in range(2):
                place = BASES * rows + side * BASE_PAD
                values = part[place : place + BASE_PAD, span] * (steady + halo_slopes[side])
                values = jnp.sum(values, axis=0, keepdims=True)
                halos[side].append(values + ground(halo_vert[side], horiz)[0:1])
    model = jnp.concatenate(models, axis=1)
    below_model, above_model = (jnp.concatenate(side, axis=1) for side in halos)
    own = good_ref[0] * (science_ref[0] - model)

    def halo(edge, values):
        science = jnp.concatenate([edge[20:21], edge[21:22]], axis=1)
        good = jnp.concatenate([edge[22:23], edge[23:24]], axis=1)
        return good * (science - values)

    above_row = halo(top, above_model)
    below_row = halo(bottom, below_model)
    lines = lax.broadcasted_iota(jnp.int32, (rows, wide), 0)
    spots = lax.broadcasted_iota(jnp.int32, (rows, wide), 1)
    above = jnp.where(lines == 0, above_row, pltpu.roll(own, 1, 0))
    below = jnp.where(lines == rows - 1, below_row, pltpu.roll(own, rows - 1, 0))
    before = jnp.where(spots == 0, 0.0, pltpu.roll(own, 1, 1))
    after = jnp.where(spots == wide - 1, 0.0, pltpu.roll(own, wide - 1, 1))
    out_ref[0] = 4.0 * own - (below + above + after + before)


def whole_vmem(count):
    return [pl.BlockSpec(memory_space=pltpu.VMEM)] * count


def add(values, other, after, params):
    return pl.pallas_call(
        add_kernel,
        out_shape=jax.ShapeDtypeStruct(values.shape, values.dtype),
        in_specs=whole_vmem(3),
        out_specs=pl.BlockSpec(memory_space=pltpu.VMEM),
        compiler_params=params,
        name="add",
    )(values, other, after)


def summed(values, axis, beside, params):
    count = lax.axis_size(axis)
    if count & (count - 1):
        for work in beside:
            work(values)
        return lax.psum(values, axis)
    step = 1
    waiting = list(beside)
    while step < count:
        other = lax.ppermute(values, axis, [(i, i ^ step) for i in range(count)])
        if waiting:
            values = add(values, other, waiting.pop(0)(values), params)
        else:
            values = values + other
        step *= 2
    for work in waiting:
        work(values)
    return values


def shards(template, exposure, cosmic_mask, stamp_blocks, row_filters, col_filters):
    arguments = (template, exposure, cosmic_mask, row_filters, col_filters, stamp_blocks)
    rows, half = template.shape
    wide = exposure.shape[2]
    cores = lax.axis_size("exp")
    stripes = lax.axis_size("stripe")
    params = pltpu.CompilerParams(vmem_limit_bytes=24 * 1024 * 1024)
    pieces = [template] + [
        lax.ppermute(template, "exp", [((i + step) % cores, i) for i in range(cores)])
        for step in range(1, cores)
    ]
    stamps = stamp_blocks.shape[1]
    template_in, science, good, row_in, col_in, odd = pl.pallas_call(
        load_kernel,
        out_shape=(
            jax.ShapeDtypeStruct(template.shape, F32),
            jax.ShapeDtypeStruct(exposure.shape, F32),
            jax.ShapeDtypeStruct(exposure.shape, F32),
            jax.ShapeDtypeStruct(row_filters.shape, F32),
            jax.ShapeDtypeStruct(col_filters.shape, F32),
            jax.ShapeDtypeStruct((stamps, LANES), jnp.int32),
        ),
        in_specs=[pl.BlockSpec(memory_space=pltpu.HBM)] * 6,
        out_specs=tuple(whole_vmem(6)),
        scratch_shapes=[
            pltpu.VMEM(cosmic_mask.shape, jnp.int32),
            pltpu.SMEM(stamp_blocks.shape, jnp.int32),
            pltpu.SemaphoreType.DMA((6,)),
        ],
        compiler_params=params,
        name="load",
    )(*[pltpu.with_memory_space_constraint(array, pltpu.HBM) for array in arguments])
    pieces = [template_in] + pieces[1:]
    edge_shape = jax.ShapeDtypeStruct((24, wide // 2), F32)

    def edge(toward_near, *others):
        return pl.pallas_call(
            functools.partial(edge_kernel, cores, toward_near),
            out_shape=edge_shape,
            in_specs=whole_vmem(cores + 2 + len(others)),
            out_specs=pl.BlockSpec(memory_space=pltpu.VMEM),
            scratch_shapes=[pltpu.VMEM((rows, wide), F32)],
            compiler_params=params,
            name="edges",
        )(*pieces, science, good, *others)

    far = edge(False)
    near = edge(True)
    near_pairs = [(i, i + 1) for i in range(0, stripes - 1, 2)]
    far_pairs = [(i, i + 1) for i in range(1, stripes - 1, 2)]

    def swapped(values, couples):
        return lax.ppermute(values, "stripe", couples + [(b, a) for a, b in couples])

    far = swapped(far, far_pairs)
    near = swapped(near, near_pairs)
    early_shape = jax.ShapeDtypeStruct((rows * BASE_PAD, EARLY), BF16)
    late_shape = jax.ShapeDtypeStruct((LATE_ROWS, LATE), BF16)
    high, low, late_high, late_low, base = pl.pallas_call(
        weight_kernel,
        out_shape=(
            early_shape,
            early_shape,
            late_shape,
            late_shape,
            jax.ShapeDtypeStruct((BASE_PAD, DEPTH + LANES), F32),
        ),
        in_specs=whole_vmem(2),
        out_specs=tuple(whole_vmem(5)),
        scratch_shapes=[pltpu.VMEM((2, BASE_PAD, LANES), F32)],
        compiler_params=params,
        name="weights",
    )(row_in, col_in)
    width = wide // 2
    reach = wide + 2 * LANES
    normal_shape = jax.ShapeDtypeStruct((FIT_ROWS, LANES), F32)
    part, kept, aux = pl.pallas_call(
        functools.partial(early_kernel, cores, stripes),
        out_shape=(
            normal_shape,
            jax.ShapeDtypeStruct((HALF * BASE_PAD, width), F32),
            jax.ShapeDtypeStruct((2 * rows + 8, width), F32),
        ),
        in_specs=whole_vmem(cores + 6),
        out_specs=tuple(whole_vmem(3)),
        scratch_shapes=[
            pltpu.VMEM((rows + 16, reach), F32),
            pltpu.VMEM((rows + 32, reach), BF16),
            pltpu.VMEM((rows + 32, reach), BF16),
            pltpu.VMEM((EARLY, width), BF16),
            pltpu.VMEM((EARLY, width), BF16),
            pltpu.VMEM(((rows - HALF) * BASE_PAD, width), F32),
        ],
        compiler_params=params,
        name="early",
    )(*pieces, near, science, good, odd, high, low)
    normal = pl.pallas_call(
        functools.partial(late_kernel, stripes, rows),
        out_shape=jax.ShapeDtypeStruct((PACKED, LANES), F32),
        in_specs=whole_vmem(7),
        out_specs=pl.BlockSpec(memory_space=pltpu.VMEM),
        scratch_shapes=[
            pltpu.VMEM((16, reach), F32),
            pltpu.VMEM((32, reach), BF16),
            pltpu.VMEM((32, reach), BF16),
            pltpu.VMEM((HALF * BASE_PAD, width), F32),
        ],
        compiler_params=params,
        name="late",
    )(far, odd, late_high, late_low, part, kept, aux)
    region_rows = BASES * rows + 2 * BASE_PAD
    blocks = wide // (2 * LANES)
    cuts = [blocks * cut // 8 * 2 * LANES for cut in (0, 2, 5, 8)]
    weight_shape = jax.ShapeDtypeStruct((region_rows, DEPTH), BF16)
    source_shape = jax.ShapeDtypeStruct((GROUP + 16, reach), BF16)
    parts, shared = [], []

    def shift_scratch(size):
        return [pltpu.VMEM((DEPTH, size), BF16)] * 2

    def first_bases(after):
        size = cuts[1]
        *made, part = pl.pallas_call(
            functools.partial(first_bases_kernel, cores),
            out_shape=(
                weight_shape,
                weight_shape,
                source_shape,
                source_shape,
                jax.ShapeDtypeStruct((region_rows, size), F32),
            ),
            in_specs=whole_vmem(cores + 4),
            out_specs=tuple(whole_vmem(5)),
            scratch_shapes=[pltpu.VMEM((rows + 24, reach), F32)] + shift_scratch(size),
            compiler_params=params,
            name="bases",
        )(*pieces, far, near, base, after)
        shared.extend(made)
        parts.append(part)
        return part

    def next_bases(cut, after):
        size = cuts[cut + 1] - cuts[cut]
        high, low, highs, lows = shared
        part = pl.pallas_call(
            functools.partial(next_bases_kernel, cuts[cut]),
            out_shape=jax.ShapeDtypeStruct((region_rows, size), F32),
            in_specs=whole_vmem(5),
            out_specs=pl.BlockSpec(memory_space=pltpu.VMEM),
            scratch_shapes=shift_scratch(size),
            compiler_params=params,
            name="bases",
        )(highs, lows, high, low, after)
        parts.append(part)
        return part

    beside = [first_bases, functools.partial(next_bases, 1), functools.partial(next_bases, 2)]
    normal = summed(normal, "stripe", beside, params)
    filtered, coef = pl.pallas_call(
        functools.partial(model_kernel, stripes),
        out_shape=(
            jax.ShapeDtypeStruct(exposure.shape, F32),
            jax.ShapeDtypeStruct((1, 3 * BASES + BACK), F32),
        ),
        in_specs=whole_vmem(1 + len(parts) + 4),
        out_specs=tuple(whole_vmem(2)),
        compiler_params=params,
        name="model",
    )(normal, *parts, far, near, science, good)
    return filtered, coef


def solution(mesh):
    placed = (
        P(("groups", "stripe"), "exp"),
        P(("groups", "exp"), "stripe", None),
        P(("groups", "exp"), "stripe", None),
        P(("groups", "stripe"), None),
        P(),
        P(),
    )
    return jax.shard_map(
        shards,
        mesh=mesh,
        in_specs=placed,
        out_specs=(P(("groups", "exp"), "stripe", None), P(("groups", "exp"), None)),
        check_vma=False,
    )
```

```python
import functools

import jax
import jax.numpy as jnp
from jax import lax
from jax.experimental import pallas as pl
from jax.experimental.pallas import tpu as pltpu
from jax.sharding import PartitionSpec as P

HALF = 9
TAPS = 2 * HALF + 1
BASES = 19
STAMP_W = 64
LANES = 128
BASE_PAD = 24
BACK = 7
FIT_ROWS = 3 * BASE_PAD
BACK_FIRST = BASE_PAD - BASES
TARGET = BASE_PAD + BASES + BACK - BACK_FIRST
PACKED = 2 * BASE_PAD
REACH = HALF + 1
GROUP = 32
GROUPS_TILE = LANES // GROUP
MAIN_TILES = 5
MAIN = MAIN_TILES * LANES
DEPTH = MAIN + LANES
EXTRA_ROWS = 80
NEAR_AT = TAPS * 16
NEAR_EXTRA_AT = NEAR_AT + 160
EARLY = NEAR_EXTRA_AT + 48
FAR_EXTRA_AT = 160
LATE = 2 * LANES
LATE_ROWS = -(-HALF * BASE_PAD // 16) * 16
F32 = jnp.float32
BF16 = jnp.bfloat16


def lane_id(rows):
    return lax.broadcasted_iota(jnp.int32, (rows, LANES), 1)


def row_id(rows):
    return lax.broadcasted_iota(jnp.int32, (rows, LANES), 0)


def split_two(values):
    high = values.astype(BF16)
    low = (values - high.astype(F32)).astype(BF16)
    return high, low


def put_split(target, start, values):
    size = values.shape[0]
    gap = target.shape[0] // 2
    target[start : start + size], target[gap + start : gap + start + size] = split_two(values)


def position(index, total):
    return (2.0 * index.astype(F32) + 1.0) / total - 1.0


def even_stripe():
    return lax.rem(lax.axis_index("stripe"), 2) == 0


def edge_kernel(cores, toward_near, *refs):
    pieces = refs[:cores]
    science_ref, good_ref = refs[cores : cores + 2]
    edge_ref, ext = refs[-2:]
    rows, half = pieces[0].shape
    wide = science_ref.shape[2]
    me = lax.axis_index("exp")
    for step in range(cores):
        start = lax.rem(me + step, cores) * half
        ext[:, pl.ds(pl.multiple_of(start, LANES), half)] = pieces[step][...]
    fold = wide // 2
    low_first = rows - 8

    def edge(first, extra, outer):
        parts = [ext[first : first + 8, :fold], ext[first : first + 8, fold:]]
        tail = []
        for line in (extra, extra + 1):
            tail += [ext[line : line + 1, :fold], ext[line : line + 1, fold:]]
        science = science_ref[0, outer : outer + 1, :]
        good = good_ref[0, outer : outer + 1, :]
        for line in (science, good):
            tail += [line[:, :fold], line[:, fold:]]
        return jnp.concatenate(parts + tail, axis=0)

    bottom = edge(low_first, rows - REACH, rows - 1)
    top = edge(0, 8, 0)
    edge_ref[...] = jnp.where(even_stripe() == toward_near, bottom, top)


def load_kernel(
    template_hbm,
    science_hbm,
    good_hbm,
    row_hbm,
    col_hbm,
    stamps_hbm,
    template_ref,
    science_ref,
    good_ref,
    row_ref,
    col_ref,
    odd_ref,
    mask_ref,
    stamps_ref,
    sems,
):
    moves = [
        pltpu.make_async_copy(source, target, sems.at[spot])
        for spot, (source, target) in enumerate(
            [
                (science_hbm, science_ref),
                (good_hbm, mask_ref),
                (template_hbm, template_ref),
                (row_hbm, row_ref),
                (col_hbm, col_ref),
                (stamps_hbm, stamps_ref),
            ]
        )
    ]
    for move in moves:
        move.start()
    for move in moves:
        move.wait()
    good_ref[...] = mask_ref[...].astype(F32)
    odd_ref[...] = jnp.concatenate(
        [
            jnp.full((1, LANES), lax.rem(stamps_ref[0, stamp], 2), jnp.int32)
            for stamp in range(odd_ref.shape[0])
        ],
        axis=0,
    )


def weight_kernel(
    row_ref, col_ref, weight_ref, late_ref, base_ref, pad
):
    pad[...] = jnp.zeros_like(pad)
    pad[0, 0:BASES, 0:TAPS] = row_ref[...]
    pad[1, 0:BASES, 0:TAPS] = col_ref[...]
    row = pad[0]
    lane = lane_id(BASE_PAD)
    group = lane // GROUP
    tiled = row
    for part in range(1, GROUPS_TILE):
        tiled = tiled + pltpu.roll(row, part * GROUP, 1)
    columns = [
        jnp.broadcast_to(pad[1, :, tap : tap + 1], (BASE_PAD, LANES)) for tap in range(TAPS)
    ]
    zero = jnp.zeros((BASE_PAD, LANES), F32)
    mains = []
    for tile in range(MAIN_TILES):
        spread = zero
        for part in range(GROUPS_TILE):
            tap = tile * GROUPS_TILE + part
            if tap < TAPS:
                spread = jnp.where(group == part, columns[tap], spread)
        mains.append(tiled * spread)
    spread = zero
    for tap in range(TAPS):
        spread = jnp.where(lane // 4 == tap, columns[tap], spread)
    corner = lax.rem(lane, 4)

    def tap_at(tap):
        return jnp.broadcast_to(pad[0, :, tap : tap + 1], (BASE_PAD, LANES))

    outer = jnp.where(
        corner == 0,
        tap_at(0),
        jnp.where(corner == 1, tap_at(1), jnp.where(corner == 2, tap_at(TAPS - 2), tap_at(TAPS - 1))),
    )
    inner = jnp.where(corner == 1, tap_at(0), jnp.where(corner == 2, tap_at(TAPS - 1), 0.0))
    outer = outer * spread
    inner = inner * spread
    for tile in range(MAIN_TILES):
        base_ref[:, tile * LANES : (tile + 1) * LANES] = mains[tile]
    base_ref[:, MAIN : MAIN + LANES] = outer
    base_ref[:, MAIN + LANES :] = inner
    rows = weight_ref.shape[0] // (2 * BASE_PAD)
    even = even_stripe()
    first_tap, last_tap = tap_at(0), tap_at(TAPS - 1)

    def column_tile(tap_of):
        spread = zero
        begin = 0
        for end in range(1, LANES + 1):
            if end < LANES and tap_of(end) == tap_of(begin):
                continue
            if tap_of(begin) < TAPS:
                spread = jnp.where((lane >= begin) & (lane < end), columns[tap_of(begin)], spread)
            begin = end
        return spread

    def early_tap(place):
        if place < NEAR_AT:
            return place // 16
        return (place - NEAR_AT) // 8 if place < NEAR_EXTRA_AT else (place - NEAR_EXTRA_AT) // 2

    def late_tap(place):
        return place // 8 if place < FAR_EXTRA_AT else (place - FAR_EXTRA_AT) // 2

    early_tiles = [
        column_tile(lambda spot, tile=tile: early_tap(tile * LANES + spot))
        for tile in range(EARLY // LANES)
    ]
    late_tiles = [
        column_tile(lambda spot, tile=tile: late_tap(tile * LANES + spot))
        for tile in range(LATE // LANES)
    ]

    def repeats(period):
        blocks = []
        for start in range(0, TAPS, period):
            block = pltpu.roll(row, (LANES - start) % LANES, 1) if start else row
            block = jnp.where(lane < period, block, 0.0)
            size = period
            while size < LANES:
                block = block + pltpu.roll(block, size, 1)
                size *= 2
            blocks.append(block)
        return blocks

    def window(blocks, period, first):
        block, move = first // period, first % period
        here = blocks[block] if 0 <= block < len(blocks) else None
        beyond = blocks[block + 1] if 0 <= block + 1 < len(blocks) else None
        if move == 0:
            return zero if here is None else here
        ready = lax.rem(lane, period) < period - move
        parts = [zero if part is None else pltpu.roll(part, LANES - move, 1) for part in (here, beyond)]
        return jnp.where(ready, parts[0], parts[1])

    by_sixteen, by_eight = repeats(16), repeats(8)
    own_rows = [window(by_sixteen, 16, HALF - line) for line in range(rows)]
    top_rows = [window(by_eight, 8, 1 - line) for line in range(rows)]
    bottom_rows = [window(by_eight, 8, rows + HALF - line) for line in range(rows)]

    parity = lax.rem(lane, 2)

    def corner_taps(upper, lower, is_upper):
        top = jnp.where(parity == 1, first_tap, 0.0) if upper else zero
        bottom = jnp.where(parity == 0, last_tap, 0.0) if lower else zero
        return jnp.where(is_upper, top, bottom)

    near_is_top = ~even
    early_rows, late_rows = [], []
    for spot in range(rows):
        odd_line = spot + rows - HALF if spot < HALF else spot - HALF
        own = jnp.where(even, own_rows[spot], own_rows[odd_line])
        side = jnp.where(even, bottom_rows[spot], top_rows[odd_line])
        extra = zero
        if spot >= HALF:
            extra = corner_taps(spot == HALF, spot == rows - 1, near_is_top)
        tiles = [
            own,
            own,
            jnp.where(lane < NEAR_AT - 2 * LANES, own, side),
            jnp.where(lane < NEAR_EXTRA_AT - 3 * LANES, side, extra),
        ]
        early_rows.append(
            jnp.concatenate([mine * tile for mine, tile in zip(tiles, early_tiles)], axis=1)
        )
        if spot < HALF:
            side = jnp.where(even, top_rows[spot], bottom_rows[odd_line])
            extra = corner_taps(spot == 0, spot == HALF - 1, even)
            tiles = [side, jnp.where(lane < FAR_EXTRA_AT - LANES, side, extra)]
            late_rows.append(
                jnp.concatenate([mine * tile for mine, tile in zip(tiles, late_tiles)], axis=1)
            )
    for spot in range(0, rows, 2):
        put_split(weight_ref, spot * BASE_PAD, jnp.concatenate(early_rows[spot : spot + 2], axis=0))
    spare = late_ref.shape[0] // 2 - HALF * BASE_PAD
    late_rows.append(jnp.zeros((spare, LATE), F32))
    put_split(late_ref, 0, jnp.concatenate(late_rows, axis=0))


def edges_of(near_ref, far_ref):
    even = even_stripe()
    near = near_ref[...]
    far = far_ref[...]
    return jnp.where(even, far, near), jnp.where(even, near, far)


def fill_extended(ext, highs, lows, cores, pieces, near_ref, far_ref):
    rows, half = pieces[0].shape
    wide = half * cores
    fold = wide // 2
    ext[:, 0:LANES] = jnp.zeros((ext.shape[0], LANES), F32)
    ext[:, LANES + wide :] = jnp.zeros((ext.shape[0], LANES), F32)
    me = lax.axis_index("exp")
    for step in range(cores):
        start = lax.rem(me + step, cores) * half + LANES
        ext[8 : 8 + rows, pl.ds(pl.multiple_of(start, LANES), half)] = pieces[step][...]
    top, bottom = edges_of(near_ref, far_ref)
    for side in range(2):
        where = pl.ds(LANES + side * fold, fold)
        ext[0:8, where] = top[8 * side : 8 * side + 8]
        ext[8 + rows : 16 + rows, where] = bottom[8 * side : 8 * side + 8]
        spare = [
            top[16 + side : 17 + side],
            top[18 + side : 19 + side],
            bottom[16 + side : 17 + side],
            bottom[18 + side : 19 + side],
        ]
        ext[16 + rows : 24 + rows, where] = jnp.concatenate(spare + spare, axis=0)
    main = slice(0, GROUP)
    highs[main], lows[main] = split_two(ext[main])
    extra = ext[GROUP : GROUP + 8]
    span = extra.shape[1]
    early = lax.broadcasted_iota(jnp.int32, extra.shape, 0) < 4
    ahead = [extra] + [pltpu.roll(extra, span - part, 1) for part in range(1, 4)]
    lines = jnp.concatenate(
        [jnp.where(early, ahead[0], ahead[1]), jnp.where(early, ahead[2], ahead[3])], axis=0
    )
    highs[GROUP:], lows[GROUP:] = split_two(lines)


def spread_window(shifted, put):
    for tap in range(TAPS):
        put(tap * GROUP, shifted(tap, slice(0, GROUP)))
    for quad in range(MAIN_TILES):
        put(MAIN + 16 * quad, shifted(4 * quad, slice(GROUP, GROUP + 16)))


def clear_spare(refs):
    for ref in refs:
        wide = ref.shape[1]
        ref[TAPS * GROUP : MAIN] = jnp.zeros((MAIN - TAPS * GROUP, wide), BF16)
        ref[MAIN + EXTRA_ROWS :] = jnp.zeros((LANES - EXTRA_ROWS, wide), BF16)


def back_profile(horiz):
    steady = jnp.ones_like(horiz)
    square = 0.5 * (3.0 * horiz * horiz - 1.0)
    return [steady, horiz, steady, horiz, square, steady, horiz]


def put_halves(target, edge_ref, rows, first):
    fold = edge_ref.shape[1]
    for side in range(2):
        where = pl.ds(LANES + side * fold, fold)
        target[first : first + 8, where] = edge_ref[8 * side : 8 * side + 8]
        for line in range(2):
            spot = 16 + 2 * line + side
            target[rows + line : rows + line + 1, where] = edge_ref[spot : spot + 1]


def paired(values):
    span = values.shape[1]
    return jnp.concatenate([values, pltpu.roll(values, span - 1, 1)], axis=0)


def corner_block(lines):
    span = lines.shape[1]
    parts = [lines] + [pltpu.roll(lines, span - move, 1) for move in range(1, 8)]
    return jnp.concatenate(parts, axis=0)


def odd_rows(odd_ref, stamp, height):
    return jnp.broadcast_to(odd_ref[stamp : stamp + 1, :] == 1, (height, LANES))


def stamp_window(source, odd_ref, stamp, offset):
    height = source.shape[0]
    lane = lane_id(height)
    left = source[:, stamp * LANES : (stamp + 1) * LANES]
    centre = source[:, (stamp + 1) * LANES : (stamp + 2) * LANES]
    right = source[:, (stamp + 2) * LANES : (stamp + 3) * LANES]
    odd = jnp.where(lane < LANES // 4, right, centre)
    even = jnp.where(lane >= LANES - HALF, left, centre)
    odd = pltpu.roll(odd, (HALF + STAMP_W + offset) % LANES, 1)
    even = pltpu.roll(even, HALF + offset, 1)
    return jnp.where(odd_rows(odd_ref, stamp, height), odd, even)


def stamp_shifts(sources, targets, odd_ref, pair, moves):
    columns = slice(pair * LANES, (pair + 1) * LANES)
    for source, target in zip(sources, targets):
        first = stamp_window(source, odd_ref, 2 * pair, 0)
        second = stamp_window(source, odd_ref, 2 * pair + 1, STAMP_W)
        for spot, (tile, move) in enumerate(moves):
            a, b = first[16 * tile : 16 * tile + 16], second[16 * tile : 16 * tile + 16]
            if move:
                a = pltpu.roll(a, LANES - move, 1)
                b = pltpu.roll(b, LANES - move, 1)
            target[16 * spot : 16 * spot + 16, columns] = jnp.where(
                lane_id(16) < STAMP_W, a, b
            )


def stamp_values(sources, odd_ref, pair, moves):
    out = []
    for source in sources:
        first = stamp_window(source, odd_ref, 2 * pair, 0)
        second = stamp_window(source, odd_ref, 2 * pair + 1, STAMP_W)
        tiles = []
        for tile, move in moves:
            a, b = first[16 * tile : 16 * tile + 16], second[16 * tile : 16 * tile + 16]
            if move:
                a = pltpu.roll(a, LANES - move, 1)
                b = pltpu.roll(b, LANES - move, 1)
            tiles.append(jnp.where(lane_id(16) < STAMP_W, a, b))
        out.append(jnp.concatenate(tiles, axis=0))
    return out


def three_products(weights, xhigh, xlow):
    rows = weights.shape[0] // 2
    both = jnp.dot(weights, xhigh, preferred_element_type=F32)
    return both[:rows] + (
        both[rows:] + jnp.dot(weights[:rows], xlow, preferred_element_type=F32)
    )


def back_rows(rows):
    empty = jnp.zeros_like(rows[0])
    lead = [empty] * (8 - BACK_FIRST)
    second = lead + rows[BACK_FIRST:]
    second += [empty] * (8 - len(second))
    return [jnp.concatenate(part, axis=0) for part in (lead + rows[:BACK_FIRST], second)]


def design_line(bases, keep, target, horiz, profiles, row, region_rows):
    own = bases * keep
    vert = position(jnp.full(horiz.shape, row, jnp.int32), region_rows)
    square = 0.5 * (3.0 * vert * vert - 1.0)
    steady = jnp.ones_like(vert)
    scales = back_rows([steady, steady, vert, vert, steady, square, square])
    first, second = (profile * scale * keep for profile, scale in zip(profiles, scales))
    spot = lax.broadcasted_iota(jnp.int32, second.shape, 0)
    second = jnp.where(spot == TARGET % 8, target, second)
    sloped = own * horiz
    return jnp.concatenate(
        [own[:16], own[16:] + first, sloped[:16], sloped[16:] + second, own * vert], axis=0
    )


def gram(lines):
    design = jnp.concatenate([line.astype(BF16) for line in lines], axis=1)
    return lax.dot_general(design, design, (((1,), (1,)), ((), ())), preferred_element_type=F32)


def early_kernel(cores, stripes, *refs):
    pieces = refs[:cores]
    (
        near_ref,
        science_ref,
        good_ref,
        odd_ref,
        weight_ref,
        total_ref,
        late_ref,
        aux_ref,
        ext,
        highs,
        lows,
        xhigh,
        xlow,
        bases,
    ) = refs[cores:]
    rows, half = pieces[0].shape
    wide = science_ref.shape[2]
    pairs = wide // (4 * STAMP_W)
    me = lax.axis_index("exp")
    ext[:, 0:LANES] = jnp.zeros((ext.shape[0], LANES), F32)
    ext[:, LANES + wide :] = jnp.zeros((ext.shape[0], LANES), F32)
    for step in range(cores):
        start = lax.rem(me + step, cores) * half + LANES
        ext[0:rows, pl.ds(pl.multiple_of(start, LANES), half)] = pieces[step][...]
    put_halves(ext, near_ref, rows + 8, rows)
    lines = jnp.concatenate(
        [ext[0:rows], paired(ext[rows : rows + 8]), corner_block(ext[rows + 8 : rows + 10])], axis=0
    )
    highs[...], lows[...] = split_two(lines)
    moves = [(0, tap) for tap in range(TAPS)]
    moves += [(1, 2 * step) for step in range(10)]
    moves += [(2, 8 * step) for step in range(3)]
    lane = lane_id(1)
    for pair in range(pairs):
        columns = slice(pair * LANES, (pair + 1) * LANES)
        stamp_shifts((highs, lows), (xhigh, xlow), odd_ref, pair, moves)
        odd = jnp.where(
            lane < STAMP_W,
            odd_ref[2 * pair : 2 * pair + 1],
            odd_ref[2 * pair + 1 : 2 * pair + 2] + 1,
        )
        horiz = position(4 * pair * STAMP_W + odd * STAMP_W + lane, wide)
        aux_ref[2 * rows : 2 * rows + 8, columns] = jnp.broadcast_to(horiz, (8, LANES))
        picked = []
        for source in (good_ref, science_ref):
            lower = source[0, :, 2 * pair * LANES : (2 * pair + 1) * LANES]
            upper = source[0, :, (2 * pair + 1) * LANES : (2 * pair + 2) * LANES]
            lower = jnp.where(
                odd_rows(odd_ref, 2 * pair, rows), pltpu.roll(lower, STAMP_W, 1), lower
            )
            upper = jnp.where(
                odd_rows(odd_ref, 2 * pair + 1, rows), upper, pltpu.roll(upper, STAMP_W, 1)
            )
            picked.append(jnp.where(lane_id(rows) < STAMP_W, lower, upper))
        aux_ref[0:rows, columns] = picked[0]
        aux_ref[rows : 2 * rows, columns] = picked[0] * picked[1]
    split = HALF * BASE_PAD
    chunk = 2 * LANES
    for start in range(0, wide // 2, chunk):
        span = slice(start, start + chunk)
        values = three_products(weight_ref[...], xhigh[:, span], xlow[:, span])
        late_ref[:, span] = values[:split]
        bases[:, span] = values[split:]
    horiz = aux_ref[2 * rows : 2 * rows + 1]
    profile = back_rows(back_profile(horiz))
    first_line = jnp.where(even_stripe(), HALF, 0)
    first_row = lax.axis_index("stripe") * rows
    designs = []
    for spot in range(rows - HALF):
        line = first_line + spot
        designs.append(design_line(
            bases[spot * BASE_PAD : (spot + 1) * BASE_PAD],
            aux_ref[pl.ds(line, 1), :],
            aux_ref[pl.ds(rows + line, 1), :],
            horiz,
            profile,
            first_row + line,
            rows * stripes,
        ))
    total = gram(designs)
    total_ref[...] = jnp.concatenate(
        [total, jnp.zeros((FIT_ROWS, LANES - FIT_ROWS), F32)], axis=1
    )


def late_kernel(stripes, rows, *refs):
    (
        far_ref,
        odd_ref,
        weight_ref,
        total_ref,
        early_ref,
        aux_ref,
        out_ref,
        ext,
        highs,
        lows,
        bases,
    ) = refs
    width = early_ref.shape[1]
    pairs = width // LANES
    ext[:, 0:LANES] = jnp.zeros((ext.shape[0], LANES), F32)
    ext[:, ext.shape[1] - LANES :] = jnp.zeros((ext.shape[0], LANES), F32)
    put_halves(ext, far_ref, 8, 0)
    lines = jnp.concatenate([paired(ext[0:8]), corner_block(ext[8:10])], axis=0)
    highs[...], lows[...] = split_two(lines)
    moves = [(0, 2 * step) for step in range(10)] + [(1, 8 * step) for step in range(3)]
    used = 16 * len(moves)
    split = HALF * BASE_PAD
    chunk = 4 * LANES
    for start in range(0, width, chunk):
        span = slice(start, start + chunk)
        made = [
            stamp_values((highs, lows), odd_ref, pair, moves)
            for pair in range(start // LANES, (start + chunk) // LANES)
        ]
        spare = jnp.zeros((LATE - used, chunk), BF16)
        xh, xl = (
            jnp.concatenate([jnp.concatenate([one[side] for one in made], axis=1), spare], axis=0)
            for side in range(2)
        )
        values = three_products(weight_ref[...], xh, xl)
        bases[:, span] = early_ref[:, span] + values[:split]
    horiz = aux_ref[2 * rows : 2 * rows + 1]
    profile = back_rows(back_profile(horiz))
    first_line = jnp.where(even_stripe(), 0, rows - HALF)
    first_row = lax.axis_index("stripe") * rows
    designs = []
    for spot in range(HALF):
        line = first_line + spot
        designs.append(
            design_line(
                bases[spot * BASE_PAD : (spot + 1) * BASE_PAD],
                aux_ref[pl.ds(line, 1), :],
                aux_ref[pl.ds(rows + line, 1), :],
                horiz,
                profile,
                first_row + line,
                rows * stripes,
            )
        )
    own = total_ref[:, :FIT_ROWS] + gram(designs)
    out_ref[...] = packed_normal(own)


def packed_normal(normal):
    room = LANES - FIT_ROWS
    last = normal[PACKED:]
    spare = jnp.zeros((BASE_PAD, 2 * room - FIT_ROWS), F32)
    return jnp.concatenate(
        [
            jnp.concatenate([normal[:BASE_PAD], last[:, :room]], axis=1),
            jnp.concatenate([normal[BASE_PAD:PACKED], last[:, room:], spare], axis=1),
        ],
        axis=0,
    )


def unpacked_normal(packed):
    room = LANES - FIT_ROWS
    lane = lane_id(BASE_PAD)
    last = jnp.where(
        lane < room,
        pltpu.roll(packed[:BASE_PAD], room, 1),
        pltpu.roll(packed[BASE_PAD:], 2 * room, 1),
    )
    values = jnp.concatenate([packed, last], axis=0)
    return jnp.where(lane_id(FIT_ROWS) < FIT_ROWS, values, 0.0)


def panels():
    out = []
    for term, used in enumerate((BASE_PAD, BASES + BACK - BACK_FIRST, BASES)):
        for start in range(0, used, 8):
            out.append((term * BASE_PAD + start, min(8, used - start)))
    return out


def tree_sum(values):
    while len(values) > 1:
        values = [sum(values[spot : spot + 2][1:], values[spot]) for spot in range(0, len(values), 2)]
    return values[0]


def solve_rows(matrix):
    sub = row_id(8)
    tiles = [matrix[start : start + 8] for start in range(0, FIT_ROWS, 8)]
    order = panels()

    def spread(tile, spot):
        return jnp.broadcast_to(tile[spot : spot + 1], (8, LANES))

    def column(tile, spot):
        return jnp.broadcast_to(tile[:, spot : spot + 1], (8, LANES))

    start, size = order[0]
    corner = [column(tiles[start // 8], start + j) for j in range(size)]
    for step, (start, size) in enumerate(order):
        home = start // 8
        columns = [
            [None if place == home else column(tile, start + j) for place, tile in enumerate(tiles)]
            for j in range(size)
        ]
        rows = tiles[home]
        following = order[step + 1] if step + 1 < len(order) else (0, 0)
        next_home = following[0] // 8
        ahead = [column(rows, following[0] + j) for j in range(following[1])]
        below = [column(tiles[next_home], following[0] + j) for j in range(following[1])]
        for spot in range(size):
            keep = sub == spot
            inverse = 1.0 / spread(corner[spot], spot)
            others = jnp.where(keep, 0.0, corner[spot])

            def eliminated(values):
                scaled = spread(values, spot) * inverse
                return jnp.where(keep, scaled, values - others * scaled)

            corner = [
                eliminated(values) if j > spot else values for j, values in enumerate(corner)
            ]
            ahead = [eliminated(values) for values in ahead]
            rows = eliminated(rows)
        if following[1]:
            corner = [
                values - tree_sum([columns[i][next_home] * spread(ahead[j], i) for i in range(size)])
                for j, values in enumerate(below)
            ]
        for place in range(len(tiles)):
            if place == home:
                tiles[place] = rows
            else:
                tiles[place] = tiles[place] - tree_sum(
                    [columns[i][place] * spread(rows, i) for i in range(size)]
                )
    line = row_id(FIT_ROWS)
    used = (line < TARGET) | ((line >= PACKED) & (line < PACKED + BASES))
    right = jnp.concatenate(tiles, axis=0)[:, TARGET : TARGET + 1]
    return jnp.where(used, jnp.broadcast_to(right, (FIT_ROWS, LANES)), 0.0)


def region_weights(base_ref, weight_ref, rows):
    lane = lane_id(8)
    spot = lax.rem(lane, GROUP)
    corner = lax.rem(lane, 4)
    line = row_id(8)
    mains = [base_ref[:, tile * LANES : (tile + 1) * LANES] for tile in range(MAIN_TILES)]
    outer = base_ref[:, MAIN : MAIN + LANES]
    inner = base_ref[:, MAIN + LANES :]
    blocks = [[] for _ in range(BASES)]
    for start in range(0, rows, 8):
        tap = spot - (start + line - 1)
        inside = (tap >= 0) & (tap < TAPS)
        moved = [pltpu.roll(main, (start - 1) % LANES, 1) for main in mains]
        extra = zero_row = jnp.zeros((8, LANES), F32)
        for b in range(BASES):
            tiles = []
            for main in moved:
                wide = jnp.broadcast_to(main[b : b + 1], (8, LANES))
                tiles.append(
                    jnp.where(inside, pltpu.roll(wide, 0, 1, stride=1, stride_axis=0), 0.0)
                )
            extra = zero_row
            mine = jnp.broadcast_to(inner[b : b + 1], (8, LANES))
            if start == 0:
                extra = jnp.where((line == 0) & (corner < 2), mine, extra)
            if start == rows - 8:
                extra = jnp.where((line == 7) & (corner >= 2), mine, extra)
            blocks[b].append(jnp.concatenate(tiles + [extra], axis=1))
    for b in range(BASES):
        put_split(weight_ref, b * rows, jnp.concatenate(blocks[b], axis=0))
    lane = lane_id(BASE_PAD)
    spot = lax.rem(lane, GROUP)
    corner = lax.rem(lane, 4)
    halos = []
    for shift, extra in ((rows - 1, corner >= 2), (-2, corner < 2)):
        tap = spot - shift
        inside = (tap >= 0) & (tap < TAPS)
        tiles = [jnp.where(inside, pltpu.roll(main, shift % LANES, 1), 0.0) for main in mains]
        halos.append(jnp.concatenate(tiles + [jnp.where(extra, outer, 0.0)], axis=1))
    put_split(weight_ref, BASES * rows, jnp.concatenate(halos, axis=0))


def region_bases(highs, lows, weight_ref, first, out_ref, xhigh, xlow):
    clear_spare((xhigh, xlow))
    wide = out_ref.shape[1]
    chunk = 2 * LANES
    for start in range(0, wide, chunk):
        span = slice(start, start + chunk)
        for source, target in ((highs, xhigh), (lows, xlow)):

            def shifted(tap, lines):
                begin = first + start + LANES - HALF + tap
                return source[lines, begin : begin + chunk]

            def put(place, values):
                target[place : place + values.shape[0], span] = values

            spread_window(shifted, put)
        out_ref[:, span] = three_products(weight_ref[...], xhigh[:, span], xlow[:, span])


def first_bases_kernel(cores, *refs):
    pieces = refs[:cores]
    (
        far_ref,
        near_ref,
        base_ref,
        after_ref,
        weight_ref,
        highs,
        lows,
        out_ref,
        ext,
        xhigh,
        xlow,
    ) = refs[cores:]
    region_weights(base_ref, weight_ref, pieces[0].shape[0])
    fill_extended(ext, highs, lows, cores, pieces, near_ref, far_ref)
    region_bases(highs, lows, weight_ref, 0, out_ref, xhigh, xlow)


def next_bases_kernel(first, highs, lows, weight_ref, after_ref, out_ref, xhigh, xlow):
    region_bases(highs, lows, weight_ref, first, out_ref, xhigh, xlow)


def add_kernel(count, *refs):
    values = [ref[...] for ref in refs[:count]]
    if count == 4:
        order = (1, 2, 0)
        values = [values[0]] + [values[1 + order.index(k)] for k in range(3)]
    refs[-1][...] = tree_sum(values)


def model_kernel(stripes, normal_ref, *refs):
    far_ref, near_ref, science_ref, good_ref, out_ref, coef_ref = refs[-6:]
    parts = refs[:-6]
    rows = science_ref.shape[1]
    wide = science_ref.shape[2]
    top, bottom = edges_of(near_ref, far_ref)
    coef = solve_rows(unpacked_normal(normal_ref[...]))
    lane = lane_id(FIT_ROWS)
    home = lane - 3 * BASES + jnp.where(lane < 3 * BASES + BACK_FIRST, BASES, BASE_PAD + BASES - BACK_FIRST)
    home = jnp.where(lane < 3 * BASES, lax.rem(lane, 3) * BASE_PAD + lane // 3, home)
    flat = jnp.sum(jnp.where(row_id(FIT_ROWS) == home, coef, 0.0), axis=0, keepdims=True)
    coef_ref[...] = flat[:, : coef_ref.shape[1]]

    def share(spot, height):
        return jnp.broadcast_to(coef[spot : spot + 1], (height, LANES))

    first_row = lax.axis_index("stripe") * rows
    vert = position(first_row + row_id(rows), rows * stripes)
    halo_vert = [
        position(jnp.full((8, LANES), first_row + line, jnp.int32), rows * stripes)
        for line in (rows, -1)
    ]
    slopes = [share(2 * BASE_PAD + b, rows) * vert for b in range(BASES)]
    halo_slopes = [
        coef[2 * BASE_PAD : 3 * BASE_PAD] * jnp.concatenate([line] * 3, axis=0) for line in halo_vert
    ]
    level = [
        share(BASES + m + (0 if m < BACK_FIRST else BASE_PAD - BACK_FIRST), 8) for m in range(BACK)
    ]

    def ground(here, horiz):
        square = 0.5 * (3.0 * here * here - 1.0)
        horiz_square = 0.5 * (3.0 * horiz * horiz - 1.0)
        steady = level[0] + level[1] * horiz + level[4] * horiz_square
        sloped = level[2] + level[3] * horiz
        curved = level[5] + level[6] * horiz
        if here.shape[0] > 8:
            steady, sloped, curved = (
                jnp.concatenate([part] * (here.shape[0] // 8), axis=0)
                for part in (steady, sloped, curved)
            )
        return steady + here * sloped + square * curved

    models, halos = [], [[], []]
    for part in parts:
        for start in range(0, part.shape[1], LANES):
            span = slice(start, start + LANES)
            begin = len(models) * LANES
            horiz = position(begin + lane_id(8), wide)
            total = ground(vert, horiz)
            for b in range(BASES):
                steady = share(b, 8) + share(BASE_PAD + b, 8) * horiz
                scale = jnp.concatenate([steady] * (rows // 8), axis=0) + slopes[b]
                total = total + part[b * rows : (b + 1) * rows, span] * scale
            models.append(total)
            steady = coef[:BASE_PAD] + coef[BASE_PAD : 2 * BASE_PAD] * horiz[0:1]
            for side in range(2):
                place = BASES * rows + side * BASE_PAD
                values = part[place : place + BASE_PAD, span] * (steady + halo_slopes[side])
                values = jnp.sum(values, axis=0, keepdims=True)
                halos[side].append(values + ground(halo_vert[side], horiz)[0:1])
    model = jnp.concatenate(models, axis=1)
    below_model, above_model = (jnp.concatenate(side, axis=1) for side in halos)
    own = good_ref[0] * (science_ref[0] - model)

    def halo(edge, values):
        science = jnp.concatenate([edge[20:21], edge[21:22]], axis=1)
        good = jnp.concatenate([edge[22:23], edge[23:24]], axis=1)
        return good * (science - values)

    above_row = halo(top, above_model)
    below_row = halo(bottom, below_model)
    lines = lax.broadcasted_iota(jnp.int32, (rows, wide), 0)
    spots = lax.broadcasted_iota(jnp.int32, (rows, wide), 1)
    above = jnp.where(lines == 0, above_row, pltpu.roll(own, 1, 0))
    below = jnp.where(lines == rows - 1, below_row, pltpu.roll(own, rows - 1, 0))
    before = jnp.where(spots == 0, 0.0, pltpu.roll(own, 1, 1))
    after = jnp.where(spots == wide - 1, 0.0, pltpu.roll(own, wide - 1, 1))
    out_ref[0] = 4.0 * own - (below + above + after + before)


def whole_vmem(count):
    return [pl.BlockSpec(memory_space=pltpu.VMEM)] * count


def add(values, after, params):
    return pl.pallas_call(
        functools.partial(add_kernel, len(values)),
        out_shape=jax.ShapeDtypeStruct(values[0].shape, values[0].dtype),
        in_specs=whole_vmem(len(values) + len(after)),
        out_specs=pl.BlockSpec(memory_space=pltpu.VMEM),
        compiler_params=params,
        name="add",
    )(*values, *after)


def summed(values, axis, beside, params):
    count = lax.axis_size(axis)
    if count & (count - 1):
        for works in beside:
            for work in works:
                work(values)
        return lax.psum(values, axis)
    rounds = [(1, 2, 3)] if count >= 4 else []
    step = 4 if rounds else 1
    while step < count:
        rounds.append((step,))
        step *= 2
    rounds += [()] * (len(beside) - len(rounds))
    for spot, steps in enumerate(rounds):
        others = [
            lax.ppermute(values, axis, [(i, i ^ step) for i in range(count)]) for step in steps
        ]
        after = [work(values) for work in beside[spot]] if spot < len(beside) else []
        if steps:
            if len(others) == 3:
                others = [others[k] for k in (1, 2, 0)]
            values = add([values] + others, after, params)
    return values


def shards(template, exposure, cosmic_mask, stamp_blocks, row_filters, col_filters):
    arguments = (template, exposure, cosmic_mask, row_filters, col_filters, stamp_blocks)
    rows, half = template.shape
    wide = exposure.shape[2]
    cores = lax.axis_size("exp")
    stripes = lax.axis_size("stripe")
    params = pltpu.CompilerParams(vmem_limit_bytes=24 * 1024 * 1024)
    pieces = [template] + [
        lax.ppermute(template, "exp", [((i + step) % cores, i) for i in range(cores)])
        for step in range(1, cores)
    ]
    stamps = stamp_blocks.shape[1]
    template_in, science, good, row_in, col_in, odd = pl.pallas_call(
        load_kernel,
        out_shape=(
            jax.ShapeDtypeStruct(template.shape, F32),
            jax.ShapeDtypeStruct(exposure.shape, F32),
            jax.ShapeDtypeStruct(exposure.shape, F32),
            jax.ShapeDtypeStruct(row_filters.shape, F32),
            jax.ShapeDtypeStruct(col_filters.shape, F32),
            jax.ShapeDtypeStruct((stamps, LANES), jnp.int32),
        ),
        in_specs=[pl.BlockSpec(memory_space=pltpu.HBM)] * 6,
        out_specs=tuple(whole_vmem(6)),
        scratch_shapes=[
            pltpu.VMEM(cosmic_mask.shape, jnp.int32),
            pltpu.SMEM(stamp_blocks.shape, jnp.int32),
            pltpu.SemaphoreType.DMA((6,)),
        ],
        compiler_params=params,
        name="load",
    )(*[pltpu.with_memory_space_constraint(array, pltpu.HBM) for array in arguments])
    pieces = [template_in] + pieces[1:]
    edge_shape = jax.ShapeDtypeStruct((24, wide // 2), F32)

    def edge(toward_near, *others):
        return pl.pallas_call(
            functools.partial(edge_kernel, cores, toward_near),
            out_shape=edge_shape,
            in_specs=whole_vmem(cores + 2 + len(others)),
            out_specs=pl.BlockSpec(memory_space=pltpu.VMEM),
            scratch_shapes=[pltpu.VMEM((rows, wide), F32)],
            compiler_params=params,
            name="edges",
        )(*pieces, science, good, *others)

    far = edge(False)
    near = edge(True)
    near_pairs = [(i, i + 1) for i in range(0, stripes - 1, 2)]
    far_pairs = [(i, i + 1) for i in range(1, stripes - 1, 2)]

    def swapped(values, couples):
        return lax.ppermute(values, "stripe", couples + [(b, a) for a, b in couples])

    far = swapped(far, far_pairs)
    near = swapped(near, near_pairs)
    early_shape = jax.ShapeDtypeStruct((2 * rows * BASE_PAD, EARLY), BF16)
    late_shape = jax.ShapeDtypeStruct((2 * LATE_ROWS, LATE), BF16)
    early_weights, late_weights, base = pl.pallas_call(
        weight_kernel,
        out_shape=(
            early_shape,
            late_shape,
            jax.ShapeDtypeStruct((BASE_PAD, DEPTH + LANES), F32),
        ),
        in_specs=whole_vmem(2),
        out_specs=tuple(whole_vmem(3)),
        scratch_shapes=[pltpu.VMEM((2, BASE_PAD, LANES), F32)],
        compiler_params=params,
        name="weights",
    )(row_in, col_in)
    width = wide // 2
    reach = wide + 2 * LANES
    normal_shape = jax.ShapeDtypeStruct((FIT_ROWS, LANES), F32)
    part, kept, aux = pl.pallas_call(
        functools.partial(early_kernel, cores, stripes),
        out_shape=(
            normal_shape,
            jax.ShapeDtypeStruct((HALF * BASE_PAD, width), F32),
            jax.ShapeDtypeStruct((2 * rows + 8, width), F32),
        ),
        in_specs=whole_vmem(cores + 5),
        out_specs=tuple(whole_vmem(3)),
        scratch_shapes=[
            pltpu.VMEM((rows + 16, reach), F32),
            pltpu.VMEM((rows + 32, reach), BF16),
            pltpu.VMEM((rows + 32, reach), BF16),
            pltpu.VMEM((EARLY, width), BF16),
            pltpu.VMEM((EARLY, width), BF16),
            pltpu.VMEM(((rows - HALF) * BASE_PAD, width), F32),
        ],
        compiler_params=params,
        name="early",
    )(*pieces, near, science, good, odd, early_weights)
    normal = pl.pallas_call(
        functools.partial(late_kernel, stripes, rows),
        out_shape=jax.ShapeDtypeStruct((PACKED, LANES), F32),
        in_specs=whole_vmem(6),
        out_specs=pl.BlockSpec(memory_space=pltpu.VMEM),
        scratch_shapes=[
            pltpu.VMEM((16, reach), F32),
            pltpu.VMEM((32, reach), BF16),
            pltpu.VMEM((32, reach), BF16),
            pltpu.VMEM((HALF * BASE_PAD, width), F32),
        ],
        compiler_params=params,
        name="late",
    )(far, odd, late_weights, part, kept, aux)
    region_rows = BASES * rows + 2 * BASE_PAD
    blocks = wide // (2 * LANES)
    cuts = [blocks * cut // 8 * 2 * LANES for cut in (0, 2, 5, 8)]
    weight_shape = jax.ShapeDtypeStruct((2 * region_rows, DEPTH), BF16)
    source_shape = jax.ShapeDtypeStruct((GROUP + 16, reach), BF16)
    parts, shared = [], []

    def shift_scratch(size):
        return [pltpu.VMEM((DEPTH, size), BF16)] * 2

    def first_bases(after):
        size = cuts[1]
        *made, part = pl.pallas_call(
            functools.partial(first_bases_kernel, cores),
            out_shape=(
                weight_shape,
                source_shape,
                source_shape,
                jax.ShapeDtypeStruct((region_rows, size), F32),
            ),
            in_specs=whole_vmem(cores + 4),
            out_specs=tuple(whole_vmem(4)),
            scratch_shapes=[pltpu.VMEM((rows + 24, reach), F32)] + shift_scratch(size),
            compiler_params=params,
            name="bases",
        )(*pieces, far, near, base, after)
        shared.extend(made)
        parts.append(part)
        return part

    def next_bases(cut, after):
        size = cuts[cut + 1] - cuts[cut]
        region_weight, highs, lows = shared
        part = pl.pallas_call(
            functools.partial(next_bases_kernel, cuts[cut]),
            out_shape=jax.ShapeDtypeStruct((region_rows, size), F32),
            in_specs=whole_vmem(4),
            out_specs=pl.BlockSpec(memory_space=pltpu.VMEM),
            scratch_shapes=shift_scratch(size),
            compiler_params=params,
            name="bases",
        )(highs, lows, region_weight, after)
        parts.append(part)
        return part

    beside = [[first_bases, functools.partial(next_bases, 1)], [functools.partial(next_bases, 2)]]
    normal = summed(normal, "stripe", beside, params)
    filtered, coef = pl.pallas_call(
        functools.partial(model_kernel, stripes),
        out_shape=(
            jax.ShapeDtypeStruct(exposure.shape, F32),
            jax.ShapeDtypeStruct((1, 3 * BASES + BACK), F32),
        ),
        in_specs=whole_vmem(1 + len(parts) + 4),
        out_specs=tuple(whole_vmem(2)),
        compiler_params=params,
        name="model",
    )(normal, *parts, far, near, science, good)
    return filtered, coef


def solution(mesh):
    placed = (
        P(("groups", "stripe"), "exp"),
        P(("groups", "exp"), "stripe", None),
        P(("groups", "exp"), "stripe", None),
        P(("groups", "stripe"), None),
        P(),
        P(),
    )
    return jax.shard_map(
        shards,
        mesh=mesh,
        in_specs=placed,
        out_specs=(P(("groups", "exp"), "stripe", None), P(("groups", "exp"), None)),
        check_vma=False,
    )
```

```python
import functools

import jax
import jax.numpy as jnp
from jax import lax
from jax.experimental import pallas as pl
from jax.experimental.pallas import tpu as pltpu
from jax.sharding import PartitionSpec as P

HALF = 9
TAPS = 2 * HALF + 1
BASES = 19
STAMP_W = 64
LANES = 128
BASE_PAD = 24
BACK = 7
BACK_FIRST = BASE_PAD - BASES
ALIGNED = BASES // 8 * 8
SPILL = BASES - ALIGNED
SPILL_AT = BASE_PAD - SPILL
UNKNOWNS = 2 * BASE_PAD + ALIGNED
FIT_ROWS = UNKNOWNS + 8
REACH = HALF + 1
GROUP = 32
GROUPS_TILE = LANES // GROUP
MAIN_TILES = 5
MAIN = MAIN_TILES * LANES
DEPTH = MAIN + LANES
EXTRA_ROWS = 80
NEAR_AT = TAPS * 16
NEAR_EXTRA_AT = NEAR_AT + 160
EARLY = NEAR_EXTRA_AT + 48
FAR_EXTRA_AT = 160
LATE = 2 * LANES
LATE_ROWS = -(-HALF * BASE_PAD // 16) * 16
F32 = jnp.float32
BF16 = jnp.bfloat16


def lane_id(rows):
    return lax.broadcasted_iota(jnp.int32, (rows, LANES), 1)


def row_id(rows):
    return lax.broadcasted_iota(jnp.int32, (rows, LANES), 0)


def split_two(values):
    high = values.astype(BF16)
    low = (values - high.astype(F32)).astype(BF16)
    return high, low


def put_split(target, start, values):
    size = values.shape[0]
    gap = target.shape[0] // 2
    target[start : start + size], target[gap + start : gap + start + size] = split_two(values)


def position(index, total):
    return (2.0 * index.astype(F32) + 1.0) / total - 1.0


def even_stripe():
    return lax.rem(lax.axis_index("stripe"), 2) == 0


def edge_lines(rows, toward_near):
    last = (rows - 8, rows - REACH, rows - 1)
    first = (0, 8, 0)
    return (last, first) if toward_near else (first, last)


def sides_of(line, cores):
    fold = line.shape[1] // cores
    return [line[:, side * fold : (side + 1) * fold] for side in range(cores)]


def near_kernel(cores, template_ref, science_ref, good_ref, edge_ref):
    rows = template_ref.shape[0]

    def edge(main, extra, outer):
        parts = [template_ref[main : main + 8], template_ref[extra : extra + 2]]
        for source in (science_ref, good_ref):
            parts += sides_of(source[0, outer : outer + 1, :], cores)
        spare = edge_ref.shape[0] - REACH - 2 * cores
        return jnp.concatenate(parts + [jnp.zeros((spare, edge_ref.shape[1]), F32)], axis=0)

    if_even, if_odd = (edge(*lines) for lines in edge_lines(rows, True))
    edge_ref[...] = jnp.where(even_stripe(), if_even, if_odd)


def far_kernel(cores, *refs):
    pieces = refs[:cores]
    science_ref, good_ref, edge_ref, ext = refs[cores:]
    rows, half = pieces[0].shape
    me = lax.axis_index("exp")
    for step in range(cores):
        start = lax.rem(me + step, cores) * half
        ext[:, pl.ds(pl.multiple_of(start, LANES), half)] = pieces[step][...]

    def edge(main, extra, outer):
        parts = sides_of(ext[main : main + 8], cores)
        for line in (extra, extra + 1):
            parts += sides_of(ext[line : line + 1], cores)
        for source in (science_ref, good_ref):
            parts += sides_of(source[0, outer : outer + 1, :], cores)
        return jnp.concatenate(parts, axis=0)

    if_even, if_odd = (edge(*lines) for lines in edge_lines(rows, False))
    edge_ref[...] = jnp.where(even_stripe(), if_even, if_odd)


def load_kernel(
    template_hbm,
    science_hbm,
    good_hbm,
    row_hbm,
    col_hbm,
    stamps_hbm,
    template_ref,
    science_ref,
    good_ref,
    row_ref,
    col_ref,
    odd_ref,
    mask_ref,
    stamps_ref,
    sems,
):
    moves = [
        pltpu.make_async_copy(source, target, sems.at[spot])
        for spot, (source, target) in enumerate(
            [
                (science_hbm, science_ref),
                (good_hbm, mask_ref),
                (template_hbm, template_ref),
                (row_hbm, row_ref),
                (col_hbm, col_ref),
                (stamps_hbm, stamps_ref),
            ]
        )
    ]
    for move in moves:
        move.start()
    for move in moves:
        move.wait()
    good_ref[...] = mask_ref[...].astype(F32)
    odd_ref[...] = jnp.concatenate(
        [
            jnp.full((1, LANES), lax.rem(stamps_ref[0, stamp], 2), jnp.int32)
            for stamp in range(odd_ref.shape[0])
        ],
        axis=0,
    )


def weight_kernel(
    row_ref, col_ref, weight_ref, late_ref, base_ref, pad
):
    pad[...] = jnp.zeros_like(pad)
    for spot, source in enumerate((row_ref, col_ref)):
        pad[spot, 0:BASES, 0:TAPS] = source[...]
        pad[spot, SPILL_AT:BASE_PAD, 0:TAPS] = source[ALIGNED:BASES]
    row = pad[0]
    lane = lane_id(BASE_PAD)
    group = lane // GROUP
    tiled = row
    for part in range(1, GROUPS_TILE):
        tiled = tiled + pltpu.roll(row, part * GROUP, 1)
    columns = [
        jnp.broadcast_to(pad[1, :, tap : tap + 1], (BASE_PAD, LANES)) for tap in range(TAPS)
    ]
    zero = jnp.zeros((BASE_PAD, LANES), F32)
    mains = []
    for tile in range(MAIN_TILES):
        spread = zero
        for part in range(GROUPS_TILE):
            tap = tile * GROUPS_TILE + part
            if tap < TAPS:
                spread = jnp.where(group == part, columns[tap], spread)
        mains.append(tiled * spread)
    spread = zero
    for tap in range(TAPS):
        spread = jnp.where(lane // 4 == tap, columns[tap], spread)
    corner = lax.rem(lane, 4)

    def tap_at(tap):
        return jnp.broadcast_to(pad[0, :, tap : tap + 1], (BASE_PAD, LANES))

    outer = jnp.where(
        corner == 0,
        tap_at(0),
        jnp.where(corner == 1, tap_at(1), jnp.where(corner == 2, tap_at(TAPS - 2), tap_at(TAPS - 1))),
    )
    inner = jnp.where(corner == 1, tap_at(0), jnp.where(corner == 2, tap_at(TAPS - 1), 0.0))
    outer = outer * spread
    inner = inner * spread
    for tile, values in enumerate(mains + [outer, inner]):
        base_ref[:, tile * LANES : (tile + 1) * LANES] = jnp.where(
            row_id(BASE_PAD) < BASES, values, 0.0
        )
    rows = weight_ref.shape[0] // (2 * BASE_PAD)
    even = even_stripe()
    first_tap, last_tap = tap_at(0), tap_at(TAPS - 1)

    def column_tile(tap_of):
        spread = zero
        begin = 0
        for end in range(1, LANES + 1):
            if end < LANES and tap_of(end) == tap_of(begin):
                continue
            if tap_of(begin) < TAPS:
                spread = jnp.where((lane >= begin) & (lane < end), columns[tap_of(begin)], spread)
            begin = end
        return spread

    def early_tap(place):
        if place < NEAR_AT:
            return place // 16
        return (place - NEAR_AT) // 8 if place < NEAR_EXTRA_AT else (place - NEAR_EXTRA_AT) // 2

    def late_tap(place):
        return place // 8 if place < FAR_EXTRA_AT else (place - FAR_EXTRA_AT) // 2

    early_tiles = [
        column_tile(lambda spot, tile=tile: early_tap(tile * LANES + spot))
        for tile in range(EARLY // LANES)
    ]
    late_tiles = [
        column_tile(lambda spot, tile=tile: late_tap(tile * LANES + spot))
        for tile in range(LATE // LANES)
    ]

    def repeats(period):
        blocks = []
        for start in range(0, TAPS, period):
            block = pltpu.roll(row, (LANES - start) % LANES, 1) if start else row
            block = jnp.where(lane < period, block, 0.0)
            size = period
            while size < LANES:
                block = block + pltpu.roll(block, size, 1)
                size *= 2
            blocks.append(block)
        return blocks

    def window(blocks, period, first):
        block, move = first // period, first % period
        here = blocks[block] if 0 <= block < len(blocks) else None
        beyond = blocks[block + 1] if 0 <= block + 1 < len(blocks) else None
        if move == 0:
            return zero if here is None else here
        ready = lax.rem(lane, period) < period - move
        parts = [zero if part is None else pltpu.roll(part, LANES - move, 1) for part in (here, beyond)]
        return jnp.where(ready, parts[0], parts[1])

    by_sixteen, by_eight = repeats(16), repeats(8)
    own_rows = [window(by_sixteen, 16, HALF - line) for line in range(rows)]
    top_rows = [window(by_eight, 8, 1 - line) for line in range(rows)]
    bottom_rows = [window(by_eight, 8, rows + HALF - line) for line in range(rows)]

    parity = lax.rem(lane, 2)

    def corner_taps(upper, lower, is_upper):
        top = jnp.where(parity == 1, first_tap, 0.0) if upper else zero
        bottom = jnp.where(parity == 0, last_tap, 0.0) if lower else zero
        return jnp.where(is_upper, top, bottom)

    near_is_top = ~even
    early_rows, late_rows = [], []
    for spot in range(rows):
        odd_line = spot + rows - HALF if spot < HALF else spot - HALF
        own = jnp.where(even, own_rows[spot], own_rows[odd_line])
        side = jnp.where(even, bottom_rows[spot], top_rows[odd_line])
        extra = zero
        if spot >= HALF:
            extra = corner_taps(spot == HALF, spot == rows - 1, near_is_top)
        tiles = [
            own,
            own,
            jnp.where(lane < NEAR_AT - 2 * LANES, own, side),
            jnp.where(lane < NEAR_EXTRA_AT - 3 * LANES, side, extra),
        ]
        early_rows.append(
            jnp.concatenate([mine * tile for mine, tile in zip(tiles, early_tiles)], axis=1)
        )
        if spot < HALF:
            side = jnp.where(even, top_rows[spot], bottom_rows[odd_line])
            extra = corner_taps(spot == 0, spot == HALF - 1, even)
            tiles = [side, jnp.where(lane < FAR_EXTRA_AT - LANES, side, extra)]
            late_rows.append(
                jnp.concatenate([mine * tile for mine, tile in zip(tiles, late_tiles)], axis=1)
            )
    for spot in range(0, rows, 2):
        put_split(weight_ref, spot * BASE_PAD, jnp.concatenate(early_rows[spot : spot + 2], axis=0))
    spare = late_ref.shape[0] // 2 - HALF * BASE_PAD
    late_rows.append(jnp.zeros((spare, LATE), F32))
    put_split(late_ref, 0, jnp.concatenate(late_rows, axis=0))


def edges_of(near_ref, far_ref):
    even = even_stripe()
    near = near_ref[...]
    far = far_ref[...]
    return jnp.where(even, far, near), jnp.where(even, near, far)


def fill_extended(ext, highs, lows, cores, pieces, near_ref, far_ref):
    rows, half = pieces[0].shape
    wide = half * cores
    ext[:, 0:LANES] = jnp.zeros((ext.shape[0], LANES), F32)
    ext[:, LANES + wide :] = jnp.zeros((ext.shape[0], LANES), F32)
    me = lax.axis_index("exp")
    for step in range(cores):
        start = lax.rem(me + step, cores) * half + LANES
        ext[8 : 8 + rows, pl.ds(pl.multiple_of(start, LANES), half)] = pieces[step][...]
    top, bottom = edges_of(near_ref, far_ref)
    for side in range(cores):
        where = pl.ds(LANES + side * half, half)
        ext[0:8, where] = top[8 * side : 8 * side + 8]
        ext[8 + rows : 16 + rows, where] = bottom[8 * side : 8 * side + 8]
        spots = [8 * cores + side, 9 * cores + side]
        spare = [edge[spot : spot + 1] for edge in (top, bottom) for spot in spots]
        ext[16 + rows : 24 + rows, where] = jnp.concatenate(spare + spare, axis=0)
    main = slice(0, GROUP)
    highs[main], lows[main] = split_two(ext[main])
    extra = ext[GROUP : GROUP + 8]
    span = extra.shape[1]
    early = lax.broadcasted_iota(jnp.int32, extra.shape, 0) < 4
    ahead = [extra] + [pltpu.roll(extra, span - part, 1) for part in range(1, 4)]
    lines = jnp.concatenate(
        [jnp.where(early, ahead[0], ahead[1]), jnp.where(early, ahead[2], ahead[3])], axis=0
    )
    highs[GROUP:], lows[GROUP:] = split_two(lines)


def spread_window(shifted, put):
    for tap in range(TAPS):
        put(tap * GROUP, shifted(tap, slice(0, GROUP)))
    for quad in range(MAIN_TILES):
        put(MAIN + 16 * quad, shifted(4 * quad, slice(GROUP, GROUP + 16)))


def clear_spare(refs):
    for ref in refs:
        wide = ref.shape[1]
        ref[TAPS * GROUP : MAIN] = jnp.zeros((MAIN - TAPS * GROUP, wide), BF16)
        ref[MAIN + EXTRA_ROWS :] = jnp.zeros((LANES - EXTRA_ROWS, wide), BF16)


def back_profile(horiz):
    steady = jnp.ones_like(horiz)
    square = 0.5 * (3.0 * horiz * horiz - 1.0)
    return [steady, horiz, steady, horiz, square, steady, horiz]


def put_sides(target, edge_ref):
    fold = edge_ref.shape[1]
    cores = edge_ref.shape[0] // (REACH + 2)
    for side in range(cores):
        where = pl.ds(LANES + side * fold, fold)
        target[0:8, where] = edge_ref[8 * side : 8 * side + 8]
        for line in range(2):
            spot = (8 + line) * cores + side
            target[8 + line : 9 + line, where] = edge_ref[spot : spot + 1]


def paired(values):
    span = values.shape[1]
    return jnp.concatenate([values, pltpu.roll(values, span - 1, 1)], axis=0)


def corner_block(lines):
    span = lines.shape[1]
    parts = [lines] + [pltpu.roll(lines, span - move, 1) for move in range(1, 8)]
    return jnp.concatenate(parts, axis=0)


def odd_rows(odd_ref, stamp, height):
    return jnp.broadcast_to(odd_ref[stamp : stamp + 1, :] == 1, (height, LANES))


def stamp_window(source, odd_ref, stamp, offset):
    height = source.shape[0]
    lane = lane_id(height)
    left = source[:, stamp * LANES : (stamp + 1) * LANES]
    centre = source[:, (stamp + 1) * LANES : (stamp + 2) * LANES]
    right = source[:, (stamp + 2) * LANES : (stamp + 3) * LANES]
    odd = jnp.where(lane < LANES // 4, right, centre)
    even = jnp.where(lane >= LANES - HALF, left, centre)
    odd = pltpu.roll(odd, (HALF + STAMP_W + offset) % LANES, 1)
    even = pltpu.roll(even, HALF + offset, 1)
    return jnp.where(odd_rows(odd_ref, stamp, height), odd, even)


def stamp_values(sources, odd_ref, pair, moves):
    out = []
    for source in sources:
        first = stamp_window(source, odd_ref, 2 * pair, 0)
        second = stamp_window(source, odd_ref, 2 * pair + 1, STAMP_W)
        tiles = []
        for tile, move in moves:
            a, b = first[16 * tile : 16 * tile + 16], second[16 * tile : 16 * tile + 16]
            if move:
                a = pltpu.roll(a, LANES - move, 1)
                b = pltpu.roll(b, LANES - move, 1)
            tiles.append(jnp.where(lane_id(16) < STAMP_W, a, b))
        out.append(jnp.concatenate(tiles, axis=0))
    return out


def three_products(weights, xhigh, xlow):
    rows = weights.shape[0] // 2
    both = jnp.dot(weights, xhigh, preferred_element_type=F32)
    return both[:rows] + (
        both[rows:] + jnp.dot(weights[:rows], xlow, preferred_element_type=F32)
    )


def back_rows(rows):
    empty = jnp.zeros_like(rows[0])
    lead = [empty] * (8 - BACK_FIRST)
    second = lead + rows[BACK_FIRST:]
    second += [empty] * (8 - len(second))
    return [jnp.concatenate(part, axis=0) for part in (lead + rows[:BACK_FIRST], second)]


def design_line(bases, keep, target, horiz, profiles, row, region_rows):
    own = bases * keep
    vert = position(jnp.full(horiz.shape, row, jnp.int32), region_rows)
    square = 0.5 * (3.0 * vert * vert - 1.0)
    steady = jnp.ones_like(vert)
    scales = back_rows([steady, steady, vert, vert, steady, square, square])
    first, second = (profile * scale * keep for profile, scale in zip(profiles, scales))
    spot = lax.broadcasted_iota(jnp.int32, second.shape, 0)
    sloped = own * horiz
    tilted = own * vert
    mixed = jnp.where(spot < SPILL_AT - ALIGNED, second, tilted[ALIGNED:])
    return jnp.concatenate(
        [
            own[:ALIGNED],
            jnp.where(spot < SPILL, own[ALIGNED:], first),
            sloped[:ALIGNED],
            jnp.where(spot < SPILL, sloped[ALIGNED:], mixed),
            tilted[:ALIGNED],
            jnp.where(spot == 0, target, 0.0),
        ],
        axis=0,
    )


def gram(lines):
    design = jnp.concatenate([line.astype(BF16) for line in lines], axis=1)
    return lax.dot_general(design, design, (((1,), (1,)), ((), ())), preferred_element_type=F32)


def early_kernel(cores, stripes, *refs):
    pieces = refs[:cores]
    near_pieces = refs[cores : 2 * cores]
    (
        science_ref,
        good_ref,
        odd_ref,
        weight_ref,
        total_ref,
        late_ref,
        aux_ref,
        near_ref,
        ext,
        highs,
        lows,
        bases,
    ) = refs[2 * cores :]
    rows, half = pieces[0].shape
    wide = science_ref.shape[2]
    pairs = wide // (4 * STAMP_W)
    me = lax.axis_index("exp")
    ext[:, 0:LANES] = jnp.zeros((ext.shape[0], LANES), F32)
    ext[:, LANES + wide :] = jnp.zeros((ext.shape[0], LANES), F32)
    for step in range(cores):
        side = lax.rem(me + step, cores)
        where = pl.ds(pl.multiple_of(side * half + LANES, LANES), half)
        ext[0:rows, where] = pieces[step][...]
        edge = near_pieces[step][...]
        ext[rows : rows + REACH, where] = edge[:REACH]
        near_ref[pl.ds(pl.multiple_of(8 * side, 8), 8), :] = edge[:8]
        for line in range(2):
            near_ref[pl.ds((8 + line) * cores + side, 1), :] = edge[8 + line : 9 + line]
    near_ref[REACH * cores :] = near_pieces[0][REACH : REACH + 2 * cores]
    lines = jnp.concatenate(
        [ext[0:rows], paired(ext[rows : rows + 8]), corner_block(ext[rows + 8 : rows + 10])], axis=0
    )
    highs[...], lows[...] = split_two(lines)
    moves = [(0, tap) for tap in range(TAPS)]
    moves += [(1, 2 * step) for step in range(10)]
    moves += [(2, 8 * step) for step in range(3)]
    lane = lane_id(1)
    for pair in range(pairs):
        columns = slice(pair * LANES, (pair + 1) * LANES)
        odd = jnp.where(
            lane < STAMP_W,
            odd_ref[2 * pair : 2 * pair + 1],
            odd_ref[2 * pair + 1 : 2 * pair + 2] + 1,
        )
        horiz = position(4 * pair * STAMP_W + odd * STAMP_W + lane, wide)
        aux_ref[2 * rows : 2 * rows + 8, columns] = jnp.broadcast_to(horiz, (8, LANES))
        picked = []
        for source in (good_ref, science_ref):
            lower = source[0, :, 2 * pair * LANES : (2 * pair + 1) * LANES]
            upper = source[0, :, (2 * pair + 1) * LANES : (2 * pair + 2) * LANES]
            lower = jnp.where(
                odd_rows(odd_ref, 2 * pair, rows), pltpu.roll(lower, STAMP_W, 1), lower
            )
            upper = jnp.where(
                odd_rows(odd_ref, 2 * pair + 1, rows), upper, pltpu.roll(upper, STAMP_W, 1)
            )
            picked.append(jnp.where(lane_id(rows) < STAMP_W, lower, upper))
        aux_ref[0:rows, columns] = picked[0]
        aux_ref[rows : 2 * rows, columns] = picked[0] * picked[1]
    split = HALF * BASE_PAD
    chunk = 2 * LANES
    for start in range(0, wide // 2, chunk):
        span = slice(start, start + chunk)
        made = [
            stamp_values((highs, lows), odd_ref, pair, moves)
            for pair in range(start // LANES, (start + chunk) // LANES)
        ]
        values = three_products(
            weight_ref[...],
            *(jnp.concatenate([one[side] for one in made], axis=1) for side in range(2)),
        )
        late_ref[:, span] = values[:split]
        bases[:, span] = values[split:]
    horiz = aux_ref[2 * rows : 2 * rows + 1]
    profile = back_rows(back_profile(horiz))
    first_line = jnp.where(even_stripe(), HALF, 0)
    first_row = lax.axis_index("stripe") * rows
    designs = []
    for spot in range(rows - HALF):
        line = first_line + spot
        designs.append(design_line(
            bases[spot * BASE_PAD : (spot + 1) * BASE_PAD],
            aux_ref[pl.ds(line, 1), :],
            aux_ref[pl.ds(rows + line, 1), :],
            horiz,
            profile,
            first_row + line,
            rows * stripes,
        ))
    total = gram(designs)
    total_ref[...] = jnp.concatenate(
        [total, jnp.zeros((FIT_ROWS, LANES - FIT_ROWS), F32)], axis=1
    )


def late_kernel(stripes, rows, *refs):
    (
        far_ref,
        odd_ref,
        weight_ref,
        total_ref,
        early_ref,
        aux_ref,
        out_ref,
        ext,
        highs,
        lows,
        bases,
    ) = refs
    width = early_ref.shape[1]
    pairs = width // LANES
    ext[:, 0:LANES] = jnp.zeros((ext.shape[0], LANES), F32)
    ext[:, ext.shape[1] - LANES :] = jnp.zeros((ext.shape[0], LANES), F32)
    put_sides(ext, far_ref)
    lines = jnp.concatenate([paired(ext[0:8]), corner_block(ext[8:10])], axis=0)
    highs[...], lows[...] = split_two(lines)
    moves = [(0, 2 * step) for step in range(10)] + [(1, 8 * step) for step in range(3)]
    used = 16 * len(moves)
    split = HALF * BASE_PAD
    chunk = 4 * LANES
    for start in range(0, width, chunk):
        span = slice(start, start + chunk)
        made = [
            stamp_values((highs, lows), odd_ref, pair, moves)
            for pair in range(start // LANES, (start + chunk) // LANES)
        ]
        spare = jnp.zeros((LATE - used, chunk), BF16)
        xh, xl = (
            jnp.concatenate([jnp.concatenate([one[side] for one in made], axis=1), spare], axis=0)
            for side in range(2)
        )
        values = three_products(weight_ref[...], xh, xl)
        bases[:, span] = early_ref[:, span] + values[:split]
    horiz = aux_ref[2 * rows : 2 * rows + 1]
    profile = back_rows(back_profile(horiz))
    first_line = jnp.where(even_stripe(), 0, rows - HALF)
    first_row = lax.axis_index("stripe") * rows
    designs = []
    for spot in range(HALF):
        line = first_line + spot
        designs.append(
            design_line(
                bases[spot * BASE_PAD : (spot + 1) * BASE_PAD],
                aux_ref[pl.ds(line, 1), :],
                aux_ref[pl.ds(rows + line, 1), :],
                horiz,
                profile,
                first_row + line,
                rows * stripes,
            )
        )
    own = total_ref[:, :FIT_ROWS] + gram(designs)
    out_ref[...] = packed_normal(own)


def packed_normal(normal):
    half = UNKNOWNS // 2
    lane = lane_id(8)
    right = jnp.zeros((8, LANES), F32)
    for tile in range(UNKNOWNS // 8):
        column = normal[8 * tile : 8 * tile + 8, UNKNOWNS : UNKNOWNS + 1]
        right = jnp.where(lane == tile, jnp.broadcast_to(column, (8, LANES)), right)
    both = [normal[:half, :UNKNOWNS], normal[half:UNKNOWNS, :UNKNOWNS]]
    return jnp.concatenate([jnp.concatenate(both, axis=1), right], axis=0)


def unpacked_normal(packed):
    half = UNKNOWNS // 2
    lane = lane_id(UNKNOWNS)
    values = jnp.concatenate([packed[:half], pltpu.roll(packed[:half], UNKNOWNS, 1)], axis=0)
    right = jnp.concatenate(
        [
            jnp.broadcast_to(packed[half:, tile : tile + 1], (8, LANES))
            for tile in range(UNKNOWNS // 8)
        ],
        axis=0,
    )
    return jnp.where(lane < UNKNOWNS, values, jnp.where(lane == UNKNOWNS, right, 0.0))


def tree_sum(values):
    while len(values) > 1:
        values = [sum(values[spot : spot + 2][1:], values[spot]) for spot in range(0, len(values), 2)]
    return values[0]


def solve_rows(matrix):
    sub = row_id(8)
    tiles = [matrix[start : start + 8] for start in range(0, UNKNOWNS, 8)]
    order = [(start, 8) for start in range(0, UNKNOWNS, 8)]

    def spread(tile, spot):
        return jnp.broadcast_to(tile[spot : spot + 1], (8, LANES))

    def column(tile, spot):
        return jnp.broadcast_to(tile[:, spot : spot + 1], (8, LANES))

    start, size = order[0]
    corner = [column(tiles[start // 8], start + j) for j in range(size)]
    for step, (start, size) in enumerate(order):
        home = start // 8
        columns = [
            [None if place == home else column(tile, start + j) for place, tile in enumerate(tiles)]
            for j in range(size)
        ]
        rows = tiles[home]
        following = order[step + 1] if step + 1 < len(order) else (0, 0)
        next_home = following[0] // 8
        ahead = [column(rows, following[0] + j) for j in range(following[1])]
        below = [column(tiles[next_home], following[0] + j) for j in range(following[1])]
        for spot in range(size):
            keep = sub == spot
            inverse = 1.0 / spread(corner[spot], spot)
            others = jnp.where(keep, 0.0, corner[spot])

            def eliminated(values):
                scaled = spread(values, spot) * inverse
                return jnp.where(keep, scaled, values - others * scaled)

            corner = [
                eliminated(values) if j > spot else values for j, values in enumerate(corner)
            ]
            ahead = [eliminated(values) for values in ahead]
            rows = eliminated(rows)
        if following[1]:
            corner = [
                values - tree_sum([columns[i][next_home] * spread(ahead[j], i) for i in range(size)])
                for j, values in enumerate(below)
            ]
        for place in range(len(tiles)):
            if place == home:
                tiles[place] = rows
            else:
                tiles[place] = tiles[place] - tree_sum(
                    [columns[i][place] * spread(rows, i) for i in range(size)]
                )
    right = jnp.concatenate(tiles, axis=0)[:, UNKNOWNS : UNKNOWNS + 1]
    return jnp.broadcast_to(right, (UNKNOWNS, LANES))


def region_weights(base_ref, weight_ref, rows):
    lane = lane_id(8)
    spot = lax.rem(lane, GROUP)
    corner = lax.rem(lane, 4)
    line = row_id(8)
    mains = [base_ref[:, tile * LANES : (tile + 1) * LANES] for tile in range(MAIN_TILES)]
    outer = base_ref[:, MAIN : MAIN + LANES]
    inner = base_ref[:, MAIN + LANES :]
    blocks = [[] for _ in range(BASES)]
    for start in range(0, rows, 8):
        tap = spot - (start + line - 1)
        inside = (tap >= 0) & (tap < TAPS)
        moved = [pltpu.roll(main, (start - 1) % LANES, 1) for main in mains]
        extra = zero_row = jnp.zeros((8, LANES), F32)
        for b in range(BASES):
            tiles = []
            for main in moved:
                wide = jnp.broadcast_to(main[b : b + 1], (8, LANES))
                tiles.append(
                    jnp.where(inside, pltpu.roll(wide, 0, 1, stride=1, stride_axis=0), 0.0)
                )
            extra = zero_row
            mine = jnp.broadcast_to(inner[b : b + 1], (8, LANES))
            if start == 0:
                extra = jnp.where((line == 0) & (corner < 2), mine, extra)
            if start == rows - 8:
                extra = jnp.where((line == 7) & (corner >= 2), mine, extra)
            blocks[b].append(jnp.concatenate(tiles + [extra], axis=1))
    for b in range(BASES):
        put_split(weight_ref, b * rows, jnp.concatenate(blocks[b], axis=0))
    lane = lane_id(BASE_PAD)
    spot = lax.rem(lane, GROUP)
    corner = lax.rem(lane, 4)
    halos = []
    for shift, extra in ((rows - 1, corner >= 2), (-2, corner < 2)):
        tap = spot - shift
        inside = (tap >= 0) & (tap < TAPS)
        tiles = [jnp.where(inside, pltpu.roll(main, shift % LANES, 1), 0.0) for main in mains]
        halos.append(jnp.concatenate(tiles + [jnp.where(extra, outer, 0.0)], axis=1))
    put_split(weight_ref, BASES * rows, jnp.concatenate(halos, axis=0))


def region_bases(highs, lows, weight_ref, first, out_ref, scratch):
    wide = out_ref.shape[1]
    chunk = scratch[0].shape[1]
    for spot, start in enumerate(range(0, wide, chunk)):
        targets = scratch[2 * spot : 2 * spot + 2]
        clear_spare(targets)
        for source, target in zip((highs, lows), targets):

            def shifted(tap, lines):
                begin = first + start + LANES - HALF + tap
                return source[lines, begin : begin + chunk]

            def put(place, values):
                target[place : place + values.shape[0]] = values

            spread_window(shifted, put)
        out_ref[:, start : start + chunk] = three_products(
            weight_ref[...], targets[0][...], targets[1][...]
        )


def first_bases_kernel(cores, *refs):
    pieces = refs[:cores]
    (
        far_ref,
        near_ref,
        base_ref,
        after_ref,
        weight_ref,
        highs,
        lows,
        out_ref,
        ext,
        *scratch,
    ) = refs[cores:]
    region_weights(base_ref, weight_ref, pieces[0].shape[0])
    fill_extended(ext, highs, lows, cores, pieces, near_ref, far_ref)
    region_bases(highs, lows, weight_ref, 0, out_ref, scratch)


def next_bases_kernel(first, highs, lows, weight_ref, after_ref, out_ref, *scratch):
    region_bases(highs, lows, weight_ref, first, out_ref, scratch)


def add_kernel(count, *refs):
    values = [ref[...] for ref in refs[:count]]
    if count == 4:
        order = (1, 2, 0)
        values = [values[0]] + [values[1 + order.index(k)] for k in range(3)]
    refs[-1][...] = tree_sum(values)


def model_kernel(stripes, normal_ref, *refs):
    far_ref, near_ref, science_ref, good_ref, out_ref, coef_ref = refs[-6:]
    parts = refs[:-6]
    rows = science_ref.shape[1]
    wide = science_ref.shape[2]
    top, bottom = edges_of(near_ref, far_ref)
    coef = solve_rows(unpacked_normal(normal_ref[...]))
    lane = lane_id(UNKNOWNS)
    base, term = lane // 3, lax.rem(lane, 3)
    tilt = jnp.where(base < ALIGNED, 2 * BASE_PAD, BASE_PAD + SPILL_AT - ALIGNED) + base
    home = lane - 3 * BASES + jnp.where(lane < 3 * BASES + BACK_FIRST, BASES, BASE_PAD + BASES - BACK_FIRST)
    home = jnp.where(lane < 3 * BASES, jnp.where(term == 2, tilt, term * BASE_PAD + base), home)
    flat = jnp.sum(jnp.where(row_id(UNKNOWNS) == home, coef, 0.0), axis=0, keepdims=True)
    coef_ref[...] = flat[:, : coef_ref.shape[1]]

    def share(spot, height):
        return jnp.broadcast_to(coef[spot : spot + 1], (height, LANES))

    first_row = lax.axis_index("stripe") * rows
    vert = position(first_row + row_id(rows), rows * stripes)
    halo_vert = [
        position(jnp.full((8, LANES), first_row + line, jnp.int32), rows * stripes)
        for line in (rows, -1)
    ]
    tilts = [
        2 * BASE_PAD + b if b < ALIGNED else BASE_PAD + SPILL_AT + b - ALIGNED for b in range(BASES)
    ]
    slopes = [share(spot, rows) * vert for spot in tilts]
    tilted = jnp.concatenate(
        [
            coef[2 * BASE_PAD :],
            coef[BASE_PAD + SPILL_AT : 2 * BASE_PAD],
            jnp.zeros((BACK_FIRST, LANES), F32),
        ],
        axis=0,
    )
    halo_slopes = [tilted * jnp.concatenate([line] * 3, axis=0) for line in halo_vert]
    level = [
        share(BASES + m + (0 if m < BACK_FIRST else BASE_PAD - BACK_FIRST), 8) for m in range(BACK)
    ]

    def ground(here, horiz):
        square = 0.5 * (3.0 * here * here - 1.0)
        horiz_square = 0.5 * (3.0 * horiz * horiz - 1.0)
        steady = level[0] + level[1] * horiz + level[4] * horiz_square
        sloped = level[2] + level[3] * horiz
        curved = level[5] + level[6] * horiz
        if here.shape[0] > 8:
            steady, sloped, curved = (
                jnp.concatenate([part] * (here.shape[0] // 8), axis=0)
                for part in (steady, sloped, curved)
            )
        return steady + here * sloped + square * curved

    models, halos = [], [[], []]
    for part in parts:
        for start in range(0, part.shape[1], LANES):
            span = slice(start, start + LANES)
            begin = len(models) * LANES
            horiz = position(begin + lane_id(8), wide)
            total = ground(vert, horiz)
            for b in range(BASES):
                steady = share(b, 8) + share(BASE_PAD + b, 8) * horiz
                scale = jnp.concatenate([steady] * (rows // 8), axis=0) + slopes[b]
                total = total + part[b * rows : (b + 1) * rows, span] * scale
            models.append(total)
            steady = coef[:BASE_PAD] + coef[BASE_PAD : 2 * BASE_PAD] * horiz[0:1]
            for side in range(2):
                place = BASES * rows + side * BASE_PAD
                values = part[place : place + BASE_PAD, span] * (steady + halo_slopes[side])
                values = jnp.sum(values, axis=0, keepdims=True)
                halos[side].append(values + ground(halo_vert[side], horiz)[0:1])
    model = jnp.concatenate(models, axis=1)
    below_model, above_model = (jnp.concatenate(side, axis=1) for side in halos)
    own = good_ref[0] * (science_ref[0] - model)

    def halo(edge, values):
        cores = edge.shape[0] // (REACH + 2)
        science, good = (
            jnp.concatenate(
                [edge[spot : spot + 1] for spot in range(start * cores, (start + 1) * cores)], axis=1
            )
            for start in (REACH, REACH + 1)
        )
        return good * (science - values)

    above_row = halo(top, above_model)
    below_row = halo(bottom, below_model)
    lines = lax.broadcasted_iota(jnp.int32, (rows, wide), 0)
    spots = lax.broadcasted_iota(jnp.int32, (rows, wide), 1)
    above = jnp.where(lines == 0, above_row, pltpu.roll(own, 1, 0))
    below = jnp.where(lines == rows - 1, below_row, pltpu.roll(own, rows - 1, 0))
    before = jnp.where(spots == 0, 0.0, pltpu.roll(own, 1, 1))
    after = jnp.where(spots == wide - 1, 0.0, pltpu.roll(own, wide - 1, 1))
    out_ref[0] = 4.0 * own - (below + above + after + before)


def whole_vmem(count):
    return [pl.BlockSpec(memory_space=pltpu.VMEM)] * count


def add(values, after, params):
    return pl.pallas_call(
        functools.partial(add_kernel, len(values)),
        out_shape=jax.ShapeDtypeStruct(values[0].shape, values[0].dtype),
        in_specs=whole_vmem(len(values) + len(after)),
        out_specs=pl.BlockSpec(memory_space=pltpu.VMEM),
        compiler_params=params,
        name="add",
    )(*values, *after)


def summed(values, axis, beside, params):
    count = lax.axis_size(axis)
    if count & (count - 1):
        for works in beside:
            for work in works:
                work(values)
        return lax.psum(values, axis)
    rounds = [(1, 2, 3)] if count >= 4 else []
    step = 4 if rounds else 1
    while step < count:
        rounds.append((step,))
        step *= 2
    rounds += [()] * (len(beside) - len(rounds))
    for spot, steps in enumerate(rounds):
        others = [
            lax.ppermute(values, axis, [(i, i ^ step) for i in range(count)]) for step in steps
        ]
        after = [work(values) for work in beside[spot]] if spot < len(beside) else []
        if steps:
            if len(others) == 3:
                others = [others[k] for k in (1, 2, 0)]
            values = add([values] + others, after, params)
    return values


def shared_pieces(values, cores):
    return [
        lax.ppermute(values, "exp", [((i + step) % cores, i) for i in range(cores)])
        for step in range(1, cores)
    ]


def shards(template, exposure, cosmic_mask, stamp_blocks, row_filters, col_filters):
    arguments = (template, exposure, cosmic_mask, row_filters, col_filters, stamp_blocks)
    rows, half = template.shape
    wide = exposure.shape[2]
    cores = lax.axis_size("exp")
    stripes = lax.axis_size("stripe")
    params = pltpu.CompilerParams(vmem_limit_bytes=24 * 1024 * 1024)
    pieces = [template] + shared_pieces(template, cores)
    stamps = stamp_blocks.shape[1]
    template_in, science, good, row_in, col_in, odd = pl.pallas_call(
        load_kernel,
        out_shape=(
            jax.ShapeDtypeStruct(template.shape, F32),
            jax.ShapeDtypeStruct(exposure.shape, F32),
            jax.ShapeDtypeStruct(exposure.shape, F32),
            jax.ShapeDtypeStruct(row_filters.shape, F32),
            jax.ShapeDtypeStruct(col_filters.shape, F32),
            jax.ShapeDtypeStruct((stamps, LANES), jnp.int32),
        ),
        in_specs=[pl.BlockSpec(memory_space=pltpu.HBM)] * 6,
        out_specs=tuple(whole_vmem(6)),
        scratch_shapes=[
            pltpu.VMEM(cosmic_mask.shape, jnp.int32),
            pltpu.SMEM(stamp_blocks.shape, jnp.int32),
            pltpu.SemaphoreType.DMA((6,)),
        ],
        compiler_params=params,
        name="load",
    )(*[pltpu.with_memory_space_constraint(array, pltpu.HBM) for array in arguments])
    pieces = [template_in] + pieces[1:]
    near_pairs = [(i, i + 1) for i in range(0, stripes - 1, 2)]
    far_pairs = [(i, i + 1) for i in range(1, stripes - 1, 2)]

    def swapped(values, couples):
        return lax.ppermute(values, "stripe", couples + [(b, a) for a, b in couples])

    near = pl.pallas_call(
        functools.partial(near_kernel, cores),
        out_shape=jax.ShapeDtypeStruct((-(-(REACH + 2 * cores) // 8) * 8, half), F32),
        in_specs=whole_vmem(3),
        out_specs=pl.BlockSpec(memory_space=pltpu.VMEM),
        compiler_params=params,
        name="near",
    )(template_in, science, good)
    near = swapped(near, near_pairs)
    near_pieces = [near] + shared_pieces(near, cores)
    edge_shape = jax.ShapeDtypeStruct(((REACH + 2) * cores, half), F32)
    far = pl.pallas_call(
        functools.partial(far_kernel, cores),
        out_shape=edge_shape,
        in_specs=whole_vmem(cores + 2),
        out_specs=pl.BlockSpec(memory_space=pltpu.VMEM),
        scratch_shapes=[pltpu.VMEM((rows, wide), F32)],
        compiler_params=params,
        name="far",
    )(*pieces, science, good)
    far = swapped(far, far_pairs)
    early_shape = jax.ShapeDtypeStruct((2 * rows * BASE_PAD, EARLY), BF16)
    late_shape = jax.ShapeDtypeStruct((2 * LATE_ROWS, LATE), BF16)
    early_weights, late_weights, base = pl.pallas_call(
        weight_kernel,
        out_shape=(
            early_shape,
            late_shape,
            jax.ShapeDtypeStruct((BASE_PAD, DEPTH + LANES), F32),
        ),
        in_specs=whole_vmem(2),
        out_specs=tuple(whole_vmem(3)),
        scratch_shapes=[pltpu.VMEM((2, BASE_PAD, LANES), F32)],
        compiler_params=params,
        name="weights",
    )(row_in, col_in)
    width = wide // 2
    reach = wide + 2 * LANES
    normal_shape = jax.ShapeDtypeStruct((FIT_ROWS, LANES), F32)
    part, kept, aux, near = pl.pallas_call(
        functools.partial(early_kernel, cores, stripes),
        out_shape=(
            normal_shape,
            jax.ShapeDtypeStruct((HALF * BASE_PAD, width), F32),
            jax.ShapeDtypeStruct((2 * rows + 8, width), F32),
            edge_shape,
        ),
        in_specs=whole_vmem(2 * cores + 4),
        out_specs=tuple(whole_vmem(4)),
        scratch_shapes=[
            pltpu.VMEM((rows + 16, reach), F32),
            pltpu.VMEM((rows + 32, reach), BF16),
            pltpu.VMEM((rows + 32, reach), BF16),
            pltpu.VMEM(((rows - HALF) * BASE_PAD, width), F32),
        ],
        compiler_params=params,
        name="early",
    )(*pieces, *near_pieces, science, good, odd, early_weights)
    normal = pl.pallas_call(
        functools.partial(late_kernel, stripes, rows),
        out_shape=jax.ShapeDtypeStruct((UNKNOWNS // 2 + 8, LANES), F32),
        in_specs=whole_vmem(6),
        out_specs=pl.BlockSpec(memory_space=pltpu.VMEM),
        scratch_shapes=[
            pltpu.VMEM((16, reach), F32),
            pltpu.VMEM((32, reach), BF16),
            pltpu.VMEM((32, reach), BF16),
            pltpu.VMEM((HALF * BASE_PAD, width), F32),
        ],
        compiler_params=params,
        name="late",
    )(far, odd, late_weights, part, kept, aux)
    region_rows = BASES * rows + 2 * BASE_PAD
    blocks = wide // (2 * LANES)
    cuts = [blocks * cut // 8 * 2 * LANES for cut in (0, 2, 4, 8)]
    weight_shape = jax.ShapeDtypeStruct((2 * region_rows, DEPTH), BF16)
    source_shape = jax.ShapeDtypeStruct((GROUP + 16, reach), BF16)
    parts, shared = [], []

    def shift_scratch(size):
        chunk = 2 * LANES
        return [pltpu.VMEM((DEPTH, chunk), BF16)] * (2 * (size // chunk))

    def first_bases(after):
        size = cuts[1]
        *made, part = pl.pallas_call(
            functools.partial(first_bases_kernel, cores),
            out_shape=(
                weight_shape,
                source_shape,
                source_shape,
                jax.ShapeDtypeStruct((region_rows, size), F32),
            ),
            in_specs=whole_vmem(cores + 4),
            out_specs=tuple(whole_vmem(4)),
            scratch_shapes=[pltpu.VMEM((rows + 24, reach), F32)] + shift_scratch(size),
            compiler_params=params,
            name="bases",
        )(*pieces, far, near, base, after)
        shared.extend(made)
        parts.append(part)
        return part

    def next_bases(cut, after):
        size = cuts[cut + 1] - cuts[cut]
        region_weight, highs, lows = shared
        part = pl.pallas_call(
            functools.partial(next_bases_kernel, cuts[cut]),
            out_shape=jax.ShapeDtypeStruct((region_rows, size), F32),
            in_specs=whole_vmem(4),
            out_specs=pl.BlockSpec(memory_space=pltpu.VMEM),
            scratch_shapes=shift_scratch(size),
            compiler_params=params,
            name="bases",
        )(highs, lows, region_weight, after)
        parts.append(part)
        return part

    beside = [[first_bases, functools.partial(next_bases, 1)], [functools.partial(next_bases, 2)]]
    normal = summed(normal, "stripe", beside, params)
    filtered, coef = pl.pallas_call(
        functools.partial(model_kernel, stripes),
        out_shape=(
            jax.ShapeDtypeStruct(exposure.shape, F32),
            jax.ShapeDtypeStruct((1, 3 * BASES + BACK), F32),
        ),
        in_specs=whole_vmem(1 + len(parts) + 4),
        out_specs=tuple(whole_vmem(2)),
        compiler_params=params,
        name="model",
    )(normal, *parts, far, near, science, good)
    return filtered, coef


def solution(mesh):
    placed = (
        P(("groups", "stripe"), "exp"),
        P(("groups", "exp"), "stripe", None),
        P(("groups", "exp"), "stripe", None),
        P(("groups", "stripe"), None),
        P(),
        P(),
    )
    return jax.shard_map(
        shards,
        mesh=mesh,
        in_specs=placed,
        out_specs=(P(("groups", "exp"), "stripe", None), P(("groups", "exp"), None)),
        check_vma=False,
    )
```

```python
import functools

import jax
import jax.numpy as jnp
from jax import lax
from jax.experimental import pallas as pl
from jax.experimental.pallas import tpu as pltpu
from jax.sharding import PartitionSpec as P

HALF = 9
TAPS = 2 * HALF + 1
BASES = 19
STAMP_W = 64
LANES = 128
BASE_PAD = 24
BACK = 7
BACK_FIRST = BASE_PAD - BASES
ALIGNED = BASES // 8 * 8
SPILL = BASES - ALIGNED
SPILL_AT = BASE_PAD - SPILL
UNKNOWNS = 2 * BASE_PAD + ALIGNED
FIT_ROWS = UNKNOWNS + 8
REACH = HALF + 1
GROUP = 32
GROUPS_TILE = LANES // GROUP
MAIN_TILES = 5
MAIN = MAIN_TILES * LANES
DEPTH = MAIN + LANES
EXTRA_ROWS = 80
NEAR_AT = TAPS * 16
NEAR_EXTRA_AT = NEAR_AT + 160
EARLY = NEAR_EXTRA_AT + 48
FAR_EXTRA_AT = 160
LATE = 2 * LANES
LATE_ROWS = -(-HALF * BASE_PAD // 16) * 16
F32 = jnp.float32
BF16 = jnp.bfloat16


def lane_id(rows):
    return lax.broadcasted_iota(jnp.int32, (rows, LANES), 1)


def row_id(rows):
    return lax.broadcasted_iota(jnp.int32, (rows, LANES), 0)


def split_two(values):
    high = values.astype(BF16)
    low = (values - high.astype(F32)).astype(BF16)
    return high, low


def put_split(target, start, values):
    size = values.shape[0]
    gap = target.shape[0] // 2
    target[start : start + size], target[gap + start : gap + start + size] = split_two(values)


def position(index, total):
    return (2.0 * index.astype(F32) + 1.0) / total - 1.0


def even_stripe():
    return lax.rem(lax.axis_index("stripe"), 2) == 0


def edge_lines(rows, toward_near):
    last = (rows - 8, rows - REACH, rows - 1)
    first = (0, 8, 0)
    return (last, first) if toward_near else (first, last)


def sides_of(line, cores):
    fold = line.shape[1] // cores
    return [line[:, side * fold : (side + 1) * fold] for side in range(cores)]


def near_kernel(cores, template_ref, science_ref, good_ref, edge_ref):
    rows = template_ref.shape[0]

    def edge(main, extra, outer):
        parts = [template_ref[main : main + 8], template_ref[extra : extra + 2]]
        for source in (science_ref, good_ref):
            parts += sides_of(source[0, outer : outer + 1, :], cores)
        spare = edge_ref.shape[0] - REACH - 2 * cores
        return jnp.concatenate(parts + [jnp.zeros((spare, edge_ref.shape[1]), F32)], axis=0)

    if_even, if_odd = (edge(*lines) for lines in edge_lines(rows, True))
    edge_ref[...] = jnp.where(even_stripe(), if_even, if_odd)


def far_kernel(cores, *refs):
    pieces = refs[:cores]
    science_ref, good_ref, edge_ref, ext = refs[cores:]
    rows, half = pieces[0].shape
    me = lax.axis_index("exp")
    for step in range(cores):
        start = lax.rem(me + step, cores) * half
        ext[:, pl.ds(pl.multiple_of(start, LANES), half)] = pieces[step][...]

    def edge(main, extra, outer):
        parts = sides_of(ext[main : main + 8], cores)
        for line in (extra, extra + 1):
            parts += sides_of(ext[line : line + 1], cores)
        for source in (science_ref, good_ref):
            parts += sides_of(source[0, outer : outer + 1, :], cores)
        return jnp.concatenate(parts, axis=0)

    if_even, if_odd = (edge(*lines) for lines in edge_lines(rows, False))
    edge_ref[...] = jnp.where(even_stripe(), if_even, if_odd)


def load_kernel(
    template_hbm,
    science_hbm,
    good_hbm,
    row_hbm,
    col_hbm,
    stamps_hbm,
    template_ref,
    science_ref,
    good_ref,
    row_ref,
    col_ref,
    odd_ref,
    mask_ref,
    stamps_ref,
    sems,
):
    moves = [
        pltpu.make_async_copy(source, target, sems.at[spot])
        for spot, (source, target) in enumerate(
            [
                (science_hbm, science_ref),
                (good_hbm, mask_ref),
                (template_hbm, template_ref),
                (row_hbm, row_ref),
                (col_hbm, col_ref),
                (stamps_hbm, stamps_ref),
            ]
        )
    ]
    for move in moves:
        move.start()
    for move in moves:
        move.wait()
    good_ref[...] = mask_ref[...].astype(F32)
    odd_ref[...] = jnp.concatenate(
        [
            jnp.full((1, LANES), lax.rem(stamps_ref[0, stamp], 2), jnp.int32)
            for stamp in range(odd_ref.shape[0])
        ],
        axis=0,
    )


def weight_kernel(
    row_ref, col_ref, weight_ref, late_ref, base_ref, pad
):
    pad[...] = jnp.zeros_like(pad)
    for spot, source in enumerate((row_ref, col_ref)):
        pad[spot, 0:BASES, 0:TAPS] = source[...]
        pad[spot, SPILL_AT:BASE_PAD, 0:TAPS] = source[ALIGNED:BASES]
    row = pad[0]
    lane = lane_id(BASE_PAD)
    group = lane // GROUP
    tiled = row
    for part in range(1, GROUPS_TILE):
        tiled = tiled + pltpu.roll(row, part * GROUP, 1)
    columns = [
        jnp.broadcast_to(pad[1, :, tap : tap + 1], (BASE_PAD, LANES)) for tap in range(TAPS)
    ]
    zero = jnp.zeros((BASE_PAD, LANES), F32)
    mains = []
    for tile in range(MAIN_TILES):
        spread = zero
        for part in range(GROUPS_TILE):
            tap = tile * GROUPS_TILE + part
            if tap < TAPS:
                spread = jnp.where(group == part, columns[tap], spread)
        mains.append(tiled * spread)
    spread = zero
    for tap in range(TAPS):
        spread = jnp.where(lane // 4 == tap, columns[tap], spread)
    corner = lax.rem(lane, 4)

    def tap_at(tap):
        return jnp.broadcast_to(pad[0, :, tap : tap + 1], (BASE_PAD, LANES))

    outer = jnp.where(
        corner == 0,
        tap_at(0),
        jnp.where(corner == 1, tap_at(1), jnp.where(corner == 2, tap_at(TAPS - 2), tap_at(TAPS - 1))),
    )
    inner = jnp.where(corner == 1, tap_at(0), jnp.where(corner == 2, tap_at(TAPS - 1), 0.0))
    outer = outer * spread
    inner = inner * spread
    for tile, values in enumerate(mains + [outer, inner]):
        base_ref[:, tile * LANES : (tile + 1) * LANES] = jnp.where(
            row_id(BASE_PAD) < BASES, values, 0.0
        )
    rows = weight_ref.shape[0] // (2 * BASE_PAD)
    even = even_stripe()
    first_tap, last_tap = tap_at(0), tap_at(TAPS - 1)

    def column_tile(tap_of):
        spread = zero
        begin = 0
        for end in range(1, LANES + 1):
            if end < LANES and tap_of(end) == tap_of(begin):
                continue
            if tap_of(begin) < TAPS:
                spread = jnp.where((lane >= begin) & (lane < end), columns[tap_of(begin)], spread)
            begin = end
        return spread

    def early_tap(place):
        if place < NEAR_AT:
            return place // 16
        return (place - NEAR_AT) // 8 if place < NEAR_EXTRA_AT else (place - NEAR_EXTRA_AT) // 2

    def late_tap(place):
        return place // 8 if place < FAR_EXTRA_AT else (place - FAR_EXTRA_AT) // 2

    early_tiles = [
        column_tile(lambda spot, tile=tile: early_tap(tile * LANES + spot))
        for tile in range(EARLY // LANES)
    ]
    late_tiles = [
        column_tile(lambda spot, tile=tile: late_tap(tile * LANES + spot))
        for tile in range(LATE // LANES)
    ]

    def repeats(period):
        blocks = []
        for start in range(0, TAPS, period):
            block = pltpu.roll(row, (LANES - start) % LANES, 1) if start else row
            block = jnp.where(lane < period, block, 0.0)
            size = period
            while size < LANES:
                block = block + pltpu.roll(block, size, 1)
                size *= 2
            blocks.append(block)
        return blocks

    def window(blocks, period, first):
        block, move = first // period, first % period
        here = blocks[block] if 0 <= block < len(blocks) else None
        beyond = blocks[block + 1] if 0 <= block + 1 < len(blocks) else None
        if move == 0:
            return zero if here is None else here
        ready = lax.rem(lane, period) < period - move
        parts = [zero if part is None else pltpu.roll(part, LANES - move, 1) for part in (here, beyond)]
        return jnp.where(ready, parts[0], parts[1])

    by_sixteen, by_eight = repeats(16), repeats(8)
    own_rows = [window(by_sixteen, 16, HALF - line) for line in range(rows)]
    top_rows = [window(by_eight, 8, 1 - line) for line in range(rows)]
    bottom_rows = [window(by_eight, 8, rows + HALF - line) for line in range(rows)]

    parity = lax.rem(lane, 2)

    def corner_taps(upper, lower, is_upper):
        top = jnp.where(parity == 1, first_tap, 0.0) if upper else zero
        bottom = jnp.where(parity == 0, last_tap, 0.0) if lower else zero
        return jnp.where(is_upper, top, bottom)

    near_is_top = ~even
    early_rows, late_rows = [], []
    for spot in range(rows):
        odd_line = spot + rows - HALF if spot < HALF else spot - HALF
        own = jnp.where(even, own_rows[spot], own_rows[odd_line])
        side = jnp.where(even, bottom_rows[spot], top_rows[odd_line])
        extra = zero
        if spot >= HALF:
            extra = corner_taps(spot == HALF, spot == rows - 1, near_is_top)
        tiles = [
            own,
            own,
            jnp.where(lane < NEAR_AT - 2 * LANES, own, side),
            jnp.where(lane < NEAR_EXTRA_AT - 3 * LANES, side, extra),
        ]
        early_rows.append(
            jnp.concatenate([mine * tile for mine, tile in zip(tiles, early_tiles)], axis=1)
        )
        if spot < HALF:
            side = jnp.where(even, top_rows[spot], bottom_rows[odd_line])
            extra = corner_taps(spot == 0, spot == HALF - 1, even)
            tiles = [side, jnp.where(lane < FAR_EXTRA_AT - LANES, side, extra)]
            late_rows.append(
                jnp.concatenate([mine * tile for mine, tile in zip(tiles, late_tiles)], axis=1)
            )
    for spot in range(0, rows, 2):
        put_split(weight_ref, spot * BASE_PAD, jnp.concatenate(early_rows[spot : spot + 2], axis=0))
    spare = late_ref.shape[0] // 2 - HALF * BASE_PAD
    late_rows.append(jnp.zeros((spare, LATE), F32))
    put_split(late_ref, 0, jnp.concatenate(late_rows, axis=0))


def edges_of(near_ref, far_ref):
    even = even_stripe()
    near = near_ref[...]
    far = far_ref[...]
    return jnp.where(even, far, near), jnp.where(even, near, far)


def fill_extended(ext, highs, lows, cores, pieces, near_ref, far_ref):
    rows, half = pieces[0].shape
    wide = half * cores
    ext[:, 0:LANES] = jnp.zeros((ext.shape[0], LANES), F32)
    ext[:, LANES + wide :] = jnp.zeros((ext.shape[0], LANES), F32)
    me = lax.axis_index("exp")
    for step in range(cores):
        start = lax.rem(me + step, cores) * half + LANES
        ext[8 : 8 + rows, pl.ds(pl.multiple_of(start, LANES), half)] = pieces[step][...]
    top, bottom = edges_of(near_ref, far_ref)
    for side in range(cores):
        where = pl.ds(LANES + side * half, half)
        ext[0:8, where] = top[8 * side : 8 * side + 8]
        ext[8 + rows : 16 + rows, where] = bottom[8 * side : 8 * side + 8]
        spots = [8 * cores + side, 9 * cores + side]
        spare = [edge[spot : spot + 1] for edge in (top, bottom) for spot in spots]
        ext[16 + rows : 24 + rows, where] = jnp.concatenate(spare + spare, axis=0)
    main = slice(0, GROUP)
    highs[main], lows[main] = split_two(ext[main])
    extra = ext[GROUP : GROUP + 8]
    span = extra.shape[1]
    early = lax.broadcasted_iota(jnp.int32, extra.shape, 0) < 4
    ahead = [extra] + [pltpu.roll(extra, span - part, 1) for part in range(1, 4)]
    lines = jnp.concatenate(
        [jnp.where(early, ahead[0], ahead[1]), jnp.where(early, ahead[2], ahead[3])], axis=0
    )
    highs[GROUP:], lows[GROUP:] = split_two(lines)


def spread_window(shifted, put):
    for tap in range(TAPS):
        put(tap * GROUP, shifted(tap, slice(0, GROUP)))
    for quad in range(MAIN_TILES):
        put(MAIN + 16 * quad, shifted(4 * quad, slice(GROUP, GROUP + 16)))


def clear_spare(refs):
    for ref in refs:
        wide = ref.shape[1]
        ref[TAPS * GROUP : MAIN] = jnp.zeros((MAIN - TAPS * GROUP, wide), BF16)
        ref[MAIN + EXTRA_ROWS :] = jnp.zeros((LANES - EXTRA_ROWS, wide), BF16)


def back_profile(horiz):
    steady = jnp.ones_like(horiz)
    square = 0.5 * (3.0 * horiz * horiz - 1.0)
    return [steady, horiz, steady, horiz, square, steady, horiz]


def put_sides(target, edge_ref):
    fold = edge_ref.shape[1]
    cores = edge_ref.shape[0] // (REACH + 2)
    for side in range(cores):
        where = pl.ds(LANES + side * fold, fold)
        target[0:8, where] = edge_ref[8 * side : 8 * side + 8]
        for line in range(2):
            spot = (8 + line) * cores + side
            target[8 + line : 9 + line, where] = edge_ref[spot : spot + 1]


def paired(values):
    span = values.shape[1]
    return jnp.concatenate([values, pltpu.roll(values, span - 1, 1)], axis=0)


def corner_block(lines):
    span = lines.shape[1]
    parts = [lines] + [pltpu.roll(lines, span - move, 1) for move in range(1, 8)]
    return jnp.concatenate(parts, axis=0)


def odd_rows(odd_ref, stamp, height):
    return jnp.broadcast_to(odd_ref[stamp : stamp + 1, :] == 1, (height, LANES))


def stamp_window(source, odd_ref, stamp, offset):
    height = source.shape[0]
    lane = lane_id(height)
    left = source[:, stamp * LANES : (stamp + 1) * LANES]
    centre = source[:, (stamp + 1) * LANES : (stamp + 2) * LANES]
    right = source[:, (stamp + 2) * LANES : (stamp + 3) * LANES]
    odd = jnp.where(lane < LANES // 4, right, centre)
    even = jnp.where(lane >= LANES - HALF, left, centre)
    odd = pltpu.roll(odd, (HALF + STAMP_W + offset) % LANES, 1)
    even = pltpu.roll(even, HALF + offset, 1)
    return jnp.where(odd_rows(odd_ref, stamp, height), odd, even)


def stamp_values(sources, odd_ref, pair, moves):
    out = []
    for source in sources:
        first = stamp_window(source, odd_ref, 2 * pair, 0)
        second = stamp_window(source, odd_ref, 2 * pair + 1, STAMP_W)
        tiles = []
        for tile, move in moves:
            a, b = first[16 * tile : 16 * tile + 16], second[16 * tile : 16 * tile + 16]
            if move:
                a = pltpu.roll(a, LANES - move, 1)
                b = pltpu.roll(b, LANES - move, 1)
            tiles.append(jnp.where(lane_id(16) < STAMP_W, a, b))
        out.append(jnp.concatenate(tiles, axis=0))
    return out


def three_products(weights, xhigh, xlow):
    rows = weights.shape[0] // 2
    both = jnp.dot(weights, xhigh, preferred_element_type=F32)
    return both[:rows] + (
        both[rows:] + jnp.dot(weights[:rows], xlow, preferred_element_type=F32)
    )


def back_rows(rows):
    empty = jnp.zeros_like(rows[0])
    lead = [empty] * (8 - BACK_FIRST)
    second = lead + rows[BACK_FIRST:]
    second += [empty] * (8 - len(second))
    return [jnp.concatenate(part, axis=0) for part in (lead + rows[:BACK_FIRST], second)]


def design_line(bases, keep, target, horiz, profiles, row, region_rows):
    own = bases * keep
    vert = position(jnp.full(horiz.shape, row, jnp.int32), region_rows)
    square = 0.5 * (3.0 * vert * vert - 1.0)
    steady = jnp.ones_like(vert)
    scales = back_rows([steady, steady, vert, vert, steady, square, square])
    first, second = (profile * scale * keep for profile, scale in zip(profiles, scales))
    spot = lax.broadcasted_iota(jnp.int32, second.shape, 0)
    sloped = own * horiz
    tilted = own * vert
    mixed = jnp.where(spot < SPILL_AT - ALIGNED, second, tilted[ALIGNED:])
    return jnp.concatenate(
        [
            own[:ALIGNED],
            jnp.where(spot < SPILL, own[ALIGNED:], first),
            sloped[:ALIGNED],
            jnp.where(spot < SPILL, sloped[ALIGNED:], mixed),
            tilted[:ALIGNED],
            jnp.where(spot == 0, target, 0.0),
        ],
        axis=0,
    )


def gram(lines):
    design = jnp.concatenate([line.astype(BF16) for line in lines], axis=1)
    return lax.dot_general(design, design, (((1,), (1,)), ((), ())), preferred_element_type=F32)


def early_kernel(cores, stripes, *refs):
    pieces = refs[:cores]
    near_pieces = refs[cores : 2 * cores]
    (
        science_ref,
        good_ref,
        odd_ref,
        weight_ref,
        total_ref,
        late_ref,
        aux_ref,
        near_ref,
        ext,
        highs,
        lows,
        bases,
    ) = refs[2 * cores :]
    rows, half = pieces[0].shape
    wide = science_ref.shape[2]
    pairs = wide // (4 * STAMP_W)
    me = lax.axis_index("exp")
    ext[:, 0:LANES] = jnp.zeros((ext.shape[0], LANES), F32)
    ext[:, LANES + wide :] = jnp.zeros((ext.shape[0], LANES), F32)
    for step in range(cores):
        side = lax.rem(me + step, cores)
        where = pl.ds(pl.multiple_of(side * half + LANES, LANES), half)
        ext[0:rows, where] = pieces[step][...]
        edge = near_pieces[step][...]
        ext[rows : rows + REACH, where] = edge[:REACH]
        near_ref[pl.ds(pl.multiple_of(8 * side, 8), 8), :] = edge[:8]
        for line in range(2):
            near_ref[pl.ds((8 + line) * cores + side, 1), :] = edge[8 + line : 9 + line]
    near_ref[REACH * cores :] = near_pieces[0][REACH : REACH + 2 * cores]
    lines = jnp.concatenate(
        [ext[0:rows], paired(ext[rows : rows + 8]), corner_block(ext[rows + 8 : rows + 10])], axis=0
    )
    highs[...], lows[...] = split_two(lines)
    moves = [(0, tap) for tap in range(TAPS)]
    moves += [(1, 2 * step) for step in range(10)]
    moves += [(2, 8 * step) for step in range(3)]
    lane = lane_id(1)
    for pair in range(pairs):
        columns = slice(pair * LANES, (pair + 1) * LANES)
        odd = jnp.where(
            lane < STAMP_W,
            odd_ref[2 * pair : 2 * pair + 1],
            odd_ref[2 * pair + 1 : 2 * pair + 2] + 1,
        )
        horiz = position(4 * pair * STAMP_W + odd * STAMP_W + lane, wide)
        aux_ref[2 * rows : 2 * rows + 8, columns] = jnp.broadcast_to(horiz, (8, LANES))
        picked = []
        for source in (good_ref, science_ref):
            lower = source[0, :, 2 * pair * LANES : (2 * pair + 1) * LANES]
            upper = source[0, :, (2 * pair + 1) * LANES : (2 * pair + 2) * LANES]
            lower = jnp.where(
                odd_rows(odd_ref, 2 * pair, rows), pltpu.roll(lower, STAMP_W, 1), lower
            )
            upper = jnp.where(
                odd_rows(odd_ref, 2 * pair + 1, rows), upper, pltpu.roll(upper, STAMP_W, 1)
            )
            picked.append(jnp.where(lane_id(rows) < STAMP_W, lower, upper))
        aux_ref[0:rows, columns] = picked[0]
        aux_ref[rows : 2 * rows, columns] = picked[0] * picked[1]
    split = HALF * BASE_PAD
    chunk = 2 * LANES
    for start in range(0, wide // 2, chunk):
        span = slice(start, start + chunk)
        made = [
            stamp_values((highs, lows), odd_ref, pair, moves)
            for pair in range(start // LANES, (start + chunk) // LANES)
        ]
        values = three_products(
            weight_ref[...],
            *(jnp.concatenate([one[side] for one in made], axis=1) for side in range(2)),
        )
        late_ref[:, span] = values[:split]
        bases[:, span] = values[split:]
    horiz = aux_ref[2 * rows : 2 * rows + 1]
    profile = back_rows(back_profile(horiz))
    first_line = jnp.where(even_stripe(), HALF, 0)
    first_row = lax.axis_index("stripe") * rows
    designs = []
    for spot in range(rows - HALF):
        line = first_line + spot
        designs.append(design_line(
            bases[spot * BASE_PAD : (spot + 1) * BASE_PAD],
            aux_ref[pl.ds(line, 1), :],
            aux_ref[pl.ds(rows + line, 1), :],
            horiz,
            profile,
            first_row + line,
            rows * stripes,
        ))
    total = gram(designs)
    total_ref[...] = jnp.concatenate(
        [total, jnp.zeros((FIT_ROWS, LANES - FIT_ROWS), F32)], axis=1
    )


def late_kernel(stripes, rows, *refs):
    (
        far_ref,
        odd_ref,
        weight_ref,
        total_ref,
        early_ref,
        aux_ref,
        out_ref,
        ext,
        highs,
        lows,
        bases,
    ) = refs
    width = early_ref.shape[1]
    pairs = width // LANES
    ext[:, 0:LANES] = jnp.zeros((ext.shape[0], LANES), F32)
    ext[:, ext.shape[1] - LANES :] = jnp.zeros((ext.shape[0], LANES), F32)
    put_sides(ext, far_ref)
    lines = jnp.concatenate([paired(ext[0:8]), corner_block(ext[8:10])], axis=0)
    highs[...], lows[...] = split_two(lines)
    moves = [(0, 2 * step) for step in range(10)] + [(1, 8 * step) for step in range(3)]
    used = 16 * len(moves)
    split = HALF * BASE_PAD
    chunk = 4 * LANES
    for start in range(0, width, chunk):
        span = slice(start, start + chunk)
        made = [
            stamp_values((highs, lows), odd_ref, pair, moves)
            for pair in range(start // LANES, (start + chunk) // LANES)
        ]
        spare = jnp.zeros((LATE - used, chunk), BF16)
        xh, xl = (
            jnp.concatenate([jnp.concatenate([one[side] for one in made], axis=1), spare], axis=0)
            for side in range(2)
        )
        values = three_products(weight_ref[...], xh, xl)
        bases[:, span] = early_ref[:, span] + values[:split]
    horiz = aux_ref[2 * rows : 2 * rows + 1]
    profile = back_rows(back_profile(horiz))
    first_line = jnp.where(even_stripe(), 0, rows - HALF)
    first_row = lax.axis_index("stripe") * rows
    designs = []
    for spot in range(HALF):
        line = first_line + spot
        designs.append(
            design_line(
                bases[spot * BASE_PAD : (spot + 1) * BASE_PAD],
                aux_ref[pl.ds(line, 1), :],
                aux_ref[pl.ds(rows + line, 1), :],
                horiz,
                profile,
                first_row + line,
                rows * stripes,
            )
        )
    own = total_ref[:, :FIT_ROWS] + gram(designs)
    out_ref[...] = packed_normal(own)


def packed_normal(normal):
    half = UNKNOWNS // 2
    lane = lane_id(8)
    right = jnp.zeros((8, LANES), F32)
    for tile in range(UNKNOWNS // 8):
        column = normal[8 * tile : 8 * tile + 8, UNKNOWNS : UNKNOWNS + 1]
        right = jnp.where(lane == tile, jnp.broadcast_to(column, (8, LANES)), right)
    both = [normal[:half, :UNKNOWNS], normal[half:UNKNOWNS, :UNKNOWNS]]
    return jnp.concatenate([jnp.concatenate(both, axis=1), right], axis=0)


def unpacked_normal(packed):
    half = UNKNOWNS // 2
    lane = lane_id(UNKNOWNS)
    values = jnp.concatenate([packed[:half], pltpu.roll(packed[:half], UNKNOWNS, 1)], axis=0)
    right = jnp.concatenate(
        [
            jnp.broadcast_to(packed[half:, tile : tile + 1], (8, LANES))
            for tile in range(UNKNOWNS // 8)
        ],
        axis=0,
    )
    return jnp.where(lane < UNKNOWNS, values, jnp.where(lane == UNKNOWNS, right, 0.0))


def tree_sum(values):
    while len(values) > 1:
        values = [sum(values[spot : spot + 2][1:], values[spot]) for spot in range(0, len(values), 2)]
    return values[0]


def solve_rows(matrix):
    sub = row_id(8)
    tiles = [matrix[start : start + 8] for start in range(0, UNKNOWNS, 8)]
    order = [(start, 8) for start in range(0, UNKNOWNS, 8)]

    def spread(tile, spot):
        return jnp.broadcast_to(tile[spot : spot + 1], (8, LANES))

    def column(tile, spot):
        return jnp.broadcast_to(tile[:, spot : spot + 1], (8, LANES))

    start, size = order[0]
    corner = [column(tiles[start // 8], start + j) for j in range(size)]
    for step, (start, size) in enumerate(order):
        home = start // 8
        columns = [
            [None if place == home else column(tile, start + j) for place, tile in enumerate(tiles)]
            for j in range(size)
        ]
        rows = tiles[home]
        following = order[step + 1] if step + 1 < len(order) else (0, 0)
        next_home = following[0] // 8
        ahead = [column(rows, following[0] + j) for j in range(following[1])]
        below = [column(tiles[next_home], following[0] + j) for j in range(following[1])]
        for spot in range(size):
            keep = sub == spot
            inverse = 1.0 / spread(corner[spot], spot)
            others = jnp.where(keep, 0.0, corner[spot])

            def eliminated(values):
                scaled = spread(values, spot) * inverse
                return jnp.where(keep, scaled, values - others * scaled)

            corner = [
                eliminated(values) if j > spot else values for j, values in enumerate(corner)
            ]
            ahead = [eliminated(values) for values in ahead]
            rows = eliminated(rows)
        if following[1]:
            corner = [
                values - tree_sum([columns[i][next_home] * spread(ahead[j], i) for i in range(size)])
                for j, values in enumerate(below)
            ]
        for place in range(len(tiles)):
            if place == home:
                tiles[place] = rows
            else:
                tiles[place] = tiles[place] - tree_sum(
                    [columns[i][place] * spread(rows, i) for i in range(size)]
                )
    right = jnp.concatenate(tiles, axis=0)[:, UNKNOWNS : UNKNOWNS + 1]
    return jnp.broadcast_to(right, (UNKNOWNS, LANES))


def region_weights(base_ref, weight_ref, rows):
    lane = lane_id(8)
    spot = lax.rem(lane, GROUP)
    corner = lax.rem(lane, 4)
    line = row_id(8)
    mains = [base_ref[:, tile * LANES : (tile + 1) * LANES] for tile in range(MAIN_TILES)]
    outer = base_ref[:, MAIN : MAIN + LANES]
    inner = base_ref[:, MAIN + LANES :]
    blocks = [[] for _ in range(BASES)]
    for start in range(0, rows, 8):
        tap = spot - (start + line - 1)
        inside = (tap >= 0) & (tap < TAPS)
        moved = [pltpu.roll(main, (start - 1) % LANES, 1) for main in mains]
        extra = zero_row = jnp.zeros((8, LANES), F32)
        for b in range(BASES):
            tiles = []
            for main in moved:
                wide = jnp.broadcast_to(main[b : b + 1], (8, LANES))
                tiles.append(
                    jnp.where(inside, pltpu.roll(wide, 0, 1, stride=1, stride_axis=0), 0.0)
                )
            extra = zero_row
            mine = jnp.broadcast_to(inner[b : b + 1], (8, LANES))
            if start == 0:
                extra = jnp.where((line == 0) & (corner < 2), mine, extra)
            if start == rows - 8:
                extra = jnp.where((line == 7) & (corner >= 2), mine, extra)
            blocks[b].append(jnp.concatenate(tiles + [extra], axis=1))
    for b in range(BASES):
        put_split(weight_ref, b * rows, jnp.concatenate(blocks[b], axis=0))
    lane = lane_id(BASE_PAD)
    spot = lax.rem(lane, GROUP)
    corner = lax.rem(lane, 4)
    halos = []
    for shift, extra in ((rows - 1, corner >= 2), (-2, corner < 2)):
        tap = spot - shift
        inside = (tap >= 0) & (tap < TAPS)
        tiles = [jnp.where(inside, pltpu.roll(main, shift % LANES, 1), 0.0) for main in mains]
        halos.append(jnp.concatenate(tiles + [jnp.where(extra, outer, 0.0)], axis=1))
    put_split(weight_ref, BASES * rows, jnp.concatenate(halos, axis=0))


def region_bases(highs, lows, weight_ref, first, out_ref, scratch):
    wide = out_ref.shape[1]
    chunk = scratch[0].shape[1]
    for spot, start in enumerate(range(0, wide, chunk)):
        targets = scratch[2 * spot : 2 * spot + 2]
        clear_spare(targets)
        for source, target in zip((highs, lows), targets):

            def shifted(tap, lines):
                begin = first + start + LANES - HALF + tap
                return source[lines, begin : begin + chunk]

            def put(place, values):
                target[place : place + values.shape[0]] = values

            spread_window(shifted, put)
        out_ref[:, start : start + chunk] = three_products(
            weight_ref[...], targets[0][...], targets[1][...]
        )


def first_bases_kernel(cores, *refs):
    pieces = refs[:cores]
    (
        far_ref,
        near_ref,
        base_ref,
        after_ref,
        weight_ref,
        highs,
        lows,
        out_ref,
        ext,
        *scratch,
    ) = refs[cores:]
    region_weights(base_ref, weight_ref, pieces[0].shape[0])
    fill_extended(ext, highs, lows, cores, pieces, near_ref, far_ref)
    region_bases(highs, lows, weight_ref, 0, out_ref, scratch)


def next_bases_kernel(first, highs, lows, weight_ref, after_ref, out_ref, *scratch):
    region_bases(highs, lows, weight_ref, first, out_ref, scratch)


def add_kernel(count, *refs):
    values = [ref[...] for ref in refs[:count]]
    if count == 4:
        order = (1, 2, 0)
        values = [values[0]] + [values[1 + order.index(k)] for k in range(3)]
    refs[-1][...] = tree_sum(values)


def model_kernel(stripes, count, *refs):
    far_ref, near_ref, science_ref, good_ref, out_ref, coef_ref = refs[-6:]
    parts = refs[count:-6]
    rows = science_ref.shape[1]
    wide = science_ref.shape[2]
    top, bottom = edges_of(near_ref, far_ref)
    coef = solve_rows(unpacked_normal(tree_sum([ref[...] for ref in refs[:count]])))
    lane = lane_id(UNKNOWNS)
    base, term = lane // 3, lax.rem(lane, 3)
    tilt = jnp.where(base < ALIGNED, 2 * BASE_PAD, BASE_PAD + SPILL_AT - ALIGNED) + base
    home = lane - 3 * BASES + jnp.where(lane < 3 * BASES + BACK_FIRST, BASES, BASE_PAD + BASES - BACK_FIRST)
    home = jnp.where(lane < 3 * BASES, jnp.where(term == 2, tilt, term * BASE_PAD + base), home)
    flat = jnp.sum(jnp.where(row_id(UNKNOWNS) == home, coef, 0.0), axis=0, keepdims=True)
    coef_ref[...] = flat[:, : coef_ref.shape[1]]

    def share(spot, height):
        return jnp.broadcast_to(coef[spot : spot + 1], (height, LANES))

    first_row = lax.axis_index("stripe") * rows
    vert = position(first_row + row_id(rows), rows * stripes)
    halo_vert = [
        position(jnp.full((8, LANES), first_row + line, jnp.int32), rows * stripes)
        for line in (rows, -1)
    ]
    tilts = [
        2 * BASE_PAD + b if b < ALIGNED else BASE_PAD + SPILL_AT + b - ALIGNED for b in range(BASES)
    ]
    slopes = [share(spot, rows) * vert for spot in tilts]
    tilted = jnp.concatenate(
        [
            coef[2 * BASE_PAD :],
            coef[BASE_PAD + SPILL_AT : 2 * BASE_PAD],
            jnp.zeros((BACK_FIRST, LANES), F32),
        ],
        axis=0,
    )
    halo_slopes = [tilted * jnp.concatenate([line] * 3, axis=0) for line in halo_vert]
    level = [
        share(BASES + m + (0 if m < BACK_FIRST else BASE_PAD - BACK_FIRST), 8) for m in range(BACK)
    ]

    def ground(here, horiz):
        square = 0.5 * (3.0 * here * here - 1.0)
        horiz_square = 0.5 * (3.0 * horiz * horiz - 1.0)
        steady = level[0] + level[1] * horiz + level[4] * horiz_square
        sloped = level[2] + level[3] * horiz
        curved = level[5] + level[6] * horiz
        if here.shape[0] > 8:
            steady, sloped, curved = (
                jnp.concatenate([part] * (here.shape[0] // 8), axis=0)
                for part in (steady, sloped, curved)
            )
        return steady + here * sloped + square * curved

    lane_row = lane_id(rows)
    line_row = row_id(rows)
    tiles = wide // LANES
    edges = []
    for edge in (top, bottom):
        cores = edge.shape[0] // (REACH + 2)
        edges.append(
            [
                jnp.concatenate(
                    [edge[spot : spot + 1] for spot in range(first * cores, (first + 1) * cores)],
                    axis=1,
                )
                for first in (REACH, REACH + 1)
            ]
        )
    owns, aboves, belows = [], [], []

    def put_tile(tile):
        own = owns[tile]
        empty = jnp.zeros_like(own)
        earlier = owns[tile - 1] if tile else empty
        later = owns[tile + 1] if tile + 1 < tiles else empty
        above = jnp.where(line_row == 0, aboves[tile], pltpu.roll(own, 1, 0))
        below = jnp.where(line_row == rows - 1, belows[tile], pltpu.roll(own, rows - 1, 0))
        before = pltpu.roll(jnp.where(lane_row == LANES - 1, earlier, own), 1, 1)
        after = pltpu.roll(jnp.where(lane_row == 0, later, own), LANES - 1, 1)
        span = slice(tile * LANES, (tile + 1) * LANES)
        out_ref[0, :, span] = 4.0 * own - (below + above + after + before)

    for part in parts:
        for start in range(0, part.shape[1], LANES):
            span = slice(start, start + LANES)
            tile = len(owns)
            begin = tile * LANES
            place = slice(begin, begin + LANES)
            horiz = position(begin + lane_id(8), wide)
            total = ground(vert, horiz)
            for b in range(BASES):
                steady = share(b, 8) + share(BASE_PAD + b, 8) * horiz
                scale = jnp.concatenate([steady] * (rows // 8), axis=0) + slopes[b]
                total = total + part[b * rows : (b + 1) * rows, span] * scale
            owns.append(good_ref[0, :, place] * (science_ref[0, :, place] - total))
            steady = coef[:BASE_PAD] + coef[BASE_PAD : 2 * BASE_PAD] * horiz[0:1]
            for side, kept in enumerate((belows, aboves)):
                spot = BASES * rows + side * BASE_PAD
                values = part[spot : spot + BASE_PAD, span] * (steady + halo_slopes[side])
                values = jnp.sum(values, axis=0, keepdims=True)
                values = values + ground(halo_vert[side], horiz)[0:1]
                science, good = edges[1 - side]
                kept.append(good[:, place] * (science[:, place] - values))
            if tile:
                put_tile(tile - 1)
    put_tile(tiles - 1)

def whole_vmem(count):
    return [pl.BlockSpec(memory_space=pltpu.VMEM)] * count


def add(values, after, params):
    return pl.pallas_call(
        functools.partial(add_kernel, len(values)),
        out_shape=jax.ShapeDtypeStruct(values[0].shape, values[0].dtype),
        in_specs=whole_vmem(len(values) + len(after)),
        out_specs=pl.BlockSpec(memory_space=pltpu.VMEM),
        compiler_params=params,
        name="add",
    )(*values, *after)


def summed(values, axis, beside, params):
    count = lax.axis_size(axis)
    if count & (count - 1):
        for works in beside:
            for work in works:
                work(values)
        return [lax.psum(values, axis)]
    rounds = [(1, 2, 3)] if count >= 4 else []
    step = 4 if rounds else 1
    while step < count:
        rounds.append((step,))
        step *= 2
    last = len(rounds) - 1
    rounds += [()] * (len(beside) - len(rounds))
    for spot, steps in enumerate(rounds):
        others = [
            lax.ppermute(values, axis, [(i, i ^ step) for i in range(count)]) for step in steps
        ]
        after = [work(values) for work in beside[spot]] if spot < len(beside) else []
        if steps:
            if len(others) == 3:
                others = [others[k] for k in (1, 2, 0)]
            if spot == last:
                for works in beside[spot + 1 :]:
                    for work in works:
                        work(values)
                return [values] + others
            values = add([values] + others, after, params)
    return [values]


def shared_pieces(values, cores):
    return [
        lax.ppermute(values, "exp", [((i + step) % cores, i) for i in range(cores)])
        for step in range(1, cores)
    ]


def shards(template, exposure, cosmic_mask, stamp_blocks, row_filters, col_filters):
    arguments = (template, exposure, cosmic_mask, row_filters, col_filters, stamp_blocks)
    rows, half = template.shape
    wide = exposure.shape[2]
    cores = lax.axis_size("exp")
    stripes = lax.axis_size("stripe")
    params = pltpu.CompilerParams(vmem_limit_bytes=24 * 1024 * 1024)
    pieces = [template] + shared_pieces(template, cores)
    stamps = stamp_blocks.shape[1]
    template_in, science, good, row_in, col_in, odd = pl.pallas_call(
        load_kernel,
        out_shape=(
            jax.ShapeDtypeStruct(template.shape, F32),
            jax.ShapeDtypeStruct(exposure.shape, F32),
            jax.ShapeDtypeStruct(exposure.shape, F32),
            jax.ShapeDtypeStruct(row_filters.shape, F32),
            jax.ShapeDtypeStruct(col_filters.shape, F32),
            jax.ShapeDtypeStruct((stamps, LANES), jnp.int32),
        ),
        in_specs=[pl.BlockSpec(memory_space=pltpu.HBM)] * 6,
        out_specs=tuple(whole_vmem(6)),
        scratch_shapes=[
            pltpu.VMEM(cosmic_mask.shape, jnp.int32),
            pltpu.SMEM(stamp_blocks.shape, jnp.int32),
            pltpu.SemaphoreType.DMA((6,)),
        ],
        compiler_params=params,
        name="load",
    )(*[pltpu.with_memory_space_constraint(array, pltpu.HBM) for array in arguments])
    pieces = [template_in] + pieces[1:]
    near_pairs = [(i, i + 1) for i in range(0, stripes - 1, 2)]
    far_pairs = [(i, i + 1) for i in range(1, stripes - 1, 2)]

    def swapped(values, couples):
        return lax.ppermute(values, "stripe", couples + [(b, a) for a, b in couples])

    near = pl.pallas_call(
        functools.partial(near_kernel, cores),
        out_shape=jax.ShapeDtypeStruct((-(-(REACH + 2 * cores) // 8) * 8, half), F32),
        in_specs=whole_vmem(3),
        out_specs=pl.BlockSpec(memory_space=pltpu.VMEM),
        compiler_params=params,
        name="near",
    )(template_in, science, good)
    near = swapped(near, near_pairs)
    near_pieces = [near] + shared_pieces(near, cores)
    edge_shape = jax.ShapeDtypeStruct(((REACH + 2) * cores, half), F32)
    far = pl.pallas_call(
        functools.partial(far_kernel, cores),
        out_shape=edge_shape,
        in_specs=whole_vmem(cores + 2),
        out_specs=pl.BlockSpec(memory_space=pltpu.VMEM),
        scratch_shapes=[pltpu.VMEM((rows, wide), F32)],
        compiler_params=params,
        name="far",
    )(*pieces, science, good)
    far = swapped(far, far_pairs)
    early_shape = jax.ShapeDtypeStruct((2 * rows * BASE_PAD, EARLY), BF16)
    late_shape = jax.ShapeDtypeStruct((2 * LATE_ROWS, LATE), BF16)
    early_weights, late_weights, base = pl.pallas_call(
        weight_kernel,
        out_shape=(
            early_shape,
            late_shape,
            jax.ShapeDtypeStruct((BASE_PAD, DEPTH + LANES), F32),
        ),
        in_specs=whole_vmem(2),
        out_specs=tuple(whole_vmem(3)),
        scratch_shapes=[pltpu.VMEM((2, BASE_PAD, LANES), F32)],
        compiler_params=params,
        name="weights",
    )(row_in, col_in)
    width = wide // 2
    reach = wide + 2 * LANES
    normal_shape = jax.ShapeDtypeStruct((FIT_ROWS, LANES), F32)
    part, kept, aux, near = pl.pallas_call(
        functools.partial(early_kernel, cores, stripes),
        out_shape=(
            normal_shape,
            jax.ShapeDtypeStruct((HALF * BASE_PAD, width), F32),
            jax.ShapeDtypeStruct((2 * rows + 8, width), F32),
            edge_shape,
        ),
        in_specs=whole_vmem(2 * cores + 4),
        out_specs=tuple(whole_vmem(4)),
        scratch_shapes=[
            pltpu.VMEM((rows + 16, reach), F32),
            pltpu.VMEM((rows + 32, reach), BF16),
            pltpu.VMEM((rows + 32, reach), BF16),
            pltpu.VMEM(((rows - HALF) * BASE_PAD, width), F32),
        ],
        compiler_params=params,
        name="early",
    )(*pieces, *near_pieces, science, good, odd, early_weights)
    normal = pl.pallas_call(
        functools.partial(late_kernel, stripes, rows),
        out_shape=jax.ShapeDtypeStruct((UNKNOWNS // 2 + 8, LANES), F32),
        in_specs=whole_vmem(6),
        out_specs=pl.BlockSpec(memory_space=pltpu.VMEM),
        scratch_shapes=[
            pltpu.VMEM((16, reach), F32),
            pltpu.VMEM((32, reach), BF16),
            pltpu.VMEM((32, reach), BF16),
            pltpu.VMEM((HALF * BASE_PAD, width), F32),
        ],
        compiler_params=params,
        name="late",
    )(far, odd, late_weights, part, kept, aux)
    region_rows = BASES * rows + 2 * BASE_PAD
    blocks = wide // (2 * LANES)
    cuts = [blocks * cut // 8 * 2 * LANES for cut in (0, 2, 4, 8)]
    weight_shape = jax.ShapeDtypeStruct((2 * region_rows, DEPTH), BF16)
    source_shape = jax.ShapeDtypeStruct((GROUP + 16, reach), BF16)
    parts, shared = [], []

    def shift_scratch(size):
        chunk = 2 * LANES
        return [pltpu.VMEM((DEPTH, chunk), BF16)] * (2 * (size // chunk))

    def first_bases(after):
        size = cuts[1]
        *made, part = pl.pallas_call(
            functools.partial(first_bases_kernel, cores),
            out_shape=(
                weight_shape,
                source_shape,
                source_shape,
                jax.ShapeDtypeStruct((region_rows, size), F32),
            ),
            in_specs=whole_vmem(cores + 4),
            out_specs=tuple(whole_vmem(4)),
            scratch_shapes=[pltpu.VMEM((rows + 24, reach), F32)] + shift_scratch(size),
            compiler_params=params,
            name="bases",
        )(*pieces, far, near, base, after)
        shared.extend(made)
        parts.append(part)
        return part

    def next_bases(cut, after):
        size = cuts[cut + 1] - cuts[cut]
        region_weight, highs, lows = shared
        part = pl.pallas_call(
            functools.partial(next_bases_kernel, cuts[cut]),
            out_shape=jax.ShapeDtypeStruct((region_rows, size), F32),
            in_specs=whole_vmem(4),
            out_specs=pl.BlockSpec(memory_space=pltpu.VMEM),
            scratch_shapes=shift_scratch(size),
            compiler_params=params,
            name="bases",
        )(highs, lows, region_weight, after)
        parts.append(part)
        return part

    beside = [[first_bases, functools.partial(next_bases, 1)], [functools.partial(next_bases, 2)]]
    shares = summed(normal, "stripe", beside, params)
    filtered, coef = pl.pallas_call(
        functools.partial(model_kernel, stripes, len(shares)),
        out_shape=(
            jax.ShapeDtypeStruct(exposure.shape, F32),
            jax.ShapeDtypeStruct((1, 3 * BASES + BACK), F32),
        ),
        in_specs=whole_vmem(len(shares) + len(parts) + 4),
        out_specs=tuple(whole_vmem(2)),
        compiler_params=params,
        name="model",
    )(*shares, *parts, far, near, science, good)
    return filtered, coef


def solution(mesh):
    placed = (
        P(("groups", "stripe"), "exp"),
        P(("groups", "exp"), "stripe", None),
        P(("groups", "exp"), "stripe", None),
        P(("groups", "stripe"), None),
        P(),
        P(),
    )
    return jax.shard_map(
        shards,
        mesh=mesh,
        in_specs=placed,
        out_specs=(P(("groups", "exp"), "stripe", None), P(("groups", "exp"), None)),
        check_vma=False,
    )
```

```python
import functools

import jax
import jax.numpy as jnp
from jax import lax
from jax.experimental import pallas as pl
from jax.experimental.pallas import tpu as pltpu
from jax.sharding import PartitionSpec as P

HALF = 9
TAPS = 2 * HALF + 1
BASES = 19
STAMP_W = 64
LANES = 128
BASE_PAD = 24
BACK = 7
BACK_FIRST = BASE_PAD - BASES
ALIGNED = BASES // 8 * 8
SPILL = BASES - ALIGNED
SPILL_AT = BASE_PAD - SPILL
UNKNOWNS = 2 * BASE_PAD + ALIGNED
FIT_ROWS = UNKNOWNS + 8
REACH = HALF + 1
GROUP = 32
GROUPS_TILE = LANES // GROUP
MAIN_TILES = 5
MAIN = MAIN_TILES * LANES
DEPTH = MAIN + LANES
EXTRA_ROWS = 80
NEAR_AT = TAPS * 16
NEAR_EXTRA_AT = NEAR_AT + 160
EARLY = NEAR_EXTRA_AT + 48
FAR_EXTRA_AT = 160
LATE = 2 * LANES
LATE_ROWS = -(-HALF * BASE_PAD // 16) * 16
F32 = jnp.float32
BF16 = jnp.bfloat16


def lane_id(rows):
    return lax.broadcasted_iota(jnp.int32, (rows, LANES), 1)


def row_id(rows):
    return lax.broadcasted_iota(jnp.int32, (rows, LANES), 0)


def split_two(values):
    high = values.astype(BF16)
    low = (values - high.astype(F32)).astype(BF16)
    return high, low


def put_split(target, start, values):
    size = values.shape[0]
    gap = target.shape[0] // 2
    target[start : start + size], target[gap + start : gap + start + size] = split_two(values)


def position(index, total):
    return (2.0 * index.astype(F32) + 1.0) / total - 1.0


def even_stripe():
    return lax.rem(lax.axis_index("stripe"), 2) == 0


def edge_lines(rows, toward_near):
    last = (rows - 8, rows - REACH, rows - 1)
    first = (0, 8, 0)
    return (last, first) if toward_near else (first, last)


def sides_of(line, cores):
    fold = line.shape[1] // cores
    return [line[:, side * fold : (side + 1) * fold] for side in range(cores)]


def near_kernel(cores, template_ref, science_ref, good_ref, edge_ref):
    rows = template_ref.shape[0]

    def edge(main, extra, outer):
        parts = [template_ref[main : main + 8], template_ref[extra : extra + 2]]
        for source in (science_ref, good_ref):
            parts += sides_of(source[0, outer : outer + 1, :], cores)
        spare = edge_ref.shape[0] - REACH - 2 * cores
        return jnp.concatenate(parts + [jnp.zeros((spare, edge_ref.shape[1]), F32)], axis=0)

    if_even, if_odd = (edge(*lines) for lines in edge_lines(rows, True))
    edge_ref[...] = jnp.where(even_stripe(), if_even, if_odd)


def far_kernel(cores, *refs):
    pieces = refs[:cores]
    science_ref, good_ref, edge_ref, ext = refs[cores:]
    rows, half = pieces[0].shape
    me = lax.axis_index("exp")
    for step in range(cores):
        start = lax.rem(me + step, cores) * half
        ext[:, pl.ds(pl.multiple_of(start, LANES), half)] = pieces[step][...]

    def edge(main, extra, outer):
        parts = sides_of(ext[main : main + 8], cores)
        for line in (extra, extra + 1):
            parts += sides_of(ext[line : line + 1], cores)
        for source in (science_ref, good_ref):
            parts += sides_of(source[0, outer : outer + 1, :], cores)
        return jnp.concatenate(parts, axis=0)

    if_even, if_odd = (edge(*lines) for lines in edge_lines(rows, False))
    edge_ref[...] = jnp.where(even_stripe(), if_even, if_odd)


def load_kernel(
    template_hbm,
    science_hbm,
    good_hbm,
    row_hbm,
    col_hbm,
    stamps_hbm,
    template_ref,
    science_ref,
    good_ref,
    row_ref,
    col_ref,
    odd_ref,
    mask_ref,
    stamps_ref,
    sems,
):
    moves = [
        pltpu.make_async_copy(source, target, sems.at[spot])
        for spot, (source, target) in enumerate(
            [
                (science_hbm, science_ref),
                (good_hbm, mask_ref),
                (template_hbm, template_ref),
                (row_hbm, row_ref),
                (col_hbm, col_ref),
                (stamps_hbm, stamps_ref),
            ]
        )
    ]
    for move in moves:
        move.start()
    for move in moves:
        move.wait()
    good_ref[...] = mask_ref[...].astype(F32)
    odd_ref[...] = jnp.concatenate(
        [
            jnp.full((1, LANES), lax.rem(stamps_ref[0, stamp], 2), jnp.int32)
            for stamp in range(odd_ref.shape[0])
        ],
        axis=0,
    )


def weight_kernel(
    row_ref, col_ref, weight_ref, late_ref, base_ref, pad
):
    pad[...] = jnp.zeros_like(pad)
    for spot, source in enumerate((row_ref, col_ref)):
        pad[spot, 0:BASES, 0:TAPS] = source[...]
        pad[spot, SPILL_AT:BASE_PAD, 0:TAPS] = source[ALIGNED:BASES]
    row = pad[0]
    lane = lane_id(BASE_PAD)
    group = lane // GROUP
    tiled = row
    for part in range(1, GROUPS_TILE):
        tiled = tiled + pltpu.roll(row, part * GROUP, 1)
    columns = [
        jnp.broadcast_to(pad[1, :, tap : tap + 1], (BASE_PAD, LANES)) for tap in range(TAPS)
    ]
    zero = jnp.zeros((BASE_PAD, LANES), F32)
    mains = []
    for tile in range(MAIN_TILES):
        spread = zero
        for part in range(GROUPS_TILE):
            tap = tile * GROUPS_TILE + part
            if tap < TAPS:
                spread = jnp.where(group == part, columns[tap], spread)
        mains.append(tiled * spread)
    spread = zero
    for tap in range(TAPS):
        spread = jnp.where(lane // 4 == tap, columns[tap], spread)
    corner = lax.rem(lane, 4)

    def tap_at(tap):
        return jnp.broadcast_to(pad[0, :, tap : tap + 1], (BASE_PAD, LANES))

    outer = jnp.where(
        corner == 0,
        tap_at(0),
        jnp.where(corner == 1, tap_at(1), jnp.where(corner == 2, tap_at(TAPS - 2), tap_at(TAPS - 1))),
    )
    inner = jnp.where(corner == 1, tap_at(0), jnp.where(corner == 2, tap_at(TAPS - 1), 0.0))
    outer = outer * spread
    inner = inner * spread
    for tile, values in enumerate(mains + [outer, inner]):
        base_ref[:, tile * LANES : (tile + 1) * LANES] = jnp.where(
            row_id(BASE_PAD) < BASES, values, 0.0
        )
    rows = weight_ref.shape[0] // (2 * BASE_PAD)
    even = even_stripe()
    first_tap, last_tap = tap_at(0), tap_at(TAPS - 1)

    def column_tile(tap_of):
        spread = zero
        begin = 0
        for end in range(1, LANES + 1):
            if end < LANES and tap_of(end) == tap_of(begin):
                continue
            if tap_of(begin) < TAPS:
                spread = jnp.where((lane >= begin) & (lane < end), columns[tap_of(begin)], spread)
            begin = end
        return spread

    def early_tap(place):
        if place < NEAR_AT:
            return place // 16
        return (place - NEAR_AT) // 8 if place < NEAR_EXTRA_AT else (place - NEAR_EXTRA_AT) // 2

    def late_tap(place):
        return place // 8 if place < FAR_EXTRA_AT else (place - FAR_EXTRA_AT) // 2

    early_tiles = [
        column_tile(lambda spot, tile=tile: early_tap(tile * LANES + spot))
        for tile in range(EARLY // LANES)
    ]
    late_tiles = [
        column_tile(lambda spot, tile=tile: late_tap(tile * LANES + spot))
        for tile in range(LATE // LANES)
    ]

    def repeats(period):
        blocks = []
        for start in range(0, TAPS, period):
            block = pltpu.roll(row, (LANES - start) % LANES, 1) if start else row
            block = jnp.where(lane < period, block, 0.0)
            size = period
            while size < LANES:
                block = block + pltpu.roll(block, size, 1)
                size *= 2
            blocks.append(block)
        return blocks

    def window(blocks, period, first):
        block, move = first // period, first % period
        here = blocks[block] if 0 <= block < len(blocks) else None
        beyond = blocks[block + 1] if 0 <= block + 1 < len(blocks) else None
        if move == 0:
            return zero if here is None else here
        ready = lax.rem(lane, period) < period - move
        parts = [zero if part is None else pltpu.roll(part, LANES - move, 1) for part in (here, beyond)]
        return jnp.where(ready, parts[0], parts[1])

    by_sixteen, by_eight = repeats(16), repeats(8)
    own_rows = [window(by_sixteen, 16, HALF - line) for line in range(rows)]
    top_rows = [window(by_eight, 8, 1 - line) for line in range(rows)]
    bottom_rows = [window(by_eight, 8, rows + HALF - line) for line in range(rows)]

    parity = lax.rem(lane, 2)

    def corner_taps(upper, lower, is_upper):
        top = jnp.where(parity == 1, first_tap, 0.0) if upper else zero
        bottom = jnp.where(parity == 0, last_tap, 0.0) if lower else zero
        return jnp.where(is_upper, top, bottom)

    near_is_top = ~even
    early_rows, late_rows = [], []
    for spot in range(rows):
        odd_line = spot + rows - HALF if spot < HALF else spot - HALF
        own = jnp.where(even, own_rows[spot], own_rows[odd_line])
        side = jnp.where(even, bottom_rows[spot], top_rows[odd_line])
        extra = zero
        if spot >= HALF:
            extra = corner_taps(spot == HALF, spot == rows - 1, near_is_top)
        tiles = [
            own,
            own,
            jnp.where(lane < NEAR_AT - 2 * LANES, own, side),
            jnp.where(lane < NEAR_EXTRA_AT - 3 * LANES, side, extra),
        ]
        early_rows.append(
            jnp.concatenate([mine * tile for mine, tile in zip(tiles, early_tiles)], axis=1)
        )
        if spot < HALF:
            side = jnp.where(even, top_rows[spot], bottom_rows[odd_line])
            extra = corner_taps(spot == 0, spot == HALF - 1, even)
            tiles = [side, jnp.where(lane < FAR_EXTRA_AT - LANES, side, extra)]
            late_rows.append(
                jnp.concatenate([mine * tile for mine, tile in zip(tiles, late_tiles)], axis=1)
            )
    for spot in range(0, rows, 2):
        put_split(weight_ref, spot * BASE_PAD, jnp.concatenate(early_rows[spot : spot + 2], axis=0))
    spare = late_ref.shape[0] // 2 - HALF * BASE_PAD
    late_rows.append(jnp.zeros((spare, LATE), F32))
    put_split(late_ref, 0, jnp.concatenate(late_rows, axis=0))


def edges_of(near_ref, far_ref):
    even = even_stripe()
    near = near_ref[...]
    far = far_ref[...]
    return jnp.where(even, far, near), jnp.where(even, near, far)


def fill_extended(ext, highs, lows, cores, pieces, near_ref, far_ref):
    rows, half = pieces[0].shape
    wide = half * cores
    ext[:, 0:LANES] = jnp.zeros((ext.shape[0], LANES), F32)
    ext[:, LANES + wide :] = jnp.zeros((ext.shape[0], LANES), F32)
    me = lax.axis_index("exp")
    for step in range(cores):
        start = lax.rem(me + step, cores) * half + LANES
        ext[8 : 8 + rows, pl.ds(pl.multiple_of(start, LANES), half)] = pieces[step][...]
    top, bottom = edges_of(near_ref, far_ref)
    for side in range(cores):
        where = pl.ds(LANES + side * half, half)
        ext[0:8, where] = top[8 * side : 8 * side + 8]
        ext[8 + rows : 16 + rows, where] = bottom[8 * side : 8 * side + 8]
        spots = [8 * cores + side, 9 * cores + side]
        spare = [edge[spot : spot + 1] for edge in (top, bottom) for spot in spots]
        ext[16 + rows : 24 + rows, where] = jnp.concatenate(spare + spare, axis=0)
    main = slice(0, GROUP)
    highs[main], lows[main] = split_two(ext[main])
    extra = ext[GROUP : GROUP + 8]
    span = extra.shape[1]
    early = lax.broadcasted_iota(jnp.int32, extra.shape, 0) < 4
    ahead = [extra] + [pltpu.roll(extra, span - part, 1) for part in range(1, 4)]
    lines = jnp.concatenate(
        [jnp.where(early, ahead[0], ahead[1]), jnp.where(early, ahead[2], ahead[3])], axis=0
    )
    highs[GROUP:], lows[GROUP:] = split_two(lines)


def spread_window(shifted, put):
    for tap in range(TAPS):
        put(tap * GROUP, shifted(tap, slice(0, GROUP)))
    for quad in range(MAIN_TILES):
        put(MAIN + 16 * quad, shifted(4 * quad, slice(GROUP, GROUP + 16)))


def clear_spare(refs):
    for ref in refs:
        wide = ref.shape[1]
        ref[TAPS * GROUP : MAIN] = jnp.zeros((MAIN - TAPS * GROUP, wide), BF16)
        ref[MAIN + EXTRA_ROWS :] = jnp.zeros((LANES - EXTRA_ROWS, wide), BF16)


def back_profile(horiz):
    steady = jnp.ones_like(horiz)
    square = 0.5 * (3.0 * horiz * horiz - 1.0)
    return [steady, horiz, steady, horiz, square, steady, horiz]


def put_sides(target, edge_ref):
    fold = edge_ref.shape[1]
    cores = edge_ref.shape[0] // (REACH + 2)
    for side in range(cores):
        where = pl.ds(LANES + side * fold, fold)
        target[0:8, where] = edge_ref[8 * side : 8 * side + 8]
        for line in range(2):
            spot = (8 + line) * cores + side
            target[8 + line : 9 + line, where] = edge_ref[spot : spot + 1]


def paired(values):
    span = values.shape[1]
    return jnp.concatenate([values, pltpu.roll(values, span - 1, 1)], axis=0)


def corner_block(lines):
    span = lines.shape[1]
    parts = [lines] + [pltpu.roll(lines, span - move, 1) for move in range(1, 8)]
    return jnp.concatenate(parts, axis=0)


def odd_rows(odd_ref, stamp, height):
    return jnp.broadcast_to(odd_ref[stamp : stamp + 1, :] == 1, (height, LANES))


def stamp_window(source, odd_ref, stamp, offset):
    height = source.shape[0]
    lane = lane_id(height)
    left = source[:, stamp * LANES : (stamp + 1) * LANES]
    centre = source[:, (stamp + 1) * LANES : (stamp + 2) * LANES]
    right = source[:, (stamp + 2) * LANES : (stamp + 3) * LANES]
    odd = jnp.where(lane < LANES // 4, right, centre)
    even = jnp.where(lane >= LANES - HALF, left, centre)
    odd = pltpu.roll(odd, (HALF + STAMP_W + offset) % LANES, 1)
    even = pltpu.roll(even, HALF + offset, 1)
    return jnp.where(odd_rows(odd_ref, stamp, height), odd, even)


def stamp_values(sources, odd_ref, pair, moves):
    out = []
    for source in sources:
        first = stamp_window(source, odd_ref, 2 * pair, 0)
        second = stamp_window(source, odd_ref, 2 * pair + 1, STAMP_W)
        tiles = []
        for tile, move in moves:
            a, b = first[16 * tile : 16 * tile + 16], second[16 * tile : 16 * tile + 16]
            if move:
                a = pltpu.roll(a, LANES - move, 1)
                b = pltpu.roll(b, LANES - move, 1)
            tiles.append(jnp.where(lane_id(16) < STAMP_W, a, b))
        out.append(jnp.concatenate(tiles, axis=0))
    return out


def three_products(weights, xhigh, xlow):
    rows = weights.shape[0] // 2
    both = jnp.dot(weights, xhigh, preferred_element_type=F32)
    return both[:rows] + (
        both[rows:] + jnp.dot(weights[:rows], xlow, preferred_element_type=F32)
    )


def back_rows(rows):
    empty = jnp.zeros_like(rows[0])
    lead = [empty] * (8 - BACK_FIRST)
    second = lead + rows[BACK_FIRST:]
    second += [empty] * (8 - len(second))
    return [jnp.concatenate(part, axis=0) for part in (lead + rows[:BACK_FIRST], second)]


def design_line(bases, keep, target, horiz, profiles, row, region_rows):
    own = bases * keep
    vert = position(jnp.full(horiz.shape, row, jnp.int32), region_rows)
    square = 0.5 * (3.0 * vert * vert - 1.0)
    steady = jnp.ones_like(vert)
    scales = back_rows([steady, steady, vert, vert, steady, square, square])
    first, second = (profile * scale * keep for profile, scale in zip(profiles, scales))
    spot = lax.broadcasted_iota(jnp.int32, second.shape, 0)
    sloped = own * horiz
    tilted = own * vert
    mixed = jnp.where(spot < SPILL_AT - ALIGNED, second, tilted[ALIGNED:])
    return jnp.concatenate(
        [
            own[:ALIGNED],
            jnp.where(spot < SPILL, own[ALIGNED:], first),
            sloped[:ALIGNED],
            jnp.where(spot < SPILL, sloped[ALIGNED:], mixed),
            tilted[:ALIGNED],
            jnp.where(spot == 0, target, 0.0),
        ],
        axis=0,
    )


def gram(lines):
    design = jnp.concatenate([line.astype(BF16) for line in lines], axis=1)
    return lax.dot_general(design, design, (((1,), (1,)), ((), ())), preferred_element_type=F32)


def early_kernel(cores, stripes, *refs):
    pieces = refs[:cores]
    near_pieces = refs[cores : 2 * cores]
    (
        science_ref,
        good_ref,
        odd_ref,
        weight_ref,
        total_ref,
        late_ref,
        aux_ref,
        near_ref,
        ext,
        highs,
        lows,
        bases,
    ) = refs[2 * cores :]
    rows, half = pieces[0].shape
    wide = science_ref.shape[2]
    pairs = wide // (4 * STAMP_W)
    me = lax.axis_index("exp")
    ext[:, 0:LANES] = jnp.zeros((ext.shape[0], LANES), F32)
    ext[:, LANES + wide :] = jnp.zeros((ext.shape[0], LANES), F32)
    for step in range(cores):
        side = lax.rem(me + step, cores)
        where = pl.ds(pl.multiple_of(side * half + LANES, LANES), half)
        ext[0:rows, where] = pieces[step][...]
        edge = near_pieces[step][...]
        ext[rows : rows + REACH, where] = edge[:REACH]
        near_ref[pl.ds(pl.multiple_of(8 * side, 8), 8), :] = edge[:8]
        for line in range(2):
            near_ref[pl.ds((8 + line) * cores + side, 1), :] = edge[8 + line : 9 + line]
    near_ref[REACH * cores :] = near_pieces[0][REACH : REACH + 2 * cores]
    lines = jnp.concatenate(
        [ext[0:rows], paired(ext[rows : rows + 8]), corner_block(ext[rows + 8 : rows + 10])], axis=0
    )
    highs[...], lows[...] = split_two(lines)
    moves = [(0, tap) for tap in range(TAPS)]
    moves += [(1, 2 * step) for step in range(10)]
    moves += [(2, 8 * step) for step in range(3)]
    lane = lane_id(1)
    for pair in range(pairs):
        columns = slice(pair * LANES, (pair + 1) * LANES)
        odd = jnp.where(
            lane < STAMP_W,
            odd_ref[2 * pair : 2 * pair + 1],
            odd_ref[2 * pair + 1 : 2 * pair + 2] + 1,
        )
        horiz = position(4 * pair * STAMP_W + odd * STAMP_W + lane, wide)
        aux_ref[2 * rows : 2 * rows + 8, columns] = jnp.broadcast_to(horiz, (8, LANES))
        picked = []
        for source in (good_ref, science_ref):
            lower = source[0, :, 2 * pair * LANES : (2 * pair + 1) * LANES]
            upper = source[0, :, (2 * pair + 1) * LANES : (2 * pair + 2) * LANES]
            lower = jnp.where(
                odd_rows(odd_ref, 2 * pair, rows), pltpu.roll(lower, STAMP_W, 1), lower
            )
            upper = jnp.where(
                odd_rows(odd_ref, 2 * pair + 1, rows), upper, pltpu.roll(upper, STAMP_W, 1)
            )
            picked.append(jnp.where(lane_id(rows) < STAMP_W, lower, upper))
        aux_ref[0:rows, columns] = picked[0]
        aux_ref[rows : 2 * rows, columns] = picked[0] * picked[1]
    split = HALF * BASE_PAD
    chunk = 2 * LANES
    for start in range(0, wide // 2, chunk):
        span = slice(start, start + chunk)
        made = [
            stamp_values((highs, lows), odd_ref, pair, moves)
            for pair in range(start // LANES, (start + chunk) // LANES)
        ]
        values = three_products(
            weight_ref[...],
            *(jnp.concatenate([one[side] for one in made], axis=1) for side in range(2)),
        )
        late_ref[:, span] = values[:split]
        bases[:, span] = values[split:]
    horiz = aux_ref[2 * rows : 2 * rows + 1]
    profile = back_rows(back_profile(horiz))
    first_line = jnp.where(even_stripe(), HALF, 0)
    first_row = lax.axis_index("stripe") * rows
    designs = []
    for spot in range(rows - HALF):
        line = first_line + spot
        designs.append(design_line(
            bases[spot * BASE_PAD : (spot + 1) * BASE_PAD],
            aux_ref[pl.ds(line, 1), :],
            aux_ref[pl.ds(rows + line, 1), :],
            horiz,
            profile,
            first_row + line,
            rows * stripes,
        ))
    total = gram(designs)
    total_ref[...] = jnp.concatenate(
        [total, jnp.zeros((FIT_ROWS, LANES - FIT_ROWS), F32)], axis=1
    )


def late_kernel(stripes, rows, *refs):
    (
        far_ref,
        odd_ref,
        weight_ref,
        total_ref,
        early_ref,
        aux_ref,
        out_ref,
        ext,
        highs,
        lows,
        bases,
    ) = refs
    width = early_ref.shape[1]
    pairs = width // LANES
    ext[:, 0:LANES] = jnp.zeros((ext.shape[0], LANES), F32)
    ext[:, ext.shape[1] - LANES :] = jnp.zeros((ext.shape[0], LANES), F32)
    put_sides(ext, far_ref)
    lines = jnp.concatenate([paired(ext[0:8]), corner_block(ext[8:10])], axis=0)
    highs[...], lows[...] = split_two(lines)
    moves = [(0, 2 * step) for step in range(10)] + [(1, 8 * step) for step in range(3)]
    used = 16 * len(moves)
    split = HALF * BASE_PAD
    chunk = 4 * LANES
    for start in range(0, width, chunk):
        span = slice(start, start + chunk)
        made = [
            stamp_values((highs, lows), odd_ref, pair, moves)
            for pair in range(start // LANES, (start + chunk) // LANES)
        ]
        spare = jnp.zeros((LATE - used, chunk), BF16)
        xh, xl = (
            jnp.concatenate([jnp.concatenate([one[side] for one in made], axis=1), spare], axis=0)
            for side in range(2)
        )
        values = three_products(weight_ref[...], xh, xl)
        bases[:, span] = early_ref[:, span] + values[:split]
    horiz = aux_ref[2 * rows : 2 * rows + 1]
    profile = back_rows(back_profile(horiz))
    first_line = jnp.where(even_stripe(), 0, rows - HALF)
    first_row = lax.axis_index("stripe") * rows
    designs = []
    for spot in range(HALF):
        line = first_line + spot
        designs.append(
            design_line(
                bases[spot * BASE_PAD : (spot + 1) * BASE_PAD],
                aux_ref[pl.ds(line, 1), :],
                aux_ref[pl.ds(rows + line, 1), :],
                horiz,
                profile,
                first_row + line,
                rows * stripes,
            )
        )
    middle = width // 2
    own = total_ref[:, :FIT_ROWS] + (
        gram([design[:, :middle] for design in designs])
        + gram([design[:, middle:] for design in designs])
    )
    out_ref[...] = packed_normal(own)


def packed_normal(normal):
    half = UNKNOWNS // 2
    lane = lane_id(8)
    right = jnp.zeros((8, LANES), F32)
    for tile in range(UNKNOWNS // 8):
        column = normal[8 * tile : 8 * tile + 8, UNKNOWNS : UNKNOWNS + 1]
        right = jnp.where(lane == tile, jnp.broadcast_to(column, (8, LANES)), right)
    both = [normal[:half, :UNKNOWNS], normal[half:UNKNOWNS, :UNKNOWNS]]
    return jnp.concatenate([jnp.concatenate(both, axis=1), right], axis=0)


def unpacked_normal(packed):
    half = UNKNOWNS // 2
    lane = lane_id(UNKNOWNS)
    values = jnp.concatenate([packed[:half], pltpu.roll(packed[:half], UNKNOWNS, 1)], axis=0)
    right = jnp.concatenate(
        [
            jnp.broadcast_to(packed[half:, tile : tile + 1], (8, LANES))
            for tile in range(UNKNOWNS // 8)
        ],
        axis=0,
    )
    return jnp.where(lane < UNKNOWNS, values, jnp.where(lane == UNKNOWNS, right, 0.0))


def tree_sum(values):
    while len(values) > 1:
        values = [sum(values[spot : spot + 2][1:], values[spot]) for spot in range(0, len(values), 2)]
    return values[0]


def solve_rows(matrix):
    sub = row_id(8)
    tiles = [matrix[start : start + 8] for start in range(0, UNKNOWNS, 8)]
    order = [(start, 8) for start in range(0, UNKNOWNS, 8)]

    def spread(tile, spot):
        return jnp.broadcast_to(tile[spot : spot + 1], (8, LANES))

    def column(tile, spot):
        return jnp.broadcast_to(tile[:, spot : spot + 1], (8, LANES))

    start, size = order[0]
    corner = [column(tiles[start // 8], start + j) for j in range(size)]
    for step, (start, size) in enumerate(order):
        home = start // 8
        columns = [
            [None if place == home else column(tile, start + j) for place, tile in enumerate(tiles)]
            for j in range(size)
        ]
        rows = tiles[home]
        following = order[step + 1] if step + 1 < len(order) else (0, 0)
        next_home = following[0] // 8
        ahead = [column(rows, following[0] + j) for j in range(following[1])]
        below = [column(tiles[next_home], following[0] + j) for j in range(following[1])]
        for spot in range(size):
            keep = sub == spot
            inverse = 1.0 / spread(corner[spot], spot)
            others = jnp.where(keep, 0.0, corner[spot])

            def eliminated(values):
                scaled = spread(values, spot) * inverse
                return jnp.where(keep, scaled, values - others * scaled)

            corner = [
                eliminated(values) if j > spot else values for j, values in enumerate(corner)
            ]
            ahead = [eliminated(values) for values in ahead]
            rows = eliminated(rows)
        if following[1]:
            corner = [
                values - tree_sum([columns[i][next_home] * spread(ahead[j], i) for i in range(size)])
                for j, values in enumerate(below)
            ]
        for place in range(len(tiles)):
            if place == home:
                tiles[place] = rows
            else:
                tiles[place] = tiles[place] - tree_sum(
                    [columns[i][place] * spread(rows, i) for i in range(size)]
                )
    right = jnp.concatenate(tiles, axis=0)[:, UNKNOWNS : UNKNOWNS + 1]
    return jnp.broadcast_to(right, (UNKNOWNS, LANES))


def region_weights(base_ref, weight_ref, rows):
    lane = lane_id(8)
    spot = lax.rem(lane, GROUP)
    corner = lax.rem(lane, 4)
    line = row_id(8)
    mains = [base_ref[:, tile * LANES : (tile + 1) * LANES] for tile in range(MAIN_TILES)]
    outer = base_ref[:, MAIN : MAIN + LANES]
    inner = base_ref[:, MAIN + LANES :]
    blocks = [[] for _ in range(BASES)]
    for start in range(0, rows, 8):
        tap = spot - (start + line - 1)
        inside = (tap >= 0) & (tap < TAPS)
        moved = [pltpu.roll(main, (start - 1) % LANES, 1) for main in mains]
        extra = zero_row = jnp.zeros((8, LANES), F32)
        for b in range(BASES):
            tiles = []
            for main in moved:
                wide = jnp.broadcast_to(main[b : b + 1], (8, LANES))
                tiles.append(
                    jnp.where(inside, pltpu.roll(wide, 0, 1, stride=1, stride_axis=0), 0.0)
                )
            extra = zero_row
            mine = jnp.broadcast_to(inner[b : b + 1], (8, LANES))
            if start == 0:
                extra = jnp.where((line == 0) & (corner < 2), mine, extra)
            if start == rows - 8:
                extra = jnp.where((line == 7) & (corner >= 2), mine, extra)
            blocks[b].append(jnp.concatenate(tiles + [extra], axis=1))
    for b in range(BASES):
        put_split(weight_ref, b * rows, jnp.concatenate(blocks[b], axis=0))
    lane = lane_id(BASE_PAD)
    spot = lax.rem(lane, GROUP)
    corner = lax.rem(lane, 4)
    halos = []
    for shift, extra in ((rows - 1, corner >= 2), (-2, corner < 2)):
        tap = spot - shift
        inside = (tap >= 0) & (tap < TAPS)
        tiles = [jnp.where(inside, pltpu.roll(main, shift % LANES, 1), 0.0) for main in mains]
        halos.append(jnp.concatenate(tiles + [jnp.where(extra, outer, 0.0)], axis=1))
    put_split(weight_ref, BASES * rows, jnp.concatenate(halos, axis=0))


def region_bases(highs, lows, weight_ref, first, out_ref, scratch):
    wide = out_ref.shape[1]
    chunk = scratch[0].shape[1]
    for spot, start in enumerate(range(0, wide, chunk)):
        targets = scratch[2 * spot : 2 * spot + 2]
        clear_spare(targets)
        for source, target in zip((highs, lows), targets):

            def shifted(tap, lines):
                begin = first + start + LANES - HALF + tap
                return source[lines, begin : begin + chunk]

            def put(place, values):
                target[place : place + values.shape[0]] = values

            spread_window(shifted, put)
        out_ref[:, start : start + chunk] = three_products(
            weight_ref[...], targets[0][...], targets[1][...]
        )


def first_bases_kernel(cores, *refs):
    pieces = refs[:cores]
    (
        far_ref,
        near_ref,
        base_ref,
        after_ref,
        weight_ref,
        highs,
        lows,
        out_ref,
        ext,
        *scratch,
    ) = refs[cores:]
    region_weights(base_ref, weight_ref, pieces[0].shape[0])
    fill_extended(ext, highs, lows, cores, pieces, near_ref, far_ref)
    region_bases(highs, lows, weight_ref, 0, out_ref, scratch)


def next_bases_kernel(first, highs, lows, weight_ref, after_ref, out_ref, *scratch):
    region_bases(highs, lows, weight_ref, first, out_ref, scratch)


def add_kernel(count, *refs):
    values = [ref[...] for ref in refs[:count]]
    if count == 4:
        order = (1, 2, 0)
        values = [values[0]] + [values[1 + order.index(k)] for k in range(3)]
    refs[-1][...] = tree_sum(values)


def model_kernel(stripes, normal_ref, *refs):
    far_ref, near_ref, science_ref, good_ref, out_ref, coef_ref = refs[-6:]
    parts = refs[:-6]
    rows = science_ref.shape[1]
    wide = science_ref.shape[2]
    top, bottom = edges_of(near_ref, far_ref)
    coef = solve_rows(unpacked_normal(normal_ref[...]))
    lane = lane_id(UNKNOWNS)
    base, term = lane // 3, lax.rem(lane, 3)
    tilt = jnp.where(base < ALIGNED, 2 * BASE_PAD, BASE_PAD + SPILL_AT - ALIGNED) + base
    home = lane - 3 * BASES + jnp.where(lane < 3 * BASES + BACK_FIRST, BASES, BASE_PAD + BASES - BACK_FIRST)
    home = jnp.where(lane < 3 * BASES, jnp.where(term == 2, tilt, term * BASE_PAD + base), home)
    flat = jnp.sum(jnp.where(row_id(UNKNOWNS) == home, coef, 0.0), axis=0, keepdims=True)
    coef_ref[...] = flat[:, : coef_ref.shape[1]]

    def share(spot, height):
        return jnp.broadcast_to(coef[spot : spot + 1], (height, LANES))

    first_row = lax.axis_index("stripe") * rows
    vert = position(first_row + row_id(rows), rows * stripes)
    halo_vert = [
        position(jnp.full((8, LANES), first_row + line, jnp.int32), rows * stripes)
        for line in (rows, -1)
    ]
    tilts = [
        2 * BASE_PAD + b if b < ALIGNED else BASE_PAD + SPILL_AT + b - ALIGNED for b in range(BASES)
    ]
    slopes = [share(spot, rows) * vert for spot in tilts]
    tilted = jnp.concatenate(
        [
            coef[2 * BASE_PAD :],
            coef[BASE_PAD + SPILL_AT : 2 * BASE_PAD],
            jnp.zeros((BACK_FIRST, LANES), F32),
        ],
        axis=0,
    )
    halo_slopes = [tilted * jnp.concatenate([line] * 3, axis=0) for line in halo_vert]
    level = [
        share(BASES + m + (0 if m < BACK_FIRST else BASE_PAD - BACK_FIRST), 8) for m in range(BACK)
    ]

    def ground(here, horiz):
        square = 0.5 * (3.0 * here * here - 1.0)
        horiz_square = 0.5 * (3.0 * horiz * horiz - 1.0)
        steady = level[0] + level[1] * horiz + level[4] * horiz_square
        sloped = level[2] + level[3] * horiz
        curved = level[5] + level[6] * horiz
        if here.shape[0] > 8:
            steady, sloped, curved = (
                jnp.concatenate([part] * (here.shape[0] // 8), axis=0)
                for part in (steady, sloped, curved)
            )
        return steady + here * sloped + square * curved

    models, halos = [], [[], []]
    for part in parts:
        for start in range(0, part.shape[1], LANES):
            span = slice(start, start + LANES)
            begin = len(models) * LANES
            horiz = position(begin + lane_id(8), wide)
            total = ground(vert, horiz)
            for b in range(BASES):
                steady = share(b, 8) + share(BASE_PAD + b, 8) * horiz
                scale = jnp.concatenate([steady] * (rows // 8), axis=0) + slopes[b]
                total = total + part[b * rows : (b + 1) * rows, span] * scale
            models.append(total)
            steady = coef[:BASE_PAD] + coef[BASE_PAD : 2 * BASE_PAD] * horiz[0:1]
            for side in range(2):
                place = BASES * rows + side * BASE_PAD
                values = part[place : place + BASE_PAD, span] * (steady + halo_slopes[side])
                values = jnp.sum(values, axis=0, keepdims=True)
                halos[side].append(values + ground(halo_vert[side], horiz)[0:1])
    model = jnp.concatenate(models, axis=1)
    below_model, above_model = (jnp.concatenate(side, axis=1) for side in halos)
    own = good_ref[0] * (science_ref[0] - model)

    def halo(edge, values):
        cores = edge.shape[0] // (REACH + 2)
        science, good = (
            jnp.concatenate(
                [edge[spot : spot + 1] for spot in range(start * cores, (start + 1) * cores)], axis=1
            )
            for start in (REACH, REACH + 1)
        )
        return good * (science - values)

    above_row = halo(top, above_model)
    below_row = halo(bottom, below_model)
    lines = lax.broadcasted_iota(jnp.int32, (rows, wide), 0)
    spots = lax.broadcasted_iota(jnp.int32, (rows, wide), 1)
    above = jnp.where(lines == 0, above_row, pltpu.roll(own, 1, 0))
    below = jnp.where(lines == rows - 1, below_row, pltpu.roll(own, rows - 1, 0))
    before = jnp.where(spots == 0, 0.0, pltpu.roll(own, 1, 1))
    after = jnp.where(spots == wide - 1, 0.0, pltpu.roll(own, wide - 1, 1))
    out_ref[0] = 4.0 * own - (below + above + after + before)


def whole_vmem(count):
    return [pl.BlockSpec(memory_space=pltpu.VMEM)] * count


def add(values, after, params):
    return pl.pallas_call(
        functools.partial(add_kernel, len(values)),
        out_shape=jax.ShapeDtypeStruct(values[0].shape, values[0].dtype),
        in_specs=whole_vmem(len(values) + len(after)),
        out_specs=pl.BlockSpec(memory_space=pltpu.VMEM),
        compiler_params=params,
        name="add",
    )(*values, *after)


def summed(values, axis, beside, params):
    count = lax.axis_size(axis)
    if count & (count - 1):
        for works in beside:
            for work in works:
                work(values)
        return lax.psum(values, axis)
    rounds = [(1, 2, 3)] if count >= 4 else []
    step = 4 if rounds else 1
    while step < count:
        rounds.append((step,))
        step *= 2
    rounds += [()] * (len(beside) - len(rounds))
    for spot, steps in enumerate(rounds):
        others = [
            lax.ppermute(values, axis, [(i, i ^ step) for i in range(count)]) for step in steps
        ]
        after = [work(values) for work in beside[spot]] if spot < len(beside) else []
        if steps:
            if len(others) == 3:
                others = [others[k] for k in (1, 2, 0)]
            values = add([values] + others, after, params)
    return values


def shared_pieces(values, cores):
    return [
        lax.ppermute(values, "exp", [((i + step) % cores, i) for i in range(cores)])
        for step in range(1, cores)
    ]


def shards(template, exposure, cosmic_mask, stamp_blocks, row_filters, col_filters):
    arguments = (template, exposure, cosmic_mask, row_filters, col_filters, stamp_blocks)
    rows, half = template.shape
    wide = exposure.shape[2]
    cores = lax.axis_size("exp")
    stripes = lax.axis_size("stripe")
    params = pltpu.CompilerParams(vmem_limit_bytes=24 * 1024 * 1024)
    pieces = [template] + shared_pieces(template, cores)
    stamps = stamp_blocks.shape[1]
    template_in, science, good, row_in, col_in, odd = pl.pallas_call(
        load_kernel,
        out_shape=(
            jax.ShapeDtypeStruct(template.shape, F32),
            jax.ShapeDtypeStruct(exposure.shape, F32),
            jax.ShapeDtypeStruct(exposure.shape, F32),
            jax.ShapeDtypeStruct(row_filters.shape, F32),
            jax.ShapeDtypeStruct(col_filters.shape, F32),
            jax.ShapeDtypeStruct((stamps, LANES), jnp.int32),
        ),
        in_specs=[pl.BlockSpec(memory_space=pltpu.HBM)] * 6,
        out_specs=tuple(whole_vmem(6)),
        scratch_shapes=[
            pltpu.VMEM(cosmic_mask.shape, jnp.int32),
            pltpu.SMEM(stamp_blocks.shape, jnp.int32),
            pltpu.SemaphoreType.DMA((6,)),
        ],
        compiler_params=params,
        name="load",
    )(*[pltpu.with_memory_space_constraint(array, pltpu.HBM) for array in arguments])
    pieces = [template_in] + pieces[1:]
    near_pairs = [(i, i + 1) for i in range(0, stripes - 1, 2)]
    far_pairs = [(i, i + 1) for i in range(1, stripes - 1, 2)]

    def swapped(values, couples):
        return lax.ppermute(values, "stripe", couples + [(b, a) for a, b in couples])

    near = pl.pallas_call(
        functools.partial(near_kernel, cores),
        out_shape=jax.ShapeDtypeStruct((-(-(REACH + 2 * cores) // 8) * 8, half), F32),
        in_specs=whole_vmem(3),
        out_specs=pl.BlockSpec(memory_space=pltpu.VMEM),
        compiler_params=params,
        name="near",
    )(template_in, science, good)
    near = swapped(near, near_pairs)
    near_pieces = [near] + shared_pieces(near, cores)
    edge_shape = jax.ShapeDtypeStruct(((REACH + 2) * cores, half), F32)
    far = pl.pallas_call(
        functools.partial(far_kernel, cores),
        out_shape=edge_shape,
        in_specs=whole_vmem(cores + 2),
        out_specs=pl.BlockSpec(memory_space=pltpu.VMEM),
        scratch_shapes=[pltpu.VMEM((rows, wide), F32)],
        compiler_params=params,
        name="far",
    )(*pieces, science, good)
    far = swapped(far, far_pairs)
    early_shape = jax.ShapeDtypeStruct((2 * rows * BASE_PAD, EARLY), BF16)
    late_shape = jax.ShapeDtypeStruct((2 * LATE_ROWS, LATE), BF16)
    early_weights, late_weights, base = pl.pallas_call(
        weight_kernel,
        out_shape=(
            early_shape,
            late_shape,
            jax.ShapeDtypeStruct((BASE_PAD, DEPTH + LANES), F32),
        ),
        in_specs=whole_vmem(2),
        out_specs=tuple(whole_vmem(3)),
        scratch_shapes=[pltpu.VMEM((2, BASE_PAD, LANES), F32)],
        compiler_params=params,
        name="weights",
    )(row_in, col_in)
    width = wide // 2
    reach = wide + 2 * LANES
    normal_shape = jax.ShapeDtypeStruct((FIT_ROWS, LANES), F32)
    part, kept, aux, near = pl.pallas_call(
        functools.partial(early_kernel, cores, stripes),
        out_shape=(
            normal_shape,
            jax.ShapeDtypeStruct((HALF * BASE_PAD, width), F32),
            jax.ShapeDtypeStruct((2 * rows + 8, width), F32),
            edge_shape,
        ),
        in_specs=whole_vmem(2 * cores + 4),
        out_specs=tuple(whole_vmem(4)),
        scratch_shapes=[
            pltpu.VMEM((rows + 16, reach), F32),
            pltpu.VMEM((rows + 32, reach), BF16),
            pltpu.VMEM((rows + 32, reach), BF16),
            pltpu.VMEM(((rows - HALF) * BASE_PAD, width), F32),
        ],
        compiler_params=params,
        name="early",
    )(*pieces, *near_pieces, science, good, odd, early_weights)
    normal = pl.pallas_call(
        functools.partial(late_kernel, stripes, rows),
        out_shape=jax.ShapeDtypeStruct((UNKNOWNS // 2 + 8, LANES), F32),
        in_specs=whole_vmem(6),
        out_specs=pl.BlockSpec(memory_space=pltpu.VMEM),
        scratch_shapes=[
            pltpu.VMEM((16, reach), F32),
            pltpu.VMEM((32, reach), BF16),
            pltpu.VMEM((32, reach), BF16),
            pltpu.VMEM((HALF * BASE_PAD, width), F32),
        ],
        compiler_params=params,
        name="late",
    )(far, odd, late_weights, part, kept, aux)
    region_rows = BASES * rows + 2 * BASE_PAD
    blocks = wide // (2 * LANES)
    cuts = [blocks * cut // 8 * 2 * LANES for cut in (0, 2, 4, 8)]
    weight_shape = jax.ShapeDtypeStruct((2 * region_rows, DEPTH), BF16)
    source_shape = jax.ShapeDtypeStruct((GROUP + 16, reach), BF16)
    parts, shared = [], []

    def shift_scratch(size):
        chunk = 2 * LANES
        return [pltpu.VMEM((DEPTH, chunk), BF16)] * (2 * (size // chunk))

    def first_bases(after):
        size = cuts[1]
        *made, part = pl.pallas_call(
            functools.partial(first_bases_kernel, cores),
            out_shape=(
                weight_shape,
                source_shape,
                source_shape,
                jax.ShapeDtypeStruct((region_rows, size), F32),
            ),
            in_specs=whole_vmem(cores + 4),
            out_specs=tuple(whole_vmem(4)),
            scratch_shapes=[pltpu.VMEM((rows + 24, reach), F32)] + shift_scratch(size),
            compiler_params=params,
            name="bases",
        )(*pieces, far, near, base, after)
        shared.extend(made)
        parts.append(part)
        return part

    def next_bases(cut, after):
        size = cuts[cut + 1] - cuts[cut]
        region_weight, highs, lows = shared
        part = pl.pallas_call(
            functools.partial(next_bases_kernel, cuts[cut]),
            out_shape=jax.ShapeDtypeStruct((region_rows, size), F32),
            in_specs=whole_vmem(4),
            out_specs=pl.BlockSpec(memory_space=pltpu.VMEM),
            scratch_shapes=shift_scratch(size),
            compiler_params=params,
            name="bases",
        )(highs, lows, region_weight, after)
        parts.append(part)
        return part

    beside = [[first_bases, functools.partial(next_bases, 1)], [functools.partial(next_bases, 2)]]
    normal = summed(normal, "stripe", beside, params)
    filtered, coef = pl.pallas_call(
        functools.partial(model_kernel, stripes),
        out_shape=(
            jax.ShapeDtypeStruct(exposure.shape, F32),
            jax.ShapeDtypeStruct((1, 3 * BASES + BACK), F32),
        ),
        in_specs=whole_vmem(1 + len(parts) + 4),
        out_specs=tuple(whole_vmem(2)),
        compiler_params=params,
        name="model",
    )(normal, *parts, far, near, science, good)
    return filtered, coef


def solution(mesh):
    placed = (
        P(("groups", "stripe"), "exp"),
        P(("groups", "exp"), "stripe", None),
        P(("groups", "exp"), "stripe", None),
        P(("groups", "stripe"), None),
        P(),
        P(),
    )
    return jax.shard_map(
        shards,
        mesh=mesh,
        in_specs=placed,
        out_specs=(P(("groups", "exp"), "stripe", None), P(("groups", "exp"), None)),
        check_vma=False,
    )
```
